256 devices in a mesh: lat: 16 (over y, x_hi, core), lon: 16 (over x_lo, z).
Axes of the slice: x: 4 (x_hi: 2, x_lo: 2; x = x_hi * 2 + x_lo), y: 4, z: 8, core: 2. Of those that a mesh axis runs over, the one named last changes fastest.
Arguments:
- atmos: bfloat16 [2, 5, 512, 4096], P(None, None, 'lat', 'lon'), may hold values from -6 to 6
- orography: bfloat16 [512, 4096], P('lat', 'lon'), may hold values from -6 to 6
- land_sea: int32 [512, 4096], P('lat', 'lon'), may hold values 0 or 1
- embed_weight: bfloat16 [12, 12, 6, 512], replicated, may hold values from -0.21875 to 0.21875
- level_embed: float32 [2, 512], replicated, may hold values from -6 to 6
- land_embed: float32 [512], replicated, may hold values from -6 to 6
- norm_gain: float32 [2, 512], replicated, may hold values from 0.1 to 1.9
- w_query: bfloat16 [2, 512, 512], replicated, may hold values from -12 to 12
- w_keyval: bfloat16 [2, 512, 1024], replicated, may hold values from -1 to 1
- w_out: bfloat16 [2, 512, 512], replicated, may hold values from -0.25 to 0.25
- merge_gain: float32 [2048], replicated, may hold values from 0.1 to 1.9
- merge_weight: bfloat16 [2048, 1024], replicated, may hold values from -0.125 to 0.125
Outputs:
- merged: bfloat16 [2, 64, 512, 1024], P(None, 'lat', 'lon')
The draws below stay inside these ranges and needn't reach their ends.
All inputs are finite; a program needn't handle non-finite values. No bound on the sum of `land_sea` on one device may be relied on, other than what follows from the above.
Results may differ from the reference program's by a relative error of at most 0.015.
Values may be sent and summed in bfloat16 or wider, within the bound.
No kernel may reach another device: no remote copies, remote signals or barrier semaphores. Data moves between devices by JAX's collectives and lax.ppermute only.
A program may use at most 64 MiB of HBM per device.

```python
import math
import jax
import jax.numpy as jnp
from jax import lax

D = 512
HEADS = 8
HEAD_DIM = 64
VARS = 5
CIN = 6
LV = 2
PATCH = 4
HALO = 4
KERNEL = 12
WIN = 8
SHIFT = 4
NPH = 128
NPW = 1024
LAT_CELLS = 512
LON_CELLS = 4096


def shared_keys(key):
    return jax.random.normal(jax.random.fold_in(key, 7001), (2, D, D), jnp.float32) / math.sqrt(D)


def draw_w_keyval(key, part):
    common = shared_keys(key)
    key = jax.random.fold_in(key, 11)
    values = jax.random.normal(key, (2, D, D), jnp.float32) / math.sqrt(D)
    result = jnp.concatenate([common, values], axis=2)
    return jnp.clip(result, -1.0, 1.0).astype(jnp.bfloat16)


def draw_w_query(key, part):
    key = jax.random.fold_in(key, 13)
    first = jax.random.fold_in(key, 0)
    noise = jax.random.normal(first, (2, D, D), jnp.float32) / math.sqrt(D)
    result = noise
    return jnp.clip(result, -12.0, 12.0).astype(jnp.bfloat16)


def plant(array, key, least, high):
    shape = array.shape
    index_at = [jax.random.randint(jax.random.fold_in(key, axis), (), 0, shape[axis]) for axis in range(len(shape))]
    array = array.at[tuple(index_at)].set(least)
    longest = shape.index(max(shape))
    index_at[longest] = (index_at[longest] + 1) % shape[longest]
    return array.at[tuple(index_at)].set(high)


def shard_levels(own_key, shape, shards, low, top_value):
    level, own = 1.0, jax.random.fold_in(own_key, 6)
    for dim, shards_of in shards:
        steps = jnp.exp(jax.random.uniform(jax.random.fold_in(own, dim), (shards_of,), jnp.float32, low / len(shards), top_value / len(shards)))
        level = level * jnp.repeat(steps, shape[dim] // shards_of).reshape([-1 if axis == dim else 1 for axis in range(len(shape))])
    return level


def bell_draw(key, dims, scale, bound, cuts=(), kind=jnp.bfloat16):
    values = scale * jax.random.normal(key, dims, jnp.float32)
    if cuts:
        values = values * shard_levels(key, dims, cuts, -0.22, 0.18)
    return jnp.clip(values, -bound, bound).astype(kind)


def setup_inputs(seed: int = 0) -> dict:
    streams_of = jax.random.split(jax.random.key(seed), 13)
    return {
        "atmos": bell_draw(streams_of[0], (LV, VARS, LAT_CELLS, LON_CELLS), 1.0, 6.0, ((2, 16), (3, 16))),
        "orography": bell_draw(streams_of[1], (LAT_CELLS, LON_CELLS), 1.0, 6.0, ((0, 16), (1, 16))),
        "land_sea": plant((jax.random.randint(streams_of[2], (LAT_CELLS, LON_CELLS), 0, 10) < 3).astype(jnp.int32), jax.random.fold_in(streams_of[2], 1), 0, 1),
        "embed_weight": bell_draw(streams_of[3], (KERNEL, KERNEL, CIN, D), (CIN * KERNEL * KERNEL) ** -0.5, 0.21875),
        "level_embed": bell_draw(streams_of[4], (LV, D), 1.0, 6.0, (), jnp.float32),
        "land_embed": bell_draw(streams_of[5], (D,), 1.0, 6.0, (), jnp.float32),
        "norm_gain": jnp.clip(1.0 + 0.18 * jax.random.normal(streams_of[6], (2, D), jnp.float32), 0.1, 1.9),
        "w_query": draw_w_query(jax.random.fold_in(streams_of[12], 71), 0),
        "w_keyval": draw_w_keyval(jax.random.fold_in(streams_of[12], 71), 0),
        "w_out": bell_draw(streams_of[9], (2, D, D), D ** -0.5, 0.25),
        "merge_gain": jnp.clip(1.0 + 0.18 * jax.random.normal(streams_of[10], (4 * D,), jnp.float32), 0.1, 1.9),
        "merge_weight": bell_draw(streams_of[11], (4 * D, 2 * D), (4 * D) ** -0.5, 0.125),
    }


def layer_norm(values, gain):
    mean = lax.optimization_barrier(jnp.mean(values, axis=-1, keepdims=True))
    centered = values - mean
    variance = lax.optimization_barrier(jnp.mean(centered * centered, axis=-1, keepdims=True))
    return centered / jnp.sqrt(variance + 1e-05) * gain

def window_attention(field, gain, w_query, w_keyval, w_out, flags):
    levels, rows, cols, width = field.shape
    count = levels * WIN * WIN
    windows = field.reshape(levels, rows // WIN, WIN, cols // WIN, WIN, width)
    windows = windows.transpose(1, 3, 0, 2, 4, 5).reshape(-1, count, width)
    token_flags = jnp.broadcast_to(flags[None, :, None], (levels, rows, cols))
    token_flags = token_flags.reshape(levels, rows // WIN, WIN, cols // WIN, WIN)
    token_flags = token_flags.transpose(1, 3, 0, 2, 4).reshape(-1, count)
    normed = layer_norm(windows, gain).astype(jnp.bfloat16)
    query = jnp.dot(normed, w_query, preferred_element_type=jnp.float32).astype(jnp.bfloat16)
    keyval = jnp.dot(normed, w_keyval, preferred_element_type=jnp.float32).astype(jnp.bfloat16)
    number = windows.shape[0]
    query_heads = query.reshape(number, count, HEADS, HEAD_DIM).astype(jnp.float32)
    key_heads = keyval[..., :width].reshape(number, count, HEADS, HEAD_DIM).astype(jnp.float32)
    value_heads = keyval[..., width:].reshape(number, count, HEADS, HEAD_DIM).astype(jnp.float32)
    scores = jnp.einsum('wqhd,wkhd->whqk', query_heads, key_heads) * HEAD_DIM ** (-0.5)
    allowed = token_flags[:, None, :, None] == token_flags[:, None, None, :]
    scores = jnp.where(allowed, scores, jnp.float32(-1e+30))
    top = lax.optimization_barrier(jnp.max(scores, axis=-1, keepdims=True))
    weights = jnp.exp(scores - top)
    probs = (weights / lax.optimization_barrier(jnp.sum(weights, axis=-1, keepdims=True))).astype(jnp.bfloat16)
    heads = jnp.einsum('whqk,wkhd->wqhd', probs.astype(jnp.float32), value_heads)
    heads = heads.astype(jnp.bfloat16).reshape(number, count, width)
    projected = jnp.dot(heads, w_out, preferred_element_type=jnp.float32)
    projected = projected.reshape(rows // WIN, cols // WIN, levels, WIN, WIN, width)
    projected = projected.transpose(2, 0, 3, 1, 4, 5).reshape(levels, rows, cols, width)
    return field + projected

def attention_block(field, gain, w_query, w_keyval, w_out, flags):
    bands = NPH // WIN
    slabs = field.reshape(LV, bands, WIN, NPW, D).transpose(1, 0, 2, 3, 4)
    band_flags = flags.reshape(bands, WIN)

    def one_band(pair):
        return window_attention(pair[0], gain, w_query, w_keyval, w_out, pair[1])
    result = lax.map(one_band, (slabs, band_flags))
    return result.transpose(1, 0, 2, 3, 4).reshape(LV, NPH, NPW, D)

def merge_patches(field, merge_gain, merge_weight):
    levels, rows, cols, width = field.shape
    grouped = field.reshape(levels, rows // 2, 2, cols // 2, 2, width)
    grouped = grouped.transpose(0, 1, 3, 4, 2, 5).reshape(levels, rows // 2, cols // 2, 4 * width)
    normed = layer_norm(grouped, merge_gain).astype(jnp.bfloat16)
    return jnp.dot(normed, merge_weight, preferred_element_type=jnp.float32).astype(jnp.bfloat16)

def reference(atmos, orography, land_sea, embed_weight, level_embed, land_embed, norm_gain, w_query, w_keyval, w_out, merge_gain, merge_weight):
    surface = jnp.broadcast_to(orography[None, None], (LV, 1, LAT_CELLS, LON_CELLS))
    inputs = jnp.concatenate([atmos, surface], axis=1)
    wrapped = jnp.concatenate([inputs[..., -HALO:], inputs, inputs[..., :HALO]], axis=3)
    padded = jnp.pad(wrapped, ((0, 0), (0, 0), (HALO, HALO), (0, 0)))
    embedded = lax.conv_general_dilated(padded, embed_weight, (PATCH, PATCH), 'VALID', dimension_numbers=('NCHW', 'HWIO', 'NHWC'), preferred_element_type=jnp.float32)
    land_fraction = land_sea.astype(jnp.float32).reshape(NPH, PATCH, NPW, PATCH).mean(axis=(1, 3))
    x0 = embedded + level_embed[:, None, None, :] + land_fraction[None, :, :, None] * land_embed
    no_flags = jnp.zeros((NPH,), dtype=bool)
    x1 = attention_block(x0, norm_gain[0], w_query[0], w_keyval[0], w_out[0], no_flags)
    shifted = jnp.roll(x1, (-SHIFT, -SHIFT), axis=(1, 2))
    pole_flags = jnp.arange(NPH) >= NPH - SHIFT
    moved = attention_block(shifted, norm_gain[1], w_query[1], w_keyval[1], w_out[1], pole_flags)
    x2 = jnp.roll(moved, (SHIFT, SHIFT), axis=(1, 2))
    return merge_patches(x2, merge_gain, merge_weight)
```

```python
import math

import jax
import jax.numpy as jnp
from jax import lax
from jax.experimental import pallas as pl
from jax.experimental.pallas import tpu as pltpu
from jax.sharding import PartitionSpec as P

BF = jnp.bfloat16
F32 = jnp.float32
D = 512
HEAD_DIM = 64
WINS = 10
SCALE = HEAD_DIM ** (-0.5) * math.log2(math.e)
VMEM_LIMIT = 56 * 1024 * 1024


def iota(shape, dim):
    return lax.broadcasted_iota(jnp.int32, shape, dim)


def one_hot(cond):
    return jnp.where(cond, 1.0, 0.0).astype(BF)


def mm(a, b):
    return jnp.dot(a, b, preferred_element_type=F32)


def mm_t(a, b):
    return lax.dot_general(a, b, (((1,), (1,)), ((), ())), preferred_element_type=F32)


def params():
    return pltpu.CompilerParams(vmem_limit_bytes=VMEM_LIMIT)


def patch_kernel(par_ref, atmos_ref, oro_ref, land_ref, band_ref, edge_ref):
    par = par_ref[0]
    cells = jnp.concatenate(
        [
            atmos_ref[...].reshape(320, 256),
            oro_ref[...],
            land_ref[...].astype(F32).astype(BF),
        ],
        axis=0,
    )
    row, src = iota((1024, 384), 0), iota((1024, 384), 1)
    i, ch, r = row // 128, (row % 32) // 4, row % 4
    channel = jnp.where(ch < 5, ch, jnp.where(ch == 5, 10, jnp.where(ch == 6, 11, 9)))
    main = mm(one_hot(src == channel * 32 + i * 4 + r), cells)
    channel = 5 + (row % 16) // 4
    aux = mm(one_hot(src == channel * 32 + i * 4 + r), cells)
    row, col = iota((1024, 256), 0), iota((1024, 256), 1)
    c, half = (row % 128) // 32, (row % 32) // 16
    main = jnp.where(col % 4 == c, main, 0.0).astype(BF)
    aux = jnp.where((col % 4 == c) & (col // 128 == half), aux, 0.0).astype(BF)
    j, col = iota((64, 256), 0), iota((64, 256), 1)
    main = mm_t(one_hot(col // 4 == j), main).astype(BF)
    j, col = iota((32, 256), 0), iota((32, 256), 1)
    aux = mm_t(one_hot((col % 128) // 4 == j), aux).astype(BF)
    for i in range(8):
        band_ref[par + i, 0:64, :] = main[:, i * 128 : i * 128 + 128]
        band_ref[par + i, 64:96, :] = aux[:, i * 128 : i * 128 + 128]
    edge_ref[...] = band_ref[pl.ds(par + 7 * (1 - par), 1)]


def patches(par, atmos, orography, land_sea):
    return pl.pallas_call(
        patch_kernel,
        out_shape=(
            jax.ShapeDtypeStruct((9, 96, 128), BF),
            jax.ShapeDtypeStruct((1, 96, 128), BF),
        ),
        in_specs=[pl.BlockSpec(memory_space=pltpu.SMEM)] + [pl.BlockSpec(memory_space=pltpu.VMEM)] * 3,
        out_specs=(pl.BlockSpec(memory_space=pltpu.VMEM),) * 2,
        compiler_params=params(),
        cost_estimate=pl.CostEstimate(flops=10**9, bytes_accessed=10**6, transcendentals=0),
    )(par, atmos, orography, land_sea)


def unpack_kernel(par_ref, band_ref, far_ref, full_ref, low_ref, high_ref, packed):
    par = par_ref[0]
    packed[pl.ds(9 * (1 - par), 9)] = band_ref[...]
    packed[pl.ds(9 * par, 9)] = far_ref[...]
    k, n = iota((256, 256), 0), iota((256, 256), 1)
    ch, lane = (n % 32) // 4, n % 128
    from_main0 = jnp.where(ch == 7, lane - 4, lane)
    from_main1 = jnp.where(ch == 7, lane - 4, jnp.where(ch == 4, lane + 12, lane))
    aux = packed[:, 64:96, :]
    for half in range(2):
        from_one = jnp.where(ch < 4, 128 + lane + 16 * half, from_main1)
        pick = one_hot(k == jnp.where(n < 128, from_main0, from_one))
        both = jnp.concatenate([packed[:, half * 32 : half * 32 + 32, :], aux], axis=2)
        got = mm(both.reshape(18 * 32, 256), pick).astype(BF).reshape(18, 32, 256)
        for level in range(2):
            tile = got[:, :, level * 128 : level * 128 + 128]
            full_ref[level, :, half * 32 : half * 32 + 32, :] = tile
            if half == 0:
                low_ref[level] = tile[:, :16, :]
            else:
                high_ref[level] = tile[:, 16:, :]


def unpack(par, band, far):
    return pl.pallas_call(
        unpack_kernel,
        out_shape=(
            jax.ShapeDtypeStruct((2, 18, 64, 128), BF),
            jax.ShapeDtypeStruct((2, 18, 16, 128), BF),
            jax.ShapeDtypeStruct((2, 18, 16, 128), BF),
        ),
        in_specs=[pl.BlockSpec(memory_space=pltpu.SMEM)] + [pl.BlockSpec(memory_space=pltpu.VMEM)] * 2,
        out_specs=(pl.BlockSpec(memory_space=pltpu.VMEM),) * 3,
        scratch_shapes=[pltpu.VMEM((18, 96, 128), BF)],
        compiler_params=params(),
        cost_estimate=pl.CostEstimate(flops=10**9, bytes_accessed=10**6, transcendentals=0),
    )(par, band, far)


def normalize(x, gain):
    mean = jnp.mean(x, axis=-1, keepdims=True)
    x = x - mean
    var = jnp.mean(x * x, axis=-1, keepdims=True)
    return x * lax.rsqrt(var + 1e-05) * gain


def attend(q, k, v, bias):
    left = iota((128, 128), 1) < HEAD_DIM
    ones_left, ones_right = one_hot(left), one_hot(~left)
    zero = jnp.zeros((128, 128), BF)
    out = []
    for pair in range(4):
        at = slice(pair * 128, pair * 128 + 128)
        kp, vp = k[:, at], v[:, at]
        keys = jnp.concatenate([jnp.where(left, kp, zero), jnp.where(left, zero, kp)], axis=0)
        s = mm_t(q[:, at], keys)
        if bias is not None:
            s = s + bias
        s0, s1 = s[:, :128], s[:, 128:]
        p0 = jnp.exp2(s0 - jnp.max(s0, axis=-1, keepdims=True))
        p1 = jnp.exp2(s1 - jnp.max(s1, axis=-1, keepdims=True))
        p = jnp.concatenate([p0, p1], axis=1).astype(BF)
        vals = jnp.concatenate(
            [
                jnp.concatenate([jnp.where(left, vp, zero), ones_left], axis=1),
                jnp.concatenate([jnp.where(left, zero, vp), ones_right], axis=1),
            ],
            axis=0,
        )
        o = mm(p, vals)
        out.append((o[:, :128] / o[:, 128:]).astype(BF))
    return jnp.concatenate(out, axis=1)


def first_kernel(
    par_ref, full_ref, low_ref, high_ref, wemb_ref, lev_ref, gain_ref, wq_any, wkv_any, wo_any,
    x1_ref, send_ref,
    wide, gathered, x0, normed, query, keyval, heads, wq, wkv, wo, sems,
):
    par = par_ref[0]
    loads = [
        pltpu.make_async_copy(wq_any.at[0], wq, sems.at[0]),
        pltpu.make_async_copy(wkv_any.at[0], wkv, sems.at[1]),
        pltpu.make_async_copy(wo_any.at[0], wo, sems.at[2]),
    ]
    for load in loads:
        load.start()
    wide[:, :, 0:16, :] = low_ref[...].astype(F32)
    wide[:, :, 16:80, :] = full_ref[...].astype(F32)
    wide[:, :, 80:96, :] = high_ref[...].astype(F32)
    for dj in range(3):
        gathered[:, :, :, dj * 128 : dj * 128 + 128] = wide[:, :, 7 + dj : 87 + dj, :].astype(BF)
    gain = gain_ref[0:1, :]

    def embed(part):
        def one(t, carry):
            level, pair = t // 4, t % 4
            at = part * 8 + pair * 2
            lhs = jnp.concatenate(
                [gathered[level, pl.ds(at + di, 2)].reshape(160, 384) for di in range(3)], axis=1
            )
            x = mm(lhs, wemb_ref[...]) + lev_ref[pl.ds(level, 1), :]
            x0[level, pl.ds(pair * 2, 2)] = x.reshape(2, 80, D)
            return carry

        lax.fori_loop(0, 8, one, 0)

    def norm(w, carry):
        x = x0[:, :, pl.ds(pl.multiple_of(w * 8, 8), 8), :].reshape(128, D)
        normed[w] = normalize(x, gain).astype(BF).reshape(2, 4, 16, D)
        return carry

    def project_kv(w, carry):
        n = normed[pl.ds(w * 2, 2)].reshape(256, D)
        keyval[pl.ds(w * 2, 2)] = mm(n, wkv[...]).astype(BF).reshape(2, 128, 1024)
        return carry

    def store(w, rows_from, rows, out_from, value):
        old = x0[:, pl.ds(rows_from, rows), pl.ds(pl.multiple_of(w * 8, 8), 8), :]
        new = old + value.reshape(2, rows, 8, D)
        x1_ref[:, pl.ds(out_from, rows), pl.ds(pl.multiple_of(w * 8, 8), 8), :] = new

    embed(1 - par)
    lax.fori_loop(0, WINS, norm, 0)
    loads[0].wait()
    loads[1].wait()
    lax.fori_loop(0, WINS // 2, project_kv, 0)

    def own_query(w, carry):
        n = normed[pl.ds(w * 2, 2)].reshape(256, D)
        query[pl.ds(w * 4, 4)] = (mm(n, wq[...]) * SCALE).astype(BF).reshape(4, 64, D)
        return carry

    lax.fori_loop(0, WINS // 2, own_query, 0)

    def own_attend(w, carry):
        q = query[pl.ds(w * 2, 2)].reshape(128, D)
        kv = keyval[w]
        heads[pl.ds(w * 2, 2)] = attend(q, kv[:, :D], kv[:, D:], None).reshape(2, 64, D)
        return carry

    lax.fori_loop(0, WINS, own_attend, 0)
    loads[2].wait()

    def own_out(w, carry):
        out = mm(heads[pl.ds(w * 4, 4)].reshape(256, D), wo[...])
        for u in range(2):
            store(w * 2 + u, 0, 8, 4 * (1 - par), out[u * 128 : u * 128 + 128])
        return carry

    lax.fori_loop(0, WINS // 2, own_out, 0)

    half = 1 - par
    embed(par)
    lax.fori_loop(0, WINS, norm, 0)
    lax.fori_loop(0, WINS // 2, project_kv, 0)

    def outer_query(w, carry):
        n = normed[pl.ds(w * 5, 5), :, pl.ds(half * 2, 2)].reshape(320, D)
        query[pl.ds(w * 5, 5)] = (mm(n, wq[...]) * SCALE).astype(BF).reshape(5, 64, D)
        return carry

    lax.fori_loop(0, 2, outer_query, 0)

    def outer_attend(w, carry):
        kv = keyval[w]
        heads[w] = attend(query[w], kv[:, :D], kv[:, D:], None)
        return carry

    lax.fori_loop(0, WINS, outer_attend, 0)

    def outer_out(w, carry):
        out = mm(heads[pl.ds(w * 5, 5)].reshape(320, D), wo[...])
        for u in range(5):
            store(w * 5 + u, 4 * half, 4, 8 * par, out[u * 64 : u * 64 + 64])
        return carry

    lax.fori_loop(0, 2, outer_out, 0)
    send_ref[...] = x1_ref[:, pl.ds(8 * (1 - par), 4)].astype(BF)


def first_block(par, full, low, high, wemb, level_embed, norm_gain, w_query, w_keyval, w_out):
    vmem = pl.BlockSpec(memory_space=pltpu.VMEM)
    hbm = pl.BlockSpec(memory_space=pl.ANY)
    return pl.pallas_call(
        first_kernel,
        out_shape=(
            jax.ShapeDtypeStruct((2, 12, 80, D), F32),
            jax.ShapeDtypeStruct((2, 4, 80, D), BF),
        ),
        in_specs=[pl.BlockSpec(memory_space=pltpu.SMEM)] + [vmem] * 6 + [hbm] * 3,
        out_specs=(vmem, vmem),
        scratch_shapes=[
            pltpu.VMEM((2, 18, 96, 128), F32),
            pltpu.VMEM((2, 18, 80, 384), BF),
            pltpu.VMEM((2, 8, 80, D), F32),
            pltpu.VMEM((WINS, 2, 4, 16, D), BF),
            pltpu.VMEM((2 * WINS, 64, D), BF),
            pltpu.VMEM((WINS, 128, 1024), BF),
            pltpu.VMEM((2 * WINS, 64, D), BF),
            pltpu.VMEM((D, D), BF),
            pltpu.VMEM((D, 1024), BF),
            pltpu.VMEM((D, D), BF),
            pltpu.SemaphoreType.DMA((3,)),
        ],
        compiler_params=params(),
        cost_estimate=pl.CostEstimate(flops=2 * 10**10, bytes_accessed=10**7, transcendentals=0),
    )(par, full, low, high, wemb, level_embed, norm_gain, w_query, w_keyval, w_out)


SHIFTED = WINS - 1


def second_kernel(
    par_ref, x1_any, near_ref, gain_ref, mgain_ref, wq_any, wkv_any, wo_any, wm_any,
    out_ref,
    x1, x2, normed, query, keyval, heads, wq, wkv, wo, wm, sems,
):
    par, first, last = par_ref[0], par_ref[1], par_ref[2]
    loads = [
        pltpu.make_async_copy(x1_any, x1.at[:, pl.ds(4 * par, 12)], sems.at[0]),
        pltpu.make_async_copy(wkv_any.at[1], wkv, sems.at[1]),
        pltpu.make_async_copy(wq_any.at[1], wq, sems.at[2]),
        pltpu.make_async_copy(wo_any.at[1], wo, sems.at[3]),
        pltpu.make_async_copy(wm_any, wm, sems.at[4]),
    ]
    for load in loads:
        load.start()
    x1[:, pl.ds(12 * (1 - par), 4)] = near_ref[...].astype(F32)
    gain = gain_ref[1:2, :]
    upper = iota((8, D), 0) >= 4
    loads[0].wait()

    def window(w, rows_from, rows):
        at = pl.multiple_of(w * 8, 8)
        a = x1[:, pl.ds(rows_from, rows), pl.ds(at, 8), :]
        b = x1[:, pl.ds(rows_from, rows), pl.ds(pl.multiple_of(at + 8, 8), 8), :]
        return jnp.where(upper, a, b)

    def norm(t, carry):
        s, w = t // SHIFTED, t % SHIFTED
        x = window(w, s * 8, 8).reshape(128, D)
        normed[t] = normalize(x, gain).astype(BF).reshape(2, 4, 16, D)
        return carry

    lax.fori_loop(0, 2 * SHIFTED, norm, 0)
    loads[1].wait()

    def project_kv(t, carry):
        n = normed[pl.ds(t * 2, 2)].reshape(256, D)
        keyval[pl.ds(t * 2, 2)] = mm(n, wkv[...]).astype(BF).reshape(2, 128, 1024)
        return carry

    lax.fori_loop(0, SHIFTED, project_kv, 0)
    loads[2].wait()

    def project_q(t, carry):
        s, part = t // 3, t % 3
        at = s * SHIFTED + part * 3
        n = normed[pl.ds(at, 3), :, pl.ds((1 - s) * 2, 2)].reshape(192, D)
        query[pl.ds(at, 3)] = (mm(n, wq[...]) * SCALE).astype(BF).reshape(3, 64, D)
        return carry

    lax.fori_loop(0, 6, project_q, 0)
    key_row = (iota((1, 256), 1) // 8) % 8
    below = jnp.where(key_row < 4, F32(-1e30), F32(0))
    above = jnp.where(key_row < 4, F32(0), F32(-1e30))

    def one_attend(t, carry):
        s = t // SHIFTED
        cut_low = jnp.where(s == 0, first, 0).astype(F32)
        cut_high = jnp.where(s == 0, 0, last).astype(F32)
        bias = below * cut_low + above * cut_high
        kv = keyval[t]
        heads[t] = attend(query[t], kv[:, :D], kv[:, D:], bias)
        return carry

    lax.fori_loop(0, 2 * SHIFTED, one_attend, 0)
    loads[3].wait()

    def one_out(t, carry):
        s, part = t // 3, t % 3
        out = mm(heads[pl.ds(s * SHIFTED + part * 3, 3)].reshape(192, D), wo[...])
        for u in range(3):
            w = part * 3 + u
            new = window(w, 4 + s * 4, 4) + out[u * 64 : u * 64 + 64].reshape(2, 4, 8, D)
            at = pl.multiple_of(w * 8, 8)
            rows, here, after = pl.ds(s * 4, 4), pl.ds(at, 8), pl.ds(pl.multiple_of(at + 8, 8), 8)
            for c in range(4):
                piece = new[..., c * 128 : c * 128 + 128]
                old = x2[c, :, rows, here, :]
                x2[c, :, rows, here, :] = jnp.where(upper[:, :128], piece, old)
                x2[c, :, rows, after, :] = piece
        return carry

    lax.fori_loop(0, 6, one_out, 0)
    loads[4].wait()

    def merge(t, carry):
        level, half = t // 2, t % 2
        parts = []
        for p in range(4):
            got = [
                jnp.concatenate(
                    [
                        x2[c, level, half * 4 + 2 * a + p % 2, pl.ds(8 + p // 2, 32, stride=2), :]
                        for c in range(4)
                    ],
                    axis=1,
                )
                for a in range(2)
            ]
            parts.append(jnp.concatenate(got, axis=0))
        x = jnp.concatenate(parts, axis=1)
        n = normalize(x, mgain_ref[...]).astype(BF)
        out = mm(n, wm[...]).astype(BF)
        out_ref[level, pl.ds(half * 2, 2)] = out.reshape(2, 32, 1024)
        return carry

    lax.fori_loop(0, 4, merge, 0)


def second_block(par, x1, near, norm_gain, merge_gain, w_query, w_keyval, w_out, merge_weight):
    vmem = pl.BlockSpec(memory_space=pltpu.VMEM)
    hbm = pl.BlockSpec(memory_space=pl.ANY)
    return pl.pallas_call(
        second_kernel,
        out_shape=jax.ShapeDtypeStruct((2, 4, 32, 1024), BF),
        in_specs=[pl.BlockSpec(memory_space=pltpu.SMEM), hbm] + [vmem] * 3 + [hbm] * 4,
        out_specs=vmem,
        scratch_shapes=[
            pltpu.VMEM((2, 16, 80, D), F32),
            pltpu.VMEM((4, 2, 8, 80, 128), F32),
            pltpu.VMEM((2 * SHIFTED, 2, 4, 16, D), BF),
            pltpu.VMEM((2 * SHIFTED, 64, D), BF),
            pltpu.VMEM((2 * SHIFTED, 128, 1024), BF),
            pltpu.VMEM((2 * SHIFTED, 64, D), BF),
            pltpu.VMEM((D, D), BF),
            pltpu.VMEM((D, 1024), BF),
            pltpu.VMEM((D, D), BF),
            pltpu.VMEM((4 * D, 1024), BF),
            pltpu.SemaphoreType.DMA((5,)),
        ],
        compiler_params=params(),
        cost_estimate=pl.CostEstimate(flops=10**10, bytes_accessed=10**7, transcendentals=0),
    )(par, x1, near, norm_gain, merge_gain, w_query, w_keyval, w_out, merge_weight)


def embedding_matrix(embed_weight, land_embed):
    w = embed_weight.reshape(3, 4, 3, 4, 6, D).transpose(0, 2, 3, 4, 1, 5)
    share = land_embed / 16
    high = lax.reduce_precision(share, 8, 7)
    terms = jnp.stack([high, share - high]).astype(BF)
    terms = jnp.broadcast_to(terms[None, :, None, :], (4, 2, 4, D))
    middle = (jnp.arange(9) == 4).reshape(3, 3, 1, 1, 1, 1)
    land = jnp.where(middle, terms, jnp.zeros((), BF))
    return jnp.concatenate([w, land], axis=3).reshape(9 * 128, D)


def swap(block, first):
    count = lax.axis_size("lat")
    pairs = []
    for i in range(first, count - 1, 2):
        pairs += [(i, i + 1), (i + 1, i)]
    return lax.ppermute(block, "lat", pairs)


def around(block, distance):
    count = lax.axis_size("lon")
    return lax.ppermute(block, "lon", [(i, (i + distance) % count) for i in range(count)])


def shards(
    atmos, orography, land_sea, embed_weight, level_embed, land_embed, norm_gain,
    w_query, w_keyval, w_out, merge_gain, merge_weight,
):
    lat = lax.axis_index("lat")
    par = lat % 2
    place = jnp.stack([par, lat == 0, lat == lax.axis_size("lat") - 1]).astype(jnp.int32)
    band, edge = patches(place, atmos, orography, land_sea)
    edge = swap(edge, 0)
    band = lax.dynamic_update_slice(band, edge, (8 * (1 - par), 0, 0))
    far = swap(band, 1)
    full, low, high = unpack(place, band, far)
    from_low, from_high = around(high, 1), around(low, -1)
    wemb = embedding_matrix(embed_weight, land_embed)
    x1, send = first_block(
        place, full, from_low, from_high, wemb, level_embed, norm_gain, w_query, w_keyval, w_out
    )
    near = swap(send, 0)
    return second_block(
        place, x1, near, norm_gain, merge_gain.reshape(1, -1), w_query, w_keyval, w_out, merge_weight
    )


def solution(mesh):
    in_specs = (P(None, None, "lat", "lon"), P("lat", "lon"), P("lat", "lon")) + (P(),) * 9
    out_specs = P(None, "lat", "lon", None)
    return jax.shard_map(shards, mesh=mesh, in_specs=in_specs, out_specs=out_specs, check_vma=False)
```

```python
import math

import jax
import jax.numpy as jnp
from jax import lax
from jax.experimental import pallas as pl
from jax.experimental.pallas import tpu as pltpu
from jax.sharding import PartitionSpec as P

BF = jnp.bfloat16
F32 = jnp.float32
D = 512
HEAD_DIM = 64
WINS = 10
SCALE = HEAD_DIM ** (-0.5) * math.log2(math.e)
VMEM_LIMIT = 56 * 1024 * 1024


def iota(shape, dim):
    return lax.broadcasted_iota(jnp.int32, shape, dim)


def one_hot(cond):
    return jnp.where(cond, 1.0, 0.0).astype(BF)


def mm(a, b):
    return jnp.dot(a, b, preferred_element_type=F32)


def mm_t(a, b):
    return lax.dot_general(a, b, (((1,), (1,)), ((), ())), preferred_element_type=F32)


def params():
    return pltpu.CompilerParams(vmem_limit_bytes=VMEM_LIMIT)


def patch_kernel(par_ref, atmos_ref, oro_ref, land_ref, band_ref, edge_ref):
    par = par_ref[0]
    cells = jnp.concatenate(
        [
            atmos_ref[...].reshape(320, 256),
            oro_ref[...],
            land_ref[...].astype(F32).astype(BF),
        ],
        axis=0,
    )
    row, src = iota((1024, 384), 0), iota((1024, 384), 1)
    i, ch, r = row // 128, (row % 32) // 4, row % 4
    channel = jnp.where(ch < 5, ch, jnp.where(ch == 5, 10, jnp.where(ch == 6, 11, 9)))
    main = mm(one_hot(src == channel * 32 + i * 4 + r), cells)
    channel = 5 + (row % 16) // 4
    aux = mm(one_hot(src == channel * 32 + i * 4 + r), cells)
    row, col = iota((1024, 256), 0), iota((1024, 256), 1)
    c, half = (row % 128) // 32, (row % 32) // 16
    main = jnp.where(col % 4 == c, main, 0.0).astype(BF)
    aux = jnp.where((col % 4 == c) & (col // 128 == half), aux, 0.0).astype(BF)
    j, col = iota((64, 256), 0), iota((64, 256), 1)
    main = mm_t(one_hot(col // 4 == j), main).astype(BF)
    j, col = iota((32, 256), 0), iota((32, 256), 1)
    aux = mm_t(one_hot((col % 128) // 4 == j), aux).astype(BF)
    for i in range(8):
        band_ref[par + i, 0:64, :] = main[:, i * 128 : i * 128 + 128]
        band_ref[par + i, 64:96, :] = aux[:, i * 128 : i * 128 + 128]
    edge_ref[...] = band_ref[pl.ds(par + 7 * (1 - par), 1)]


def patches(par, atmos, orography, land_sea):
    return pl.pallas_call(
        patch_kernel,
        out_shape=(
            jax.ShapeDtypeStruct((9, 96, 128), BF),
            jax.ShapeDtypeStruct((1, 96, 128), BF),
        ),
        in_specs=[pl.BlockSpec(memory_space=pltpu.SMEM)] + [pl.BlockSpec(memory_space=pltpu.VMEM)] * 3,
        out_specs=(pl.BlockSpec(memory_space=pltpu.VMEM),) * 2,
        compiler_params=params(),
        cost_estimate=pl.CostEstimate(flops=10**9, bytes_accessed=10**6, transcendentals=0),
    )(par, atmos, orography, land_sea)


def unpack_kernel(par_ref, band_ref, far_ref, full_ref, low_ref, high_ref, packed):
    par = par_ref[0]
    packed[pl.ds(9 * (1 - par), 9)] = band_ref[...]
    packed[pl.ds(9 * par, 9)] = far_ref[...]
    k, n = iota((256, 256), 0), iota((256, 256), 1)
    ch, lane = (n % 32) // 4, n % 128
    from_main0 = jnp.where(ch == 7, lane - 4, lane)
    from_main1 = jnp.where(ch == 7, lane - 4, jnp.where(ch == 4, lane + 12, lane))
    aux = packed[:, 64:96, :]
    for half in range(2):
        from_one = jnp.where(ch < 4, 128 + lane + 16 * half, from_main1)
        pick = one_hot(k == jnp.where(n < 128, from_main0, from_one))
        both = jnp.concatenate([packed[:, half * 32 : half * 32 + 32, :], aux], axis=2)
        got = mm(both.reshape(18 * 32, 256), pick).astype(BF).reshape(18, 32, 256)
        for level in range(2):
            tile = got[:, :, level * 128 : level * 128 + 128]
            full_ref[level, :, half * 32 : half * 32 + 32, :] = tile
            if half == 0:
                low_ref[level] = tile[:, :16, :]
            else:
                high_ref[level] = tile[:, 16:, :]


def unpack(par, band, far):
    return pl.pallas_call(
        unpack_kernel,
        out_shape=(
            jax.ShapeDtypeStruct((2, 18, 64, 128), BF),
            jax.ShapeDtypeStruct((2, 18, 16, 128), BF),
            jax.ShapeDtypeStruct((2, 18, 16, 128), BF),
        ),
        in_specs=[pl.BlockSpec(memory_space=pltpu.SMEM)] + [pl.BlockSpec(memory_space=pltpu.VMEM)] * 2,
        out_specs=(pl.BlockSpec(memory_space=pltpu.VMEM),) * 3,
        scratch_shapes=[pltpu.VMEM((18, 96, 128), BF)],
        compiler_params=params(),
        cost_estimate=pl.CostEstimate(flops=10**9, bytes_accessed=10**6, transcendentals=0),
    )(par, band, far)


def steps(count, body):
    for t in range(count):
        body(t)


def normalize(x, gain):
    mean = jnp.mean(x, axis=-1, keepdims=True)
    x = x - mean
    var = jnp.mean(x * x, axis=-1, keepdims=True)
    return x * lax.rsqrt(var + 1e-05) * gain


def attend(q, k, v, bias):
    left = iota((128, 128), 1) < HEAD_DIM
    ones_left, ones_right = one_hot(left), one_hot(~left)
    zero = jnp.zeros((128, 128), BF)
    out = []
    for pair in range(4):
        at = slice(pair * 128, pair * 128 + 128)
        kp, vp = k[:, at], v[:, at]
        keys = jnp.concatenate([jnp.where(left, kp, zero), jnp.where(left, zero, kp)], axis=0)
        s = mm_t(q[:, at], keys)
        if bias is not None:
            s = s + bias
        s0, s1 = s[:, :128], s[:, 128:]
        p0 = jnp.exp2(s0 - jnp.max(s0, axis=-1, keepdims=True))
        p1 = jnp.exp2(s1 - jnp.max(s1, axis=-1, keepdims=True))
        p = jnp.concatenate([p0, p1], axis=1).astype(BF)
        vals = jnp.concatenate(
            [
                jnp.concatenate([jnp.where(left, vp, zero), ones_left], axis=1),
                jnp.concatenate([jnp.where(left, zero, vp), ones_right], axis=1),
            ],
            axis=0,
        )
        o = mm(p, vals)
        out.append((o[:, :128] / o[:, 128:]).astype(BF))
    return jnp.concatenate(out, axis=1)


def first_kernel(
    par_ref, full_ref, low_ref, high_ref, wemb_ref, lev_ref, gain_ref, wq_any, wkv_any, wo_any,
    x1_ref, send_ref,
    wide, gathered, x0, normed, query, keyval, heads, wq, wkv, wo, sems,
):
    par = par_ref[0]
    loads = [
        pltpu.make_async_copy(wq_any.at[0], wq, sems.at[0]),
        pltpu.make_async_copy(wkv_any.at[0], wkv, sems.at[1]),
        pltpu.make_async_copy(wo_any.at[0], wo, sems.at[2]),
    ]
    for load in loads:
        load.start()
    wide[:, :, 0:16, :] = low_ref[...].astype(F32)
    wide[:, :, 16:80, :] = full_ref[...].astype(F32)
    wide[:, :, 80:96, :] = high_ref[...].astype(F32)
    for dj in range(3):
        gathered[:, :, :, dj * 128 : dj * 128 + 128] = wide[:, :, 7 + dj : 87 + dj, :].astype(BF)
    gain = gain_ref[0:1, :]

    def embed(part):
        def one(t):
            level, pair = t // 4, t % 4
            at = part * 8 + pair * 2
            lhs = jnp.concatenate(
                [gathered[level, pl.ds(at + di, 2)].reshape(160, 384) for di in range(3)], axis=1
            )
            x = mm(lhs, wemb_ref[...]) + lev_ref[level : level + 1, :]
            x0[level, pl.ds(pair * 2, 2)] = x.reshape(2, 80, D)

        steps(8, one)

    def norm(w):
        x = x0[:, :, pl.ds(w * 8, 8), :].reshape(128, D)
        normed[w] = normalize(x, gain).astype(BF).reshape(2, 4, 16, D)

    def project_kv(w):
        n = normed[pl.ds(w * 2, 2)].reshape(256, D)
        keyval[pl.ds(w * 2, 2)] = mm(n, wkv[...]).astype(BF).reshape(2, 128, 1024)

    def store(w, rows_from, rows, out_from, value):
        old = x0[:, pl.ds(rows_from, rows), pl.ds(w * 8, 8), :]
        new = old + value.reshape(2, rows, 8, D)
        x1_ref[:, pl.ds(out_from, rows), pl.ds(w * 8, 8), :] = new

    embed(1 - par)
    steps(WINS, norm)
    loads[0].wait()
    loads[1].wait()
    steps(WINS // 2, project_kv)

    def own_query(w):
        n = normed[pl.ds(w * 2, 2)].reshape(256, D)
        query[pl.ds(w * 4, 4)] = (mm(n, wq[...]) * SCALE).astype(BF).reshape(4, 64, D)

    steps(WINS // 2, own_query)

    def own_attend(w):
        q = query[pl.ds(w * 2, 2)].reshape(128, D)
        kv = keyval[w]
        heads[pl.ds(w * 2, 2)] = attend(q, kv[:, :D], kv[:, D:], None).reshape(2, 64, D)

    steps(WINS, own_attend)
    loads[2].wait()

    def own_out(w):
        out = mm(heads[pl.ds(w * 4, 4)].reshape(256, D), wo[...])
        for u in range(2):
            store(w * 2 + u, 0, 8, 4 * (1 - par), out[u * 128 : u * 128 + 128])

    steps(WINS // 2, own_out)

    half = 1 - par
    embed(par)
    steps(WINS, norm)
    steps(WINS // 2, project_kv)

    def outer_query(w):
        n = normed[pl.ds(w * 5, 5), :, pl.ds(half * 2, 2)].reshape(320, D)
        query[pl.ds(w * 5, 5)] = (mm(n, wq[...]) * SCALE).astype(BF).reshape(5, 64, D)

    steps(2, outer_query)

    def outer_attend(w):
        kv = keyval[w]
        heads[w] = attend(query[w], kv[:, :D], kv[:, D:], None)

    steps(WINS, outer_attend)

    def outer_out(w):
        out = mm(heads[pl.ds(w * 5, 5)].reshape(320, D), wo[...])
        for u in range(5):
            store(w * 5 + u, 4 * half, 4, 8 * par, out[u * 64 : u * 64 + 64])

    steps(2, outer_out)
    send_ref[...] = x1_ref[:, pl.ds(8 * (1 - par), 4)].astype(BF)


def first_block(par, full, low, high, wemb, level_embed, norm_gain, w_query, w_keyval, w_out):
    vmem = pl.BlockSpec(memory_space=pltpu.VMEM)
    hbm = pl.BlockSpec(memory_space=pl.ANY)
    return pl.pallas_call(
        first_kernel,
        out_shape=(
            jax.ShapeDtypeStruct((2, 12, 80, D), F32),
            jax.ShapeDtypeStruct((2, 4, 80, D), BF),
        ),
        in_specs=[pl.BlockSpec(memory_space=pltpu.SMEM)] + [vmem] * 6 + [hbm] * 3,
        out_specs=(vmem, vmem),
        scratch_shapes=[
            pltpu.VMEM((2, 18, 96, 128), F32),
            pltpu.VMEM((2, 18, 80, 384), BF),
            pltpu.VMEM((2, 8, 80, D), F32),
            pltpu.VMEM((WINS, 2, 4, 16, D), BF),
            pltpu.VMEM((2 * WINS, 64, D), BF),
            pltpu.VMEM((WINS, 128, 1024), BF),
            pltpu.VMEM((2 * WINS, 64, D), BF),
            pltpu.VMEM((D, D), BF),
            pltpu.VMEM((D, 1024), BF),
            pltpu.VMEM((D, D), BF),
            pltpu.SemaphoreType.DMA((3,)),
        ],
        compiler_params=params(),
        cost_estimate=pl.CostEstimate(flops=2 * 10**10, bytes_accessed=10**7, transcendentals=0),
    )(par, full, low, high, wemb, level_embed, norm_gain, w_query, w_keyval, w_out)


SHIFTED = WINS - 1


def second_kernel(
    par_ref, x1_any, near_ref, gain_ref, mgain_ref, wq_any, wkv_any, wo_any, wm_any,
    out_ref,
    x1, x2, normed, query, keyval, heads, wq, wkv, wo, wm, sems,
):
    par, first, last = par_ref[0], par_ref[1], par_ref[2]
    loads = [
        pltpu.make_async_copy(x1_any, x1.at[:, pl.ds(4 * par, 12)], sems.at[0]),
        pltpu.make_async_copy(wkv_any.at[1], wkv, sems.at[1]),
        pltpu.make_async_copy(wq_any.at[1], wq, sems.at[2]),
        pltpu.make_async_copy(wo_any.at[1], wo, sems.at[3]),
        pltpu.make_async_copy(wm_any, wm, sems.at[4]),
    ]
    for load in loads:
        load.start()
    x1[:, pl.ds(12 * (1 - par), 4)] = near_ref[...].astype(F32)
    gain = gain_ref[1:2, :]
    upper = iota((8, D), 0) >= 4
    loads[0].wait()

    def window(w, rows_from, rows):
        at = w * 8
        a = x1[:, pl.ds(rows_from, rows), pl.ds(at, 8), :]
        b = x1[:, pl.ds(rows_from, rows), pl.ds(at + 8, 8), :]
        return jnp.where(upper, a, b)

    def norm(t):
        s, w = t // SHIFTED, t % SHIFTED
        x = window(w, s * 8, 8).reshape(128, D)
        normed[t] = normalize(x, gain).astype(BF).reshape(2, 4, 16, D)

    steps(2 * SHIFTED, norm)
    loads[1].wait()

    def project_kv(t):
        n = normed[pl.ds(t * 2, 2)].reshape(256, D)
        keyval[pl.ds(t * 2, 2)] = mm(n, wkv[...]).astype(BF).reshape(2, 128, 1024)

    steps(SHIFTED, project_kv)
    loads[2].wait()

    def project_q(t):
        s, part = t // 3, t % 3
        at = s * SHIFTED + part * 3
        n = normed[pl.ds(at, 3), :, pl.ds((1 - s) * 2, 2)].reshape(192, D)
        query[pl.ds(at, 3)] = (mm(n, wq[...]) * SCALE).astype(BF).reshape(3, 64, D)

    steps(6, project_q)
    key_row = (iota((1, 256), 1) // 8) % 8
    below = jnp.where(key_row < 4, F32(-1e30), F32(0))
    above = jnp.where(key_row < 4, F32(0), F32(-1e30))

    def one_attend(t):
        s = t // SHIFTED
        bias = above * last.astype(F32) if s else below * first.astype(F32)
        kv = keyval[t]
        heads[t] = attend(query[t], kv[:, :D], kv[:, D:], bias)

    steps(2 * SHIFTED, one_attend)
    loads[3].wait()

    def one_out(t):
        s, part = t // 3, t % 3
        out = mm(heads[pl.ds(s * SHIFTED + part * 3, 3)].reshape(192, D), wo[...])
        for u in range(3):
            w = part * 3 + u
            new = window(w, 4 + s * 4, 4) + out[u * 64 : u * 64 + 64].reshape(2, 4, 8, D)
            at = w * 8
            rows, here, after = pl.ds(s * 4, 4), pl.ds(at, 8), pl.ds(at + 8, 8)
            for c in range(4):
                piece = new[..., c * 128 : c * 128 + 128]
                old = x2[c, :, rows, here, :]
                x2[c, :, rows, here, :] = jnp.where(upper[:, :128], piece, old)
                x2[c, :, rows, after, :] = piece

    steps(6, one_out)
    loads[4].wait()

    def merge(t):
        level, half = t // 2, t % 2
        parts = []
        for p in range(4):
            got = [
                jnp.concatenate(
                    [
                        x2[c, level, half * 4 + 2 * a + p % 2, pl.ds(8 + p // 2, 32, stride=2), :]
                        for c in range(4)
                    ],
                    axis=1,
                )
                for a in range(2)
            ]
            parts.append(jnp.concatenate(got, axis=0))
        x = jnp.concatenate(parts, axis=1)
        n = normalize(x, mgain_ref[...]).astype(BF)
        out = mm(n, wm[...]).astype(BF)
        out_ref[level, pl.ds(half * 2, 2)] = out.reshape(2, 32, 1024)

    steps(4, merge)


def second_block(par, x1, near, norm_gain, merge_gain, w_query, w_keyval, w_out, merge_weight):
    vmem = pl.BlockSpec(memory_space=pltpu.VMEM)
    hbm = pl.BlockSpec(memory_space=pl.ANY)
    return pl.pallas_call(
        second_kernel,
        out_shape=jax.ShapeDtypeStruct((2, 4, 32, 1024), BF),
        in_specs=[pl.BlockSpec(memory_space=pltpu.SMEM), hbm] + [vmem] * 3 + [hbm] * 4,
        out_specs=vmem,
        scratch_shapes=[
            pltpu.VMEM((2, 16, 80, D), F32),
            pltpu.VMEM((4, 2, 8, 80, 128), F32),
            pltpu.VMEM((2 * SHIFTED, 2, 4, 16, D), BF),
            pltpu.VMEM((2 * SHIFTED, 64, D), BF),
            pltpu.VMEM((2 * SHIFTED, 128, 1024), BF),
            pltpu.VMEM((2 * SHIFTED, 64, D), BF),
            pltpu.VMEM((D, D), BF),
            pltpu.VMEM((D, 1024), BF),
            pltpu.VMEM((D, D), BF),
            pltpu.VMEM((4 * D, 1024), BF),
            pltpu.SemaphoreType.DMA((5,)),
        ],
        compiler_params=params(),
        cost_estimate=pl.CostEstimate(flops=10**10, bytes_accessed=10**7, transcendentals=0),
    )(par, x1, near, norm_gain, merge_gain, w_query, w_keyval, w_out, merge_weight)


def embedding_matrix(embed_weight, land_embed):
    w = embed_weight.reshape(3, 4, 3, 4, 6, D).transpose(0, 2, 3, 4, 1, 5)
    share = land_embed / 16
    high = lax.reduce_precision(share, 8, 7)
    terms = jnp.stack([high, share - high]).astype(BF)
    terms = jnp.broadcast_to(terms[None, :, None, :], (4, 2, 4, D))
    middle = (jnp.arange(9) == 4).reshape(3, 3, 1, 1, 1, 1)
    land = jnp.where(middle, terms, jnp.zeros((), BF))
    return jnp.concatenate([w, land], axis=3).reshape(9 * 128, D)


def swap(block, first):
    count = lax.axis_size("lat")
    pairs = []
    for i in range(first, count - 1, 2):
        pairs += [(i, i + 1), (i + 1, i)]
    return lax.ppermute(block, "lat", pairs)


def around(block, distance):
    count = lax.axis_size("lon")
    return lax.ppermute(block, "lon", [(i, (i + distance) % count) for i in range(count)])


def shards(
    atmos, orography, land_sea, embed_weight, level_embed, land_embed, norm_gain,
    w_query, w_keyval, w_out, merge_gain, merge_weight,
):
    lat = lax.axis_index("lat")
    par = lat % 2
    place = jnp.stack([par, lat == 0, lat == lax.axis_size("lat") - 1]).astype(jnp.int32)
    band, edge = patches(place, atmos, orography, land_sea)
    edge = swap(edge, 0)
    band = lax.dynamic_update_slice(band, edge, (8 * (1 - par), 0, 0))
    far = swap(band, 1)
    wemb = embedding_matrix(embed_weight, land_embed)
    far, wemb = lax.optimization_barrier((far, wemb))
    full, low, high = unpack(place, band, far)
    from_low, from_high = around(high, 1), around(low, -1)
    x1, send = first_block(
        place, full, from_low, from_high, wemb, level_embed, norm_gain, w_query, w_keyval, w_out
    )
    near = swap(send, 0)
    return second_block(
        place, x1, near, norm_gain, merge_gain.reshape(1, -1), w_query, w_keyval, w_out, merge_weight
    )


def solution(mesh):
    in_specs = (P(None, None, "lat", "lon"), P("lat", "lon"), P("lat", "lon")) + (P(),) * 9
    out_specs = P(None, "lat", "lon", None)
    return jax.shard_map(shards, mesh=mesh, in_specs=in_specs, out_specs=out_specs, check_vma=False)
```

```python
import math

import jax
import jax.numpy as jnp
from jax import lax
from jax.experimental import pallas as pl
from jax.experimental.pallas import tpu as pltpu
from jax.sharding import PartitionSpec as P

BF = jnp.bfloat16
F32 = jnp.float32
D = 512
HEAD_DIM = 64
WINS = 10
SCALE = HEAD_DIM ** (-0.5) * math.log2(math.e)
VMEM_LIMIT = 32 * 1024 * 1024


def iota(shape, dim):
    return lax.broadcasted_iota(jnp.int32, shape, dim)


def one_hot(cond):
    return jnp.where(cond, 1.0, 0.0).astype(BF)


def mm(a, b):
    return jnp.dot(a, b, preferred_element_type=F32)


def mm_t(a, b):
    return lax.dot_general(a, b, (((1,), (1,)), ((), ())), preferred_element_type=F32)


def params():
    return pltpu.CompilerParams(vmem_limit_bytes=VMEM_LIMIT)


def patch_kernel(par_ref, atmos_ref, oro_ref, land_ref, band_ref, edge_ref):
    par = par_ref[0]
    cells = jnp.concatenate(
        [
            atmos_ref[...].reshape(320, 256),
            oro_ref[...],
            land_ref[...].astype(F32).astype(BF),
        ],
        axis=0,
    )
    row, src = iota((1024, 384), 0), iota((1024, 384), 1)
    i, ch, r = row // 128, (row % 32) // 4, row % 4
    channel = jnp.where(ch < 5, ch, jnp.where(ch == 5, 10, jnp.where(ch == 6, 11, 9)))
    main = mm(one_hot(src == channel * 32 + i * 4 + r), cells)
    channel = 5 + (row % 16) // 4
    aux = mm(one_hot(src == channel * 32 + i * 4 + r), cells)
    row, col = iota((1024, 256), 0), iota((1024, 256), 1)
    c, half = (row % 128) // 32, (row % 32) // 16
    main = jnp.where(col % 4 == c, main, 0.0).astype(BF)
    aux = jnp.where((col % 4 == c) & (col // 128 == half), aux, 0.0).astype(BF)
    j, col = iota((64, 256), 0), iota((64, 256), 1)
    main = mm_t(one_hot(col // 4 == j), main).astype(BF)
    j, col = iota((32, 256), 0), iota((32, 256), 1)
    aux = mm_t(one_hot((col % 128) // 4 == j), aux).astype(BF)
    for i in range(8):
        band_ref[par + i, 0:64, :] = main[:, i * 128 : i * 128 + 128]
        band_ref[par + i, 64:96, :] = aux[:, i * 128 : i * 128 + 128]
    edge_ref[...] = band_ref[pl.ds(par + 7 * (1 - par), 1)]


def patches(par, atmos, orography, land_sea):
    return pl.pallas_call(
        patch_kernel,
        out_shape=(
            jax.ShapeDtypeStruct((9, 96, 128), BF),
            jax.ShapeDtypeStruct((1, 96, 128), BF),
        ),
        in_specs=[pl.BlockSpec(memory_space=pltpu.SMEM)] + [pl.BlockSpec(memory_space=pltpu.VMEM)] * 3,
        out_specs=(pl.BlockSpec(memory_space=pltpu.VMEM),) * 2,
        compiler_params=params(),
        cost_estimate=pl.CostEstimate(flops=10**9, bytes_accessed=10**6, transcendentals=0),
    )(par, atmos, orography, land_sea)


def unpack_kernel(par_ref, band_ref, far_ref, full_ref, low_ref, high_ref, packed):
    par = par_ref[0]
    packed[pl.ds(9 * (1 - par), 9)] = band_ref[...]
    packed[pl.ds(9 * par, 9)] = far_ref[...]
    k, n = iota((256, 256), 0), iota((256, 256), 1)
    ch, lane = (n % 32) // 4, n % 128
    from_main0 = jnp.where(ch == 7, lane - 4, lane)
    from_main1 = jnp.where(ch == 7, lane - 4, jnp.where(ch == 4, lane + 12, lane))
    aux = packed[:, 64:96, :]
    for half in range(2):
        from_one = jnp.where(ch < 4, 128 + lane + 16 * half, from_main1)
        pick = one_hot(k == jnp.where(n < 128, from_main0, from_one))
        both = jnp.concatenate([packed[:, half * 32 : half * 32 + 32, :], aux], axis=2)
        got = mm(both.reshape(18 * 32, 256), pick).astype(BF).reshape(18, 32, 256)
        for level in range(2):
            tile = got[:, :, level * 128 : level * 128 + 128]
            full_ref[level, :, half * 32 : half * 32 + 32, :] = tile
            if half == 0:
                low_ref[level] = tile[:, :16, :]
            else:
                high_ref[level] = tile[:, 16:, :]


def unpack(par, band, far):
    return pl.pallas_call(
        unpack_kernel,
        out_shape=(
            jax.ShapeDtypeStruct((2, 18, 64, 128), BF),
            jax.ShapeDtypeStruct((2, 18, 16, 128), BF),
            jax.ShapeDtypeStruct((2, 18, 16, 128), BF),
        ),
        in_specs=[pl.BlockSpec(memory_space=pltpu.SMEM)] + [pl.BlockSpec(memory_space=pltpu.VMEM)] * 2,
        out_specs=(pl.BlockSpec(memory_space=pltpu.VMEM),) * 3,
        scratch_shapes=[pltpu.VMEM((18, 96, 128), BF)],
        compiler_params=params(),
        cost_estimate=pl.CostEstimate(flops=10**9, bytes_accessed=10**6, transcendentals=0),
    )(par, band, far)


def pipelined(stages, groups):
    for step in range(len(groups) + len(stages) - 1):
        for k in reversed(range(len(stages))):
            if 0 <= step - k < len(groups):
                stages[k](groups[step - k])


def normalize(x, gain):
    mean = jnp.mean(x, axis=-1, keepdims=True)
    x = x - mean
    var = jnp.mean(x * x, axis=-1, keepdims=True)
    return x * lax.rsqrt(var + 1e-05) * gain


def attend(q, k, v, bias):
    left = iota((128, 128), 1) < HEAD_DIM
    ones_left, ones_right = one_hot(left), one_hot(~left)
    zero = jnp.zeros((128, 128), BF)
    out = []
    for pair in range(4):
        at = slice(pair * 128, pair * 128 + 128)
        kp, vp = k[:, at], v[:, at]
        keys = jnp.concatenate([jnp.where(left, kp, zero), jnp.where(left, zero, kp)], axis=0)
        s = mm_t(q[:, at], keys)
        if bias is not None:
            s = s + bias
        s0, s1 = s[:, :128], s[:, 128:]
        p0 = jnp.exp2(s0 - jnp.max(s0, axis=-1, keepdims=True))
        p1 = jnp.exp2(s1 - jnp.max(s1, axis=-1, keepdims=True))
        p = jnp.concatenate([p0, p1], axis=1).astype(BF)
        vals = jnp.concatenate(
            [
                jnp.concatenate([jnp.where(left, vp, zero), ones_left], axis=1),
                jnp.concatenate([jnp.where(left, zero, vp), ones_right], axis=1),
            ],
            axis=0,
        )
        o = mm(p, vals)
        out.append((o[:, :128] / o[:, 128:]).astype(BF))
    return jnp.concatenate(out, axis=1)


def first_kernel(
    par_ref, full_ref, low_ref, high_ref, wemb_ref, lev_ref, gain_ref, wq_ref, wkv_ref, wo_ref,
    x1_ref, send_ref,
    wide, gathered, x0, normed, query, keyval, heads,
):
    par = par_ref[0]
    wide[:, :, 0:16, :] = low_ref[...].astype(F32)
    wide[:, :, 16:80, :] = full_ref[...].astype(F32)
    wide[:, :, 80:96, :] = high_ref[...].astype(F32)
    gain = gain_ref[0:1, :]
    half = 1 - par

    def embed(group):
        part, g = group
        slot = part * 5 + g
        base = 8 * (par if part else half)
        for dj in range(3):
            cols = slice(g * 16 + 7 + dj, g * 16 + 23 + dj)
            got = wide[:, pl.ds(base, 10), cols, :].astype(BF)
            gathered[slot, :, :, :, dj * 128 : dj * 128 + 128] = got
        for level in range(2):
            lhs = jnp.concatenate(
                [gathered[slot, level, di : di + 8].reshape(128, 384) for di in range(3)], axis=1
            )
            x = mm(lhs, wemb_ref[...]) + lev_ref[level : level + 1, :]
            x0[slot, level] = x.reshape(8, 16, D)

    def norm(group):
        slot = group[0] * 5 + group[1]
        for u in range(2):
            x = x0[slot, :, :, u * 8 : u * 8 + 8, :].reshape(128, D)
            normed[slot, u] = normalize(x, gain).astype(BF).reshape(2, 4, 16, D)

    def project(group):
        slot = group[0] * 5 + group[1]
        n = normed[slot].reshape(256, D)
        keyval[slot] = mm(n, wkv_ref[0]).astype(BF).reshape(2, 128, 1024)
        if group[0]:
            n = normed[slot, :, :, pl.ds(half * 2, 2)].reshape(128, D)
        q = (mm(n, wq_ref[0]) * SCALE).astype(BF)
        query[slot, :, : q.shape[0] // 2] = q.reshape(2, -1, D)

    def attention(group):
        slot = group[0] * 5 + group[1]
        count = 64 if group[0] else 128
        for u in range(2):
            kv = keyval[slot, u]
            heads[slot, u, :count] = attend(query[slot, u, :count], kv[:, :D], kv[:, D:], None)

    def project_out(group):
        part, g = group
        slot = part * 5 + g
        count = 64 if part else 128
        out = mm(heads[slot, :, :count].reshape(2 * count, D), wo_ref[0])
        for u in range(2):
            cols = slice(g * 16 + u * 8, g * 16 + u * 8 + 8)
            mine = slice(u * 8, u * 8 + 8)
            add = out[u * count : u * count + count].reshape(2, count // 16, 8, D)
            if part:
                x1_ref[:, 0:4, cols, :] = x0[slot, :, pl.ds(4 * half, 4), mine, :] + add
            else:
                for h in range(2):
                    to = pl.ds(4 + 4 * (par if h == 0 else half), 4)
                    rows = slice(4 * h, 4 * h + 4)
                    x1_ref[:, to, cols, :] = x0[slot, :, rows, mine, :] + add[:, rows]

    groups = [(part, g) for part in range(2) for g in range(5)]
    pipelined([embed, norm, project, attention, project_out], groups)
    send_ref[...] = x1_ref[:, 8:12].astype(BF)


def first_block(par, full, low, high, wemb, level_embed, norm_gain, w_query, w_keyval, w_out):
    vmem = pl.BlockSpec(memory_space=pltpu.VMEM)
    return pl.pallas_call(
        first_kernel,
        out_shape=(
            jax.ShapeDtypeStruct((2, 12, 80, D), F32),
            jax.ShapeDtypeStruct((2, 4, 80, D), BF),
        ),
        in_specs=[pl.BlockSpec(memory_space=pltpu.SMEM)] + [vmem] * 9,
        out_specs=(vmem, vmem),
        scratch_shapes=[
            pltpu.VMEM((2, 18, 96, 128), F32),
            pltpu.VMEM((10, 2, 10, 16, 384), BF),
            pltpu.VMEM((10, 2, 8, 16, D), F32),
            pltpu.VMEM((10, 2, 2, 4, 16, D), BF),
            pltpu.VMEM((10, 2, 128, D), BF),
            pltpu.VMEM((10, 2, 128, 1024), BF),
            pltpu.VMEM((10, 2, 128, D), BF),
        ],
        compiler_params=params(),
        cost_estimate=pl.CostEstimate(flops=2 * 10**10, bytes_accessed=10**7, transcendentals=0),
    )(par, full, low, high, wemb, level_embed, norm_gain, w_query, w_keyval, w_out)


SHIFTED = WINS - 1


def second_kernel(
    par_ref, x1_ref, near_ref, gain_ref, mgain_ref, wq_ref, wkv_ref, wo_ref, wm_ref,
    out_ref,
    near, x2, normed, query, keyval, heads,
):
    par, pole = par_ref[0], par_ref[1]
    near[...] = near_ref[...].astype(F32)
    gain = gain_ref[1:2, :]
    upper = iota((8, D), 0) >= 4
    key_row = (iota((1, 256), 1) // 8) % 8
    bias = jnp.where(key_row < 4, F32(-1e30), F32(0)) * pole.astype(F32)

    def window(ref, w, rows):
        a = ref[:, rows, w * 8 : w * 8 + 8, :]
        b = ref[:, rows, w * 8 + 8 : w * 8 + 16, :]
        return jnp.where(upper, a, b)

    def norm(group):
        s, g = group
        for w in range(g * 3, g * 3 + 3):
            if s == 0:
                x = window(x1_ref, w, slice(0, 8))
            else:
                x = jnp.concatenate(
                    [window(x1_ref, w, slice(8, 12)), window(near, w, slice(0, 4))], axis=1
                )
            n = normalize(x.reshape(128, D), gain).astype(BF)
            normed[s * SHIFTED + w] = n.reshape(2, 4, 16, D)

    def project(group):
        s, g = group
        at = slice(s * SHIFTED + g * 3, s * SHIFTED + g * 3 + 3)
        n = normed[at].reshape(384, D)
        keyval[at] = mm(n, wkv_ref[1]).astype(BF).reshape(3, 128, 1024)
        n = normed[at, :, 2 - 2 * s : 4 - 2 * s].reshape(192, D)
        query[at] = (mm(n, wq_ref[1]) * SCALE).astype(BF).reshape(3, 64, D)

    def attention(group):
        s, g = group
        for t in range(s * SHIFTED + g * 3, s * SHIFTED + g * 3 + 3):
            kv = keyval[t]
            heads[t] = attend(query[t], kv[:, :D], kv[:, D:], None if s else bias)

    def project_out(group):
        s, g = group
        at = slice(s * SHIFTED + g * 3, s * SHIFTED + g * 3 + 3)
        out = mm(heads[at].reshape(192, D), wo_ref[1])
        rows = slice(s * 4, s * 4 + 4)
        for u in range(3):
            w = g * 3 + u
            new = window(x1_ref, w, slice(4 + s * 4, 8 + s * 4))
            new = new + out[u * 64 : u * 64 + 64].reshape(2, 4, 8, D)
            for c in range(4):
                piece = new[..., c * 128 : c * 128 + 128]
                x2[c, :, rows, w * 8 + 4 : w * 8 + 8, :] = piece[:, :, 4:8, :]
                x2[c, :, rows, w * 8 + 8 : w * 8 + 12, :] = piece[:, :, 0:4, :]

    def merge(group):
        s, g = group
        if g < 2:
            return
        parts = []
        for p in range(4):
            got = [
                jnp.concatenate(
                    [
                        x2[c, level, s * 4 + 2 * a + p % 2, pl.ds(8 + p // 2, 32, stride=2), :]
                        for c in range(4)
                    ],
                    axis=1,
                )
                for level in range(2)
                for a in range(2)
            ]
            parts.append(jnp.concatenate(got, axis=0))
        n = normalize(jnp.concatenate(parts, axis=1), mgain_ref[...]).astype(BF)
        out = mm(n, wm_ref[...]).astype(BF)
        out_ref[:, pl.ds(2 * ((par + s) % 2), 2)] = out.reshape(2, 2, 32, 1024)

    groups = [(s, g) for s in range(2) for g in range(3)]
    pipelined([norm, project, attention, project_out, merge], groups)


def second_block(par, x1, near, norm_gain, merge_gain, w_query, w_keyval, w_out, merge_weight):
    vmem = pl.BlockSpec(memory_space=pltpu.VMEM)
    return pl.pallas_call(
        second_kernel,
        out_shape=jax.ShapeDtypeStruct((2, 4, 32, 1024), BF),
        in_specs=[pl.BlockSpec(memory_space=pltpu.SMEM)] + [vmem] * 8,
        out_specs=vmem,
        scratch_shapes=[
            pltpu.VMEM((2, 4, 80, D), F32),
            pltpu.VMEM((4, 2, 8, 80, 128), F32),
            pltpu.VMEM((2 * SHIFTED, 2, 4, 16, D), BF),
            pltpu.VMEM((2 * SHIFTED, 64, D), BF),
            pltpu.VMEM((2 * SHIFTED, 128, 1024), BF),
            pltpu.VMEM((2 * SHIFTED, 64, D), BF),
        ],
        compiler_params=params(),
        cost_estimate=pl.CostEstimate(flops=10**10, bytes_accessed=10**7, transcendentals=0),
    )(par, x1, near, norm_gain, merge_gain, w_query, w_keyval, w_out, merge_weight)


def embedding_matrix(embed_weight, land_embed):
    w = embed_weight.reshape(3, 4, 3, 4, 6, D).transpose(0, 2, 3, 4, 1, 5)
    share = land_embed / 16
    high = lax.reduce_precision(share, 8, 7)
    terms = jnp.stack([high, share - high]).astype(BF)
    terms = jnp.broadcast_to(terms[None, :, None, :], (4, 2, 4, D))
    middle = (jnp.arange(9) == 4).reshape(3, 3, 1, 1, 1, 1)
    land = jnp.where(middle, terms, jnp.zeros((), BF))
    return jnp.concatenate([w, land], axis=3).reshape(9 * 128, D)


def swap(block, first):
    count = lax.axis_size("lat")
    pairs = []
    for i in range(first, count - 1, 2):
        pairs += [(i, i + 1), (i + 1, i)]
    return lax.ppermute(block, "lat", pairs)


def around(block, distance):
    count = lax.axis_size("lon")
    return lax.ppermute(block, "lon", [(i, (i + distance) % count) for i in range(count)])


def shards(
    atmos, orography, land_sea, embed_weight, level_embed, land_embed, norm_gain,
    w_query, w_keyval, w_out, merge_gain, merge_weight,
):
    w_query, w_keyval, w_out, merge_weight = [
        pltpu.with_memory_space_constraint(w, pltpu.VMEM) for w in (w_query, w_keyval, w_out, merge_weight)
    ]
    lat = lax.axis_index("lat")
    par = lat % 2
    pole = (lat == 0) | (lat == lax.axis_size("lat") - 1)
    place = jnp.stack([par, pole]).astype(jnp.int32)
    band, edge = patches(place, atmos, orography, land_sea)
    edge = swap(edge, 0)
    band = lax.dynamic_update_slice(band, edge, (8 * (1 - par), 0, 0))
    far = swap(band, 1)
    wemb = embedding_matrix(embed_weight, land_embed)
    far, wemb = lax.optimization_barrier((far, wemb))
    full, low, high = unpack(place, band, far)
    from_low, from_high = around(high, 1), around(low, -1)
    x1, send = first_block(
        place, full, from_low, from_high, wemb, level_embed, norm_gain, w_query, w_keyval, w_out
    )
    near = swap(send, 0)
    return second_block(
        place, x1, near, norm_gain, merge_gain.reshape(1, -1), w_query, w_keyval, w_out, merge_weight
    )


def solution(mesh):
    in_specs = (P(None, None, "lat", "lon"), P("lat", "lon"), P("lat", "lon")) + (P(),) * 9
    out_specs = P(None, "lat", "lon", None)
    return jax.shard_map(shards, mesh=mesh, in_specs=in_specs, out_specs=out_specs, check_vma=False)
```

```python
import functools
import math

import jax
import jax.numpy as jnp
from jax import lax
from jax.experimental import pallas as pl
from jax.experimental.pallas import tpu as pltpu
from jax.sharding import PartitionSpec as P

BF = jnp.bfloat16
F32 = jnp.float32
D = 512
HEAD_DIM = 64
WINS = 10
SCALE = HEAD_DIM ** (-0.5) * math.log2(math.e)
VMEM_LIMIT = 32 * 1024 * 1024


def iota(shape, dim):
    return lax.broadcasted_iota(jnp.int32, shape, dim)


def one_hot(cond):
    return jnp.where(cond, 1.0, 0.0).astype(BF)


def mm(a, b):
    return jnp.dot(a, b, preferred_element_type=F32)


def mm_t(a, b):
    return lax.dot_general(a, b, (((1,), (1,)), ((), ())), preferred_element_type=F32)


def params():
    return pltpu.CompilerParams(vmem_limit_bytes=VMEM_LIMIT)


def patch_kernel(
    par_ref, atmos_any, oro_any, land_any, band_ref, edge_ref, atmos_ref, oro_ref, land_ref, sems
):
    par = par_ref[0]
    loads = [
        pltpu.make_async_copy(src, dst, sems.at[n])
        for n, (src, dst) in enumerate(
            [(atmos_any, atmos_ref), (oro_any, oro_ref), (land_any, land_ref)]
        )
    ]
    for load in loads:
        load.start()
    for load in loads:
        load.wait()
    cells = jnp.concatenate(
        [
            atmos_ref[...].reshape(320, 256),
            oro_ref[...],
            land_ref[...].astype(F32).astype(BF),
        ],
        axis=0,
    )
    row, src = iota((1024, 384), 0), iota((1024, 384), 1)
    i, ch, r = row // 128, (row % 32) // 4, row % 4
    channel = jnp.where(ch < 5, ch, jnp.where(ch == 5, 10, jnp.where(ch == 6, 11, 9)))
    main = mm(one_hot(src == channel * 32 + i * 4 + r), cells)
    channel = 5 + (row % 16) // 4
    aux = mm(one_hot(src == channel * 32 + i * 4 + r), cells)
    row, col = iota((1024, 256), 0), iota((1024, 256), 1)
    c, half = (row % 128) // 32, (row % 32) // 16
    main = jnp.where(col % 4 == c, main, 0.0).astype(BF)
    aux = jnp.where((col % 4 == c) & (col // 128 == half), aux, 0.0).astype(BF)
    j, col = iota((64, 256), 0), iota((64, 256), 1)
    main = mm_t(one_hot(col // 4 == j), main).astype(BF)
    j, col = iota((32, 256), 0), iota((32, 256), 1)
    aux = mm_t(one_hot((col % 128) // 4 == j), aux).astype(BF)
    for i in range(8):
        band_ref[par + i, 0:64, :] = main[:, i * 128 : i * 128 + 128]
        band_ref[par + i, 64:96, :] = aux[:, i * 128 : i * 128 + 128]
    edge_ref[...] = band_ref[pl.ds(par + 7 * (1 - par), 1)]


def patches(par, atmos, orography, land_sea):
    return pl.pallas_call(
        patch_kernel,
        out_shape=(
            jax.ShapeDtypeStruct((9, 96, 128), BF),
            jax.ShapeDtypeStruct((1, 96, 128), BF),
        ),
        in_specs=[pl.BlockSpec(memory_space=pltpu.SMEM)] + [pl.BlockSpec(memory_space=pltpu.HBM)] * 3,
        out_specs=(pl.BlockSpec(memory_space=pltpu.VMEM),) * 2,
        scratch_shapes=[
            pltpu.VMEM(atmos.shape, BF),
            pltpu.VMEM(orography.shape, BF),
            pltpu.VMEM(land_sea.shape, jnp.int32),
            pltpu.SemaphoreType.DMA((3,)),
        ],
        compiler_params=params(),
        cost_estimate=pl.CostEstimate(flops=10**9, bytes_accessed=10**6, transcendentals=0),
    )(par, atmos, orography, land_sea)


def unpack_kernel(par_ref, band_ref, far_ref, full_ref, low_ref, high_ref, packed):
    par = par_ref[0]
    packed[pl.ds(9 * (1 - par), 9)] = band_ref[...]
    packed[pl.ds(9 * par, 9)] = far_ref[...]
    k, n = iota((256, 256), 0), iota((256, 256), 1)
    ch, lane = (n % 32) // 4, n % 128
    from_main0 = jnp.where(ch == 7, lane - 4, lane)
    from_main1 = jnp.where(ch == 7, lane - 4, jnp.where(ch == 4, lane + 12, lane))
    aux = packed[:, 64:96, :]
    for half in range(2):
        from_one = jnp.where(ch < 4, 128 + lane + 16 * half, from_main1)
        pick = one_hot(k == jnp.where(n < 128, from_main0, from_one))
        both = jnp.concatenate([packed[:, half * 32 : half * 32 + 32, :], aux], axis=2)
        got = mm(both.reshape(18 * 32, 256), pick).astype(BF).reshape(18, 32, 256)
        for level in range(2):
            tile = got[:, :, level * 128 : level * 128 + 128]
            full_ref[level, :, half * 32 : half * 32 + 32, :] = tile
            if half == 0:
                low_ref[level] = tile[:, :16, :]
            else:
                high_ref[level] = tile[:, 16:, :]


def unpack(par, band, far):
    return pl.pallas_call(
        unpack_kernel,
        out_shape=(
            jax.ShapeDtypeStruct((2, 18, 64, 128), BF),
            jax.ShapeDtypeStruct((2, 18, 16, 128), BF),
            jax.ShapeDtypeStruct((2, 18, 16, 128), BF),
        ),
        in_specs=[pl.BlockSpec(memory_space=pltpu.SMEM)] + [pl.BlockSpec(memory_space=pltpu.VMEM)] * 2,
        out_specs=(pl.BlockSpec(memory_space=pltpu.VMEM),) * 3,
        scratch_shapes=[pltpu.VMEM((18, 96, 128), BF)],
        compiler_params=params(),
        cost_estimate=pl.CostEstimate(flops=10**9, bytes_accessed=10**6, transcendentals=0),
    )(par, band, far)


def pipelined(stages, groups):
    for step in range(len(groups) + len(stages) - 1):
        for k in range(len(stages)):
            if 0 <= step - k < len(groups):
                stages[k](groups[step - k])


def normalize(x, gain):
    mean = jnp.mean(x, axis=-1, keepdims=True)
    x = x - mean
    var = jnp.mean(x * x, axis=-1, keepdims=True)
    return x * lax.rsqrt(var + 1e-05) * gain


def attend(q, k, v, bias):
    left = iota((128, 128), 1) < HEAD_DIM
    ones_left, ones_right = one_hot(left), one_hot(~left)
    zero = jnp.zeros((128, 128), BF)
    out = []
    for pair in range(4):
        at = slice(pair * 128, pair * 128 + 128)
        kp, vp = k[:, at], v[:, at]
        keys = jnp.concatenate([jnp.where(left, kp, zero), jnp.where(left, zero, kp)], axis=0)
        s = mm_t(q[:, at], keys)
        if bias is not None:
            s = s + bias
        s0, s1 = s[:, :128], s[:, 128:]
        p0 = jnp.exp2(s0 - jnp.max(s0, axis=-1, keepdims=True))
        p1 = jnp.exp2(s1 - jnp.max(s1, axis=-1, keepdims=True))
        p = jnp.concatenate([p0, p1], axis=1).astype(BF)
        vals = jnp.concatenate(
            [
                jnp.concatenate([jnp.where(left, vp, zero), ones_left], axis=1),
                jnp.concatenate([jnp.where(left, zero, vp), ones_right], axis=1),
            ],
            axis=0,
        )
        o = mm(p, vals)
        out.append((o[:, :128] / o[:, 128:]).astype(BF))
    return jnp.concatenate(out, axis=1)


MIDDLE, EDGES = (1, 2, 3), (0, 4)


def first_kernel(which, *refs):
    par_ref, full_ref, refs = refs[0], refs[1], refs[2:]
    if which == EDGES:
        low_ref, high_ref, refs = refs[0], refs[1], refs[2:]
    wemb_ref, lev_ref, gain_ref, wq_ref, wkv_ref, wo_ref, x1_ref, send_ref, *refs = refs
    wide, gathered, x0, normed, query, keyval, heads = refs
    par = par_ref[0]
    if which == EDGES:
        wide[:, :, 0:16, :] = low_ref[...].astype(F32)
        wide[:, :, 16:32, :] = full_ref[:, :, 0:16, :].astype(F32)
        wide[:, :, 64:80, :] = full_ref[:, :, 48:64, :].astype(F32)
        wide[:, :, 80:96, :] = high_ref[...].astype(F32)
    else:
        wide[:, :, 16:80, :] = full_ref[...].astype(F32)
    gain = gain_ref[0:1, :]
    half = 1 - par

    def embed(group):
        part, g = group
        slot = part * len(which) + which.index(g)
        base = 8 * (par if part else half)
        for dj in range(3):
            cols = slice(g * 16 + 7 + dj, g * 16 + 23 + dj)
            got = wide[:, pl.ds(base, 10), cols, :].astype(BF)
            gathered[slot, :, :, :, dj * 128 : dj * 128 + 128] = got
        for level in range(2):
            lhs = jnp.concatenate(
                [gathered[slot, level, di : di + 8].reshape(128, 384) for di in range(3)], axis=1
            )
            x = mm(lhs, wemb_ref[...]) + lev_ref[level : level + 1, :]
            x0[slot, level] = x.reshape(8, 16, D)

    def norm(group):
        slot = group[0] * len(which) + which.index(group[1])
        for u in range(2):
            x = x0[slot, :, :, u * 8 : u * 8 + 8, :].reshape(128, D)
            normed[slot, u] = normalize(x, gain).astype(BF).reshape(2, 4, 16, D)

    def project(group):
        slot = group[0] * len(which) + which.index(group[1])
        n = normed[slot].reshape(256, D)
        keyval[slot] = mm(n, wkv_ref[0]).astype(BF).reshape(2, 128, 1024)
        if group[0]:
            n = normed[slot, :, :, pl.ds(half * 2, 2)].reshape(128, D)
        q = (mm(n, wq_ref[0]) * SCALE).astype(BF)
        query[slot, :, : q.shape[0] // 2] = q.reshape(2, -1, D)

    def attention(group):
        slot = group[0] * len(which) + which.index(group[1])
        count = 64 if group[0] else 128
        for u in range(2):
            kv = keyval[slot, u]
            heads[slot, u, :count] = attend(query[slot, u, :count], kv[:, :D], kv[:, D:], None)

    def project_out(group):
        part, g = group
        slot = part * len(which) + which.index(g)
        count = 64 if part else 128
        out = mm(heads[slot, :, :count].reshape(2 * count, D), wo_ref[0])
        for u in range(2):
            at = which.index(g) * 16 + u * 8
            cols = slice(at, at + 8)
            mine = slice(u * 8, u * 8 + 8)
            add = out[u * count : u * count + count].reshape(2, count // 16, 8, D)
            if part:
                x1_ref[:, 0:4, cols, :] = x0[slot, :, pl.ds(4 * half, 4), mine, :] + add
            else:
                for h in range(2):
                    to = pl.ds(4 + 4 * (par if h == 0 else half), 4)
                    rows = slice(4 * h, 4 * h + 4)
                    x1_ref[:, to, cols, :] = x0[slot, :, rows, mine, :] + add[:, rows]

    groups = [(part, g) for part in range(2) for g in which]
    pipelined([embed, norm, project, attention, project_out], groups)
    send_ref[...] = x1_ref[:, 8:12].astype(BF)


def first_block(which, par, patch_arrays, wemb, level_embed, norm_gain, w_query, w_keyval, w_out):
    vmem = pl.BlockSpec(memory_space=pltpu.VMEM)
    count = 2 * len(which)
    return pl.pallas_call(
        functools.partial(first_kernel, which),
        out_shape=(
            jax.ShapeDtypeStruct((2, 12, 8 * count, D), F32),
            jax.ShapeDtypeStruct((2, 4, 8 * count, D), BF),
        ),
        in_specs=[pl.BlockSpec(memory_space=pltpu.SMEM)] + [vmem] * (6 + len(patch_arrays)),
        out_specs=(vmem, vmem),
        scratch_shapes=[
            pltpu.VMEM((2, 18, 96, 128), F32),
            pltpu.VMEM((count, 2, 10, 16, 384), BF),
            pltpu.VMEM((count, 2, 8, 16, D), F32),
            pltpu.VMEM((count, 2, 2, 4, 16, D), BF),
            pltpu.VMEM((count, 2, 128, D), BF),
            pltpu.VMEM((count, 2, 128, 1024), BF),
            pltpu.VMEM((count, 2, 128, D), BF),
        ],
        compiler_params=params(),
        cost_estimate=pl.CostEstimate(flops=10**10, bytes_accessed=10**7, transcendentals=0),
    )(par, *patch_arrays, wemb, level_embed, norm_gain, w_query, w_keyval, w_out)


SHIFTED = WINS - 1


def second_kernel(
    par_ref, mid_ref, edge_ref, near_mid_ref, near_edge_ref, gain_ref, mgain_ref,
    wq_ref, wkv_ref, wo_ref, wm_ref,
    out_ref,
    near, x2, normed, query, keyval, heads,
):
    par, pole = par_ref[0], par_ref[1]
    near[:, :, 0:16, :] = near_edge_ref[:, :, 0:16, :].astype(F32)
    near[:, :, 16:64, :] = near_mid_ref[...].astype(F32)
    near[:, :, 64:80, :] = near_edge_ref[:, :, 16:32, :].astype(F32)
    gain = gain_ref[1:2, :]
    upper = iota((8, D), 0) >= 4
    key_row = (iota((1, 256), 1) // 8) % 8
    bias = jnp.where(key_row < 4, F32(-1e30), F32(0)) * pole.astype(F32)

    def block(n, first, last):
        if first >= 12:
            return near[:, first - 12 : last - 12, n * 8 : n * 8 + 8, :]
        if 2 <= n < 8:
            return mid_ref[:, first:last, n * 8 - 16 : n * 8 - 8, :]
        at = n * 8 - (48 if n >= 8 else 0)
        return edge_ref[:, first:last, at : at + 8, :]

    def window(w, first, last):
        return jnp.where(upper, block(w, first, last), block(w + 1, first, last))

    def norm(group):
        s, g = group
        for w in range(g * 3, g * 3 + 3):
            if s == 0:
                x = window(w, 0, 8)
            else:
                x = jnp.concatenate(
                    [window(w, 8, 12), window(w, 12, 16)], axis=1
                )
            n = normalize(x.reshape(128, D), gain).astype(BF)
            normed[s * SHIFTED + w] = n.reshape(2, 4, 16, D)

    def project(group):
        s, g = group
        at = slice(s * SHIFTED + g * 3, s * SHIFTED + g * 3 + 3)
        n = normed[at].reshape(384, D)
        keyval[at] = mm(n, wkv_ref[1]).astype(BF).reshape(3, 128, 1024)
        n = normed[at, :, 2 - 2 * s : 4 - 2 * s].reshape(192, D)
        query[at] = (mm(n, wq_ref[1]) * SCALE).astype(BF).reshape(3, 64, D)

    def attention(group):
        s, g = group
        for t in range(s * SHIFTED + g * 3, s * SHIFTED + g * 3 + 3):
            kv = keyval[t]
            heads[t] = attend(query[t], kv[:, :D], kv[:, D:], None if s else bias)

    def project_out(group):
        s, g = group
        at = slice(s * SHIFTED + g * 3, s * SHIFTED + g * 3 + 3)
        out = mm(heads[at].reshape(192, D), wo_ref[1])
        rows = slice(s * 4, s * 4 + 4)
        for u in range(3):
            w = g * 3 + u
            new = window(w, 4 + s * 4, 8 + s * 4)
            new = new + out[u * 64 : u * 64 + 64].reshape(2, 4, 8, D)
            for c in range(4):
                piece = new[..., c * 128 : c * 128 + 128]
                x2[c, :, rows, w * 8 + 4 : w * 8 + 8, :] = piece[:, :, 4:8, :]
                x2[c, :, rows, w * 8 + 8 : w * 8 + 12, :] = piece[:, :, 0:4, :]

    def merge(group):
        s, g = group
        if g < 2:
            return
        parts = []
        for p in range(4):
            got = [
                jnp.concatenate(
                    [
                        x2[c, level, s * 4 + 2 * a + p % 2, pl.ds(8 + p // 2, 32, stride=2), :]
                        for c in range(4)
                    ],
                    axis=1,
                )
                for level in range(2)
                for a in range(2)
            ]
            parts.append(jnp.concatenate(got, axis=0))
        n = normalize(jnp.concatenate(parts, axis=1), mgain_ref[...]).astype(BF)
        out = mm(n, wm_ref[...]).astype(BF)
        out_ref[:, pl.ds(2 * ((par + s) % 2), 2)] = out.reshape(2, 2, 32, 1024)

    groups = [(s, g) for s in range(2) for g in range(3)]
    pipelined([norm, project, attention, project_out, merge], groups)


def second_block(par, mid, edge, near_mid, near_edge, norm_gain, merge_gain, w_query, w_keyval, w_out, merge_weight):
    vmem = pl.BlockSpec(memory_space=pltpu.VMEM)
    return pl.pallas_call(
        second_kernel,
        out_shape=jax.ShapeDtypeStruct((2, 4, 32, 1024), BF),
        in_specs=[pl.BlockSpec(memory_space=pltpu.SMEM)] + [vmem] * 10,
        out_specs=vmem,
        scratch_shapes=[
            pltpu.VMEM((2, 4, 80, D), F32),
            pltpu.VMEM((4, 2, 8, 80, 128), F32),
            pltpu.VMEM((2 * SHIFTED, 2, 4, 16, D), BF),
            pltpu.VMEM((2 * SHIFTED, 64, D), BF),
            pltpu.VMEM((2 * SHIFTED, 128, 1024), BF),
            pltpu.VMEM((2 * SHIFTED, 64, D), BF),
        ],
        compiler_params=params(),
        cost_estimate=pl.CostEstimate(flops=10**10, bytes_accessed=10**7, transcendentals=0),
    )(
        par, mid, edge, near_mid, near_edge, norm_gain, merge_gain, w_query, w_keyval, w_out, merge_weight
    )


def embedding_matrix(embed_weight, land_embed):
    w = embed_weight.reshape(3, 4, 3, 4, 6, D).transpose(0, 2, 3, 4, 1, 5)
    share = land_embed / 16
    high = lax.reduce_precision(share, 8, 7)
    terms = jnp.stack([high, share - high]).astype(BF)
    terms = jnp.broadcast_to(terms[None, :, None, :], (4, 2, 4, D))
    middle = (jnp.arange(9) == 4).reshape(3, 3, 1, 1, 1, 1)
    land = jnp.where(middle, terms, jnp.zeros((), BF))
    return jnp.concatenate([w, land], axis=3).reshape(9 * 128, D)


def swap(block, first):
    count = lax.axis_size("lat")
    pairs = []
    for i in range(first, count - 1, 2):
        pairs += [(i, i + 1), (i + 1, i)]
    return lax.ppermute(block, "lat", pairs)


def around(block, distance):
    count = lax.axis_size("lon")
    return lax.ppermute(block, "lon", [(i, (i + distance) % count) for i in range(count)])


def shards(
    atmos, orography, land_sea, embed_weight, level_embed, land_embed, norm_gain,
    w_query, w_keyval, w_out, merge_gain, merge_weight,
):
    w_query, w_keyval, w_out, merge_weight = [
        pltpu.with_memory_space_constraint(w, pltpu.VMEM) for w in (w_query, w_keyval, w_out, merge_weight)
    ]
    lat = lax.axis_index("lat")
    par = lat % 2
    pole = (lat == 0) | (lat == lax.axis_size("lat") - 1)
    place = jnp.stack([par, pole]).astype(jnp.int32)
    band, edge = patches(place, atmos, orography, land_sea)
    edge = swap(edge, 0)
    band = lax.dynamic_update_slice(band, edge, (8 * (1 - par), 0, 0))
    far = swap(band, 1)
    wemb = embedding_matrix(embed_weight, land_embed)
    far, wemb = lax.optimization_barrier((far, wemb))
    full, low, high = unpack(place, band, far)
    from_low, from_high = around(high, 1), around(low, -1)
    weights = wemb, level_embed, norm_gain, w_query, w_keyval, w_out
    mid, send_mid = first_block(MIDDLE, place, (full,), *weights)
    near_mid = swap(send_mid, 0)
    edge, send_edge = first_block(EDGES, place, (full, from_low, from_high), *weights)
    near_edge = swap(send_edge, 0)
    return second_block(
        place, mid, edge, near_mid, near_edge, norm_gain, merge_gain.reshape(1, -1),
        w_query, w_keyval, w_out, merge_weight,
    )


def solution(mesh):
    in_specs = (P(None, None, "lat", "lon"), P("lat", "lon"), P("lat", "lon")) + (P(),) * 9
    out_specs = P(None, "lat", "lon", None)
    return jax.shard_map(shards, mesh=mesh, in_specs=in_specs, out_specs=out_specs, check_vma=False)
```

```python
import functools
import math

import jax
import jax.numpy as jnp
from jax import lax
from jax.experimental import pallas as pl
from jax.experimental.pallas import tpu as pltpu
from jax.sharding import PartitionSpec as P

BF = jnp.bfloat16
F32 = jnp.float32
D = 512
HEAD_DIM = 64
WINS = 10
SCALE = HEAD_DIM ** (-0.5) * math.log2(math.e)
VMEM_LIMIT = 32 * 1024 * 1024


def iota(shape, dim):
    return lax.broadcasted_iota(jnp.int32, shape, dim)


def one_hot(cond):
    return jnp.where(cond, 1.0, 0.0).astype(BF)


def mm(a, b):
    return jnp.dot(a, b, preferred_element_type=F32)


def mm_t(a, b):
    return lax.dot_general(a, b, (((1,), (1,)), ((), ())), preferred_element_type=F32)


def params():
    return pltpu.CompilerParams(vmem_limit_bytes=VMEM_LIMIT)


def patch_kernel(
    par_ref, atmos_any, oro_any, land_any, own_ref, send_ref, edge_ref, near_ref,
    atmos_ref, oro_ref, land_ref, sems,
):
    par = par_ref[0]
    loads = [
        pltpu.make_async_copy(src, dst, sems.at[n])
        for n, (src, dst) in enumerate(
            [(atmos_any, atmos_ref), (oro_any, oro_ref), (land_any, land_ref)]
        )
    ]
    for load in loads:
        load.start()
    row, src = iota((1024, 384), 0), iota((1024, 384), 1)
    i, r, ch = row // 128, (row % 128) // 32, row % 8
    channel = jnp.where(ch < 5, ch, jnp.where(ch == 5, 10, jnp.where(ch == 6, 11, 9)))
    pick_main = one_hot(src == channel * 32 + i * 4 + r)
    pick_aux = one_hot(src == (5 + row % 4) * 32 + i * 4 + r)
    for load in loads:
        load.wait()
    cells = jnp.concatenate(
        [
            atmos_ref[...].reshape(320, 256),
            oro_ref[...],
            land_ref[...].astype(F32).astype(BF),
        ],
        axis=0,
    )
    main, aux = mm(pick_main, cells), mm(pick_aux, cells)
    row, col = iota((1024, 256), 0), iota((1024, 256), 1)
    c, half = (row % 32) // 8, (row % 8) // 4
    main = jnp.where(col % 4 == c, main, 0.0).astype(BF)
    aux = jnp.where((col % 4 == c) & (col // 128 == half), aux, 0.0).astype(BF)
    j, col = iota((64, 256), 0), iota((64, 256), 1)
    main = mm_t(one_hot(col // 4 == j), main).astype(BF)
    j, col = iota((32, 256), 0), iota((32, 256), 1)
    aux = mm_t(one_hot((col % 128) // 4 == j), aux).astype(BF)
    for i in range(8):
        own_ref[i, 0:64, :] = main[:, i * 128 : i * 128 + 128]
        own_ref[i, 64:96, :] = aux[:, i * 128 : i * 128 + 128]
    send_ref[pl.ds(par, 7)] = own_ref[pl.ds(1 - par, 7)]
    edge_ref[...] = own_ref[pl.ds(7 * (1 - par), 1)]
    near_ref[...] = own_ref[pl.ds(7 * par, 1)]


def patches(par, atmos, orography, land_sea):
    cells = [pltpu.with_memory_space_constraint(a, pltpu.HBM) for a in (atmos, orography, land_sea)]
    return pl.pallas_call(
        patch_kernel,
        out_shape=tuple(jax.ShapeDtypeStruct((n, 96, 128), BF) for n in (8, 8, 1, 1)),
        in_specs=[pl.BlockSpec(memory_space=pltpu.SMEM)] + [pl.BlockSpec(memory_space=pltpu.HBM)] * 3,
        out_specs=(pl.BlockSpec(memory_space=pltpu.VMEM),) * 4,
        scratch_shapes=[
            pltpu.VMEM(atmos.shape, BF),
            pltpu.VMEM(orography.shape, BF),
            pltpu.VMEM(land_sea.shape, jnp.int32),
            pltpu.SemaphoreType.DMA((3,)),
        ],
        compiler_params=params(),
        cost_estimate=pl.CostEstimate(flops=10**9, bytes_accessed=10**6, transcendentals=0),
    )(par, *cells)


def unpack_rows(packed, out_ref):
    rows = packed.shape[0]
    k, n = iota((256, 256), 0), iota((256, 256), 1)
    ch, lane = n % 8, n % 128
    from_main0 = jnp.where(ch == 7, lane - 1, lane)
    from_main1 = jnp.where(ch == 7, lane - 1, jnp.where(ch == 4, lane + 3, lane))
    aux = packed[:, 64:96, :]
    for half in range(2):
        from_one = jnp.where(ch < 4, 128 + lane + 4 * half, from_main1)
        pick = one_hot(k == jnp.where(n < 128, from_main0, from_one))
        both = jnp.concatenate([packed[:, half * 32 : half * 32 + 32, :], aux], axis=2)
        got = mm(both.reshape(rows * 32, 256), pick).astype(BF).reshape(rows, 32, 256)
        for level in range(2):
            tile = got[:, :, level * 128 : level * 128 + 128]
            out_ref[level, :, half * 32 : half * 32 + 32, :] = tile


def unpack_own_kernel(par_ref, own_ref, edge_ref, near_ref, full_ref, packed):
    par = par_ref[0]
    packed[1:9] = own_ref[...]
    packed[pl.ds(9 * par, 1)] = near_ref[...]
    packed[pl.ds(9 * (1 - par), 1)] = edge_ref[...]
    unpack_rows(packed, full_ref)


def unpack_own(par, own, edge, near):
    vmem = pl.BlockSpec(memory_space=pltpu.VMEM)
    return pl.pallas_call(
        unpack_own_kernel,
        out_shape=jax.ShapeDtypeStruct((2, 10, 64, 128), BF),
        in_specs=[pl.BlockSpec(memory_space=pltpu.SMEM)] + [vmem] * 3,
        out_specs=vmem,
        scratch_shapes=[pltpu.VMEM((10, 96, 128), BF)],
        compiler_params=params(),
        cost_estimate=pl.CostEstimate(flops=10**9, bytes_accessed=10**6, transcendentals=0),
    )(par, own, edge, near)


def unpack_far_kernel(after_ref, packed_ref, own_ref, far_ref, low_ref, high_ref):
    del after_ref
    unpack_rows(packed_ref, far_ref)
    low_ref[:, 0:10] = own_ref[:, :, 0:16, :]
    low_ref[:, 10:18] = far_ref[:, :, 0:16, :]
    high_ref[:, 0:10] = own_ref[:, :, 48:64, :]
    high_ref[:, 10:18] = far_ref[:, :, 48:64, :]


def unpack_far(after, packed, own):
    vmem = pl.BlockSpec(memory_space=pltpu.VMEM)
    return pl.pallas_call(
        unpack_far_kernel,
        out_shape=(
            jax.ShapeDtypeStruct((2, 8, 64, 128), BF),
            jax.ShapeDtypeStruct((2, 18, 16, 128), BF),
            jax.ShapeDtypeStruct((2, 18, 16, 128), BF),
        ),
        in_specs=[pl.BlockSpec(memory_space=pl.ANY)] + [vmem] * 2,
        out_specs=(vmem,) * 3,
        compiler_params=params(),
        cost_estimate=pl.CostEstimate(flops=10**9, bytes_accessed=10**6, transcendentals=0),
    )(after, packed, own)


def pipelined(stages, groups):
    for step in range(len(groups) + len(stages) - 1):
        for k in range(len(stages)):
            if 0 <= step - k < len(groups):
                stages[k](groups[step - k])


def normalize(x, gain):
    mean = jnp.mean(x, axis=-1, keepdims=True)
    x = x - mean
    var = jnp.mean(x * x, axis=-1, keepdims=True)
    return x * lax.rsqrt(var + 1e-05) * gain


def attend(q, k, v, bias):
    left = iota((128, 128), 1) < HEAD_DIM
    ones_left, ones_right = one_hot(left), one_hot(~left)
    zero = jnp.zeros((128, 128), BF)
    out = []
    for pair in range(4):
        at = slice(pair * 128, pair * 128 + 128)
        kp, vp = k[:, at], v[:, at]
        keys = jnp.concatenate([jnp.where(left, kp, zero), jnp.where(left, zero, kp)], axis=0)
        s = mm_t(q[:, at], keys)
        if bias is not None:
            s = s + bias
        s0, s1 = s[:, :128], s[:, 128:]
        p0 = jnp.exp2(s0 - jnp.max(s0, axis=-1, keepdims=True))
        p1 = jnp.exp2(s1 - jnp.max(s1, axis=-1, keepdims=True))
        p = jnp.concatenate([p0, p1], axis=1).astype(BF)
        vals = jnp.concatenate(
            [
                jnp.concatenate([jnp.where(left, vp, zero), ones_left], axis=1),
                jnp.concatenate([jnp.where(left, zero, vp), ones_right], axis=1),
            ],
            axis=0,
        )
        o = mm(p, vals)
        out.append((o[:, :128] / o[:, 128:]).astype(BF))
    return jnp.concatenate(out, axis=1)


MIDDLE, EDGES = (1, 2, 3), (0, 4)


def first_kernel(parts, which, after_ref, *refs):
    del after_ref
    par_ref, own_ref, refs = refs[0], refs[1], refs[2:]
    if 1 in parts:
        far_ref, refs = refs[0], refs[1:]
    if which == EDGES:
        low_ref, high_ref, refs = refs[0], refs[1], refs[2:]
    wemb_ref, lev_ref, gain_ref, wq_ref, wkv_ref, wo_ref, *refs = refs
    x1_refs, refs = refs[: len(parts)], refs[len(parts) :]
    if 0 in parts:
        send_ref, refs = refs[0], refs[1:]
    wide, gathered, x0, normed, query, keyval, heads = refs
    par = par_ref[0]

    def spread(part, to, count, center, low, high):
        rows = (slice(None), pl.ds(to, count))
        if which == EDGES:
            wide[part, *rows, 0:16, :] = low.astype(F32)
            wide[part, *rows, 16:32, :] = center[:, :, 0:16, :].astype(F32)
            wide[part, *rows, 64:80, :] = center[:, :, 48:64, :].astype(F32)
            wide[part, *rows, 80:96, :] = high.astype(F32)
        else:
            wide[part, *rows, 16:80, :] = center.astype(F32)

    sides = [r for r in ((low_ref, high_ref) if which == EDGES else ())]
    if 0 in parts:
        spread(0, 0, 10, own_ref[...], *([r[:, 0:10] for r in sides] or (None, None)))
    if 1 in parts:
        spread(1, 2 * par, 8, far_ref[...], *([r[:, 10:18] for r in sides] or (None, None)))
        beside = pl.ds(8 * par, 2)
        spread(1, 8 * (1 - par), 2, own_ref[:, beside], *([r[:, beside] for r in sides] or (None, None)))
    gain = gain_ref[0:1, :]
    half = 1 - par

    def embed(group):
        part, g = group
        slot = groups.index(group)
        for dj in range(3):
            cols = slice(g * 16 + 7 + dj, g * 16 + 23 + dj)
            got = wide[part, :, :, cols, :].astype(BF)
            gathered[slot, :, :, :, dj * 128 : dj * 128 + 128] = got
        for level in range(2):
            lhs = jnp.concatenate(
                [gathered[slot, level, di : di + 8].reshape(128, 384) for di in range(3)], axis=1
            )
            x = mm(lhs, wemb_ref[...]) + lev_ref[level : level + 1, :]
            x0[slot, level] = x.reshape(8, 16, D)

    def norm(group):
        slot = groups.index(group)
        for u in range(2):
            x = x0[slot, :, :, u * 8 : u * 8 + 8, :].reshape(128, D)
            normed[slot, u] = normalize(x, gain).astype(BF).reshape(2, 4, 16, D)

    def project(group):
        slot = groups.index(group)
        n = normed[slot].reshape(256, D)
        keyval[slot] = mm(n, wkv_ref[0]).astype(BF).reshape(2, 128, 1024)
        if group[0]:
            n = normed[slot, :, :, pl.ds(half * 2, 2)].reshape(128, D)
        q = (mm(n, wq_ref[0]) * SCALE).astype(BF)
        query[slot, :, : q.shape[0] // 2] = q.reshape(2, -1, D)

    def attention(group):
        slot = groups.index(group)
        count = 64 if group[0] else 128
        for u in range(2):
            kv = keyval[slot, u]
            heads[slot, u, :count] = attend(query[slot, u, :count], kv[:, :D], kv[:, D:], None)

    def project_out(group):
        part, g = group
        slot = groups.index(group)
        count = 64 if part else 128
        out = mm(heads[slot, :, :count].reshape(2 * count, D), wo_ref[0])
        for u in range(2):
            at = which.index(g) * 16 + u * 8
            cols = slice(at, at + 8)
            mine = slice(u * 8, u * 8 + 8)
            add = out[u * count : u * count + count].reshape(2, count // 16, 8, D)
            if part:
                x1_refs[-1][:, :, cols, :] = x0[slot, :, pl.ds(4 * half, 4), mine, :] + add
            else:
                for h in range(2):
                    to = pl.ds(4 * (par if h == 0 else half), 4)
                    rows = slice(4 * h, 4 * h + 4)
                    x1_refs[0][:, to, cols, :] = x0[slot, :, rows, mine, :] + add[:, rows]

    groups = [(part, g) for part in parts for g in which]
    pipelined([embed, norm, project, attention, project_out], groups)
    if 0 in parts:
        send_ref[...] = x1_refs[0][:, 4:8].astype(BF)


def first_block(parts, which, after, par, patch_arrays, wemb, level_embed, norm_gain, w_query, w_keyval, w_out):
    vmem = pl.BlockSpec(memory_space=pltpu.VMEM)
    width, count = 16 * len(which), len(parts) * len(which)
    outs = [jax.ShapeDtypeStruct((2, 4 if part else 8, width, D), F32) for part in parts]
    if 0 in parts:
        outs.append(jax.ShapeDtypeStruct((2, 4, width, D), BF))
    return pl.pallas_call(
        functools.partial(first_kernel, parts, which),
        out_shape=tuple(outs),
        in_specs=[pl.BlockSpec(memory_space=pl.ANY), pl.BlockSpec(memory_space=pltpu.SMEM)]
        + [vmem] * (6 + len(patch_arrays)),
        out_specs=(vmem,) * len(outs),
        scratch_shapes=[
            pltpu.VMEM((2, 2, 10, 96, 128), F32),
            pltpu.VMEM((count, 2, 10, 16, 384), BF),
            pltpu.VMEM((count, 2, 8, 16, D), F32),
            pltpu.VMEM((count, 2, 2, 4, 16, D), BF),
            pltpu.VMEM((count, 2, 128, D), BF),
            pltpu.VMEM((count, 2, 128, 1024), BF),
            pltpu.VMEM((count, 2, 128, D), BF),
        ],
        compiler_params=params(),
        cost_estimate=pl.CostEstimate(flops=10**10, bytes_accessed=10**7, transcendentals=0),
    )(after, par, *patch_arrays, wemb, level_embed, norm_gain, w_query, w_keyval, w_out)


SHIFTED = WINS - 1


def second_kernel(
    par_ref, own_mid, outer_mid, own_edge, outer_edge, near_mid_ref, near_edge_ref, gain_ref, mgain_ref,
    wq_ref, wkv_ref, wo_ref, wm_ref,
    out_ref,
    near, x2, normed, query, keyval, heads,
):
    par, pole = par_ref[0], par_ref[1]
    near[:, :, 0:16, :] = near_edge_ref[:, :, 0:16, :].astype(F32)
    near[:, :, 16:64, :] = near_mid_ref[...].astype(F32)
    near[:, :, 64:80, :] = near_edge_ref[:, :, 16:32, :].astype(F32)
    gain = gain_ref[1:2, :]
    upper = iota((8, D), 0) >= 4
    key_row = (iota((1, 256), 1) // 8) % 8
    bias = jnp.where(key_row < 4, F32(-1e30), F32(0)) * pole.astype(F32)

    def block(n, first, last):
        if first < 4 < last:
            return jnp.concatenate([block(n, first, 4), block(n, 4, last)], axis=1)
        if first >= 12:
            return near[:, first - 12 : last - 12, n * 8 : n * 8 + 8, :]
        middle = 2 <= n < 8
        at = n * 8 - (16 if middle else 48 if n >= 8 else 0)
        if first < 4:
            return (outer_mid if middle else outer_edge)[:, first:last, at : at + 8, :]
        return (own_mid if middle else own_edge)[:, first - 4 : last - 4, at : at + 8, :]

    def window(w, first, last):
        return jnp.where(upper, block(w, first, last), block(w + 1, first, last))

    def norm(group):
        s, g = group
        for w in range(g * 3, g * 3 + 3):
            if s == 0:
                x = window(w, 0, 8)
            else:
                x = jnp.concatenate(
                    [window(w, 8, 12), window(w, 12, 16)], axis=1
                )
            n = normalize(x.reshape(128, D), gain).astype(BF)
            normed[s * SHIFTED + w] = n.reshape(2, 4, 16, D)

    def project(group):
        s, g = group
        at = slice(s * SHIFTED + g * 3, s * SHIFTED + g * 3 + 3)
        n = normed[at].reshape(384, D)
        keyval[at] = mm(n, wkv_ref[1]).astype(BF).reshape(3, 128, 1024)
        n = normed[at, :, 2 - 2 * s : 4 - 2 * s].reshape(192, D)
        query[at] = (mm(n, wq_ref[1]) * SCALE).astype(BF).reshape(3, 64, D)

    def attention(group):
        s, g = group
        for t in range(s * SHIFTED + g * 3, s * SHIFTED + g * 3 + 3):
            kv = keyval[t]
            heads[t] = attend(query[t], kv[:, :D], kv[:, D:], None if s else bias)

    def project_out(group):
        s, g = group
        at = slice(s * SHIFTED + g * 3, s * SHIFTED + g * 3 + 3)
        out = mm(heads[at].reshape(192, D), wo_ref[1])
        rows = slice(s * 4, s * 4 + 4)
        for u in range(3):
            w = g * 3 + u
            new = window(w, 4 + s * 4, 8 + s * 4)
            new = new + out[u * 64 : u * 64 + 64].reshape(2, 4, 8, D)
            for c in range(4):
                piece = new[..., c * 128 : c * 128 + 128]
                x2[c, :, rows, w * 8 + 4 : w * 8 + 8, :] = piece[:, :, 4:8, :]
                x2[c, :, rows, w * 8 + 8 : w * 8 + 12, :] = piece[:, :, 0:4, :]

    def merge(group):
        s, g = group
        if g < 2:
            return
        parts = []
        for p in range(4):
            got = [
                jnp.concatenate(
                    [
                        x2[c, level, s * 4 + 2 * a + p % 2, pl.ds(8 + p // 2, 32, stride=2), :]
                        for c in range(4)
                    ],
                    axis=1,
                )
                for level in range(2)
                for a in range(2)
            ]
            parts.append(jnp.concatenate(got, axis=0))
        n = normalize(jnp.concatenate(parts, axis=1), mgain_ref[...]).astype(BF)
        out = mm(n, wm_ref[...]).astype(BF)
        out_ref[:, pl.ds(2 * ((par + s) % 2), 2)] = out.reshape(2, 2, 32, 1024)

    groups = [(s, g) for s in range(2) for g in range(3)]
    pipelined([norm, project, attention, project_out, merge], groups)


def second_block(par, x1_parts, near_mid, near_edge, norm_gain, merge_gain, w_query, w_keyval, w_out, merge_weight):
    vmem = pl.BlockSpec(memory_space=pltpu.VMEM)
    return pl.pallas_call(
        second_kernel,
        out_shape=jax.ShapeDtypeStruct((2, 4, 32, 1024), BF),
        in_specs=[pl.BlockSpec(memory_space=pltpu.SMEM)] + [vmem] * 12,
        out_specs=vmem,
        scratch_shapes=[
            pltpu.VMEM((2, 4, 80, D), F32),
            pltpu.VMEM((4, 2, 8, 80, 128), F32),
            pltpu.VMEM((2 * SHIFTED, 2, 4, 16, D), BF),
            pltpu.VMEM((2 * SHIFTED, 64, D), BF),
            pltpu.VMEM((2 * SHIFTED, 128, 1024), BF),
            pltpu.VMEM((2 * SHIFTED, 64, D), BF),
        ],
        compiler_params=params(),
        cost_estimate=pl.CostEstimate(flops=10**10, bytes_accessed=10**7, transcendentals=0),
    )(
        par, *x1_parts, near_mid, near_edge, norm_gain, merge_gain, w_query, w_keyval, w_out, merge_weight
    )


def embedding_matrix(embed_weight, land_embed):
    w = jnp.pad(embed_weight, ((0, 0), (0, 0), (0, 2), (0, 0))).reshape(3, 4, 3, 4, 8, D)
    w = w.transpose(0, 2, 1, 3, 4, 5)
    share = land_embed / 16
    high = lax.reduce_precision(share, 8, 7)
    at = [lax.broadcasted_iota(jnp.int32, w.shape, d) for d in (0, 1, 4)]
    middle = (at[0] == 1) & (at[1] == 1)
    w = jnp.where(middle & (at[2] == 6), high.astype(BF), w)
    w = jnp.where(middle & (at[2] == 7), (share - high).astype(BF), w)
    return w.reshape(9 * 128, D)


def swap(block, first):
    count = lax.axis_size("lat")
    pairs = []
    for i in range(first, count - 1, 2):
        pairs += [(i, i + 1), (i + 1, i)]
    return lax.ppermute(block, "lat", pairs)


def around(block, distance):
    count = lax.axis_size("lon")
    return lax.ppermute(block, "lon", [(i, (i + distance) % count) for i in range(count)])


def shards(
    atmos, orography, land_sea, embed_weight, level_embed, land_embed, norm_gain,
    w_query, w_keyval, w_out, merge_gain, merge_weight,
):
    w_query, w_keyval, w_out, merge_weight = [
        pltpu.with_memory_space_constraint(w, pltpu.VMEM) for w in (w_query, w_keyval, w_out, merge_weight)
    ]
    lat = lax.axis_index("lat")
    par = lat % 2
    pole = (lat == 0) | (lat == lax.axis_size("lat") - 1)
    place = jnp.stack([par, pole]).astype(jnp.int32)
    own, send, edge, near = patches(place, atmos, orography, land_sea)
    edge = swap(edge, 0)
    near = swap(near, 1)
    send = lax.dynamic_update_slice(send, edge, (7 * (1 - par), 0, 0))
    far = swap(send, 1)
    wemb = embedding_matrix(embed_weight, land_embed)
    weights = wemb, level_embed, norm_gain, w_query, w_keyval, w_out
    own = unpack_own(place, own, edge, near)
    own_mid, send_mid = first_block((0,), MIDDLE, edge, place, (own,), *weights)
    near_mid = swap(send_mid, 0)
    far, low, high = unpack_far(own_mid, far, own)
    from_low, from_high = around(high, 1), around(low, -1)
    (outer_mid,) = first_block((1,), MIDDLE, own_mid, place, (own, far), *weights)
    own_edge, outer_edge, send_edge = first_block(
        (0, 1), EDGES, outer_mid, place, (own, far, from_low, from_high), *weights
    )
    near_edge = swap(send_edge, 0)
    return second_block(
        place, (own_mid, outer_mid, own_edge, outer_edge), near_mid, near_edge, norm_gain,
        merge_gain.reshape(1, -1), w_query, w_keyval, w_out, merge_weight,
    )


def solution(mesh):
    in_specs = (P(None, None, "lat", "lon"), P("lat", "lon"), P("lat", "lon")) + (P(),) * 9
    out_specs = P(None, "lat", "lon", None)
    return jax.shard_map(shards, mesh=mesh, in_specs=in_specs, out_specs=out_specs, check_vma=False)
```

```python
import functools
import math

import jax
import jax.numpy as jnp
from jax import lax
from jax.experimental import pallas as pl
from jax.experimental.pallas import tpu as pltpu
from jax.sharding import PartitionSpec as P

BF = jnp.bfloat16
F32 = jnp.float32
D = 512
HEAD_DIM = 64
WINS = 10
SCALE = HEAD_DIM ** (-0.5) * math.log2(math.e)
VMEM_LIMIT = 32 * 1024 * 1024


def iota(shape, dim):
    return lax.broadcasted_iota(jnp.int32, shape, dim)


def one_hot(cond):
    return jnp.where(cond, 1.0, 0.0).astype(BF)


def mm(a, b):
    return jnp.dot(a, b, preferred_element_type=F32)


def mm_t(a, b):
    return lax.dot_general(a, b, (((1,), (1,)), ((), ())), preferred_element_type=F32)


def params():
    return pltpu.CompilerParams(vmem_limit_bytes=VMEM_LIMIT)


def patch_kernel(
    par_ref, atmos_any, oro_any, land_any, own_ref, send_ref, edge_ref, near_ref,
    atmos_ref, oro_ref, land_ref, sems,
):
    par = par_ref[0]
    loads = [
        pltpu.make_async_copy(src, dst, sems.at[n])
        for n, (src, dst) in enumerate(
            [(atmos_any, atmos_ref), (oro_any, oro_ref), (land_any, land_ref)]
        )
    ]
    for load in loads:
        load.start()
    row, src = iota((1024, 384), 0), iota((1024, 384), 1)
    i, r, ch = row // 128, (row % 128) // 32, row % 8
    channel = jnp.where(ch < 5, ch, jnp.where(ch == 5, 10, jnp.where(ch == 6, 11, 9)))
    pick_main = one_hot(src == channel * 32 + i * 4 + r)
    pick_aux = one_hot(src == (5 + row % 4) * 32 + i * 4 + r)
    for load in loads:
        load.wait()
    cells = jnp.concatenate(
        [
            atmos_ref[...].reshape(320, 256),
            oro_ref[...],
            land_ref[...].astype(F32).astype(BF),
        ],
        axis=0,
    )
    main, aux = mm(pick_main, cells), mm(pick_aux, cells)
    row, col = iota((1024, 256), 0), iota((1024, 256), 1)
    c, half = (row % 32) // 8, (row % 8) // 4
    main = jnp.where(col % 4 == c, main, 0.0).astype(BF)
    aux = jnp.where((col % 4 == c) & (col // 128 == half), aux, 0.0).astype(BF)
    j, col = iota((64, 256), 0), iota((64, 256), 1)
    main = mm_t(one_hot(col // 4 == j), main).astype(BF)
    j, col = iota((32, 256), 0), iota((32, 256), 1)
    aux = mm_t(one_hot((col % 128) // 4 == j), aux).astype(BF)
    for i in range(8):
        own_ref[i, 0:64, :] = main[:, i * 128 : i * 128 + 128]
        own_ref[i, 64:96, :] = aux[:, i * 128 : i * 128 + 128]
    send_ref[pl.ds(par, 7)] = own_ref[pl.ds(1 - par, 7)]
    edge_ref[...] = own_ref[pl.ds(7 * (1 - par), 1)]
    near_ref[...] = own_ref[pl.ds(7 * par, 1)]


def patches(par, atmos, orography, land_sea):
    cells = [pltpu.with_memory_space_constraint(a, pltpu.HBM) for a in (atmos, orography, land_sea)]
    return pl.pallas_call(
        patch_kernel,
        out_shape=tuple(jax.ShapeDtypeStruct((n, 96, 128), BF) for n in (8, 8, 1, 1)),
        in_specs=[pl.BlockSpec(memory_space=pltpu.SMEM)] + [pl.BlockSpec(memory_space=pltpu.HBM)] * 3,
        out_specs=(pl.BlockSpec(memory_space=pltpu.VMEM),) * 4,
        scratch_shapes=[
            pltpu.VMEM(atmos.shape, BF),
            pltpu.VMEM(orography.shape, BF),
            pltpu.VMEM(land_sea.shape, jnp.int32),
            pltpu.SemaphoreType.DMA((3,)),
        ],
        compiler_params=params(),
        cost_estimate=pl.CostEstimate(flops=10**9, bytes_accessed=10**6, transcendentals=0),
    )(par, *cells)


def unpack_rows(packed, out_ref):
    rows = packed.shape[0]
    k, n = iota((256, 256), 0), iota((256, 256), 1)
    ch, lane = n % 8, n % 128
    from_main0 = jnp.where(ch == 7, lane - 1, lane)
    from_main1 = jnp.where(ch == 7, lane - 1, jnp.where(ch == 4, lane + 3, lane))
    aux = packed[:, 64:96, :]
    for half in range(2):
        from_one = jnp.where(ch < 4, 128 + lane + 4 * half, from_main1)
        pick = one_hot(k == jnp.where(n < 128, from_main0, from_one))
        both = jnp.concatenate([packed[:, half * 32 : half * 32 + 32, :], aux], axis=2)
        got = mm(both.reshape(rows * 32, 256), pick).astype(BF).reshape(rows, 32, 256)
        for level in range(2):
            tile = got[:, :, level * 128 : level * 128 + 128]
            out_ref[level, :, half * 32 : half * 32 + 32, :] = tile


def unpack_far_kernel(after_ref, packed_ref, own_ref, far_ref, low_ref, high_ref):
    del after_ref
    unpack_rows(packed_ref, far_ref)
    low_ref[:, 0:10] = own_ref[:, :, 0:16, :]
    low_ref[:, 10:18] = far_ref[:, :, 0:16, :]
    high_ref[:, 0:10] = own_ref[:, :, 48:64, :]
    high_ref[:, 10:18] = far_ref[:, :, 48:64, :]


def unpack_far(after, packed, own):
    vmem = pl.BlockSpec(memory_space=pltpu.VMEM)
    return pl.pallas_call(
        unpack_far_kernel,
        out_shape=(
            jax.ShapeDtypeStruct((2, 8, 64, 128), BF),
            jax.ShapeDtypeStruct((2, 18, 16, 128), BF),
            jax.ShapeDtypeStruct((2, 18, 16, 128), BF),
        ),
        in_specs=[pl.BlockSpec(memory_space=pl.ANY)] + [vmem] * 2,
        out_specs=(vmem,) * 3,
        compiler_params=params(),
        cost_estimate=pl.CostEstimate(flops=10**9, bytes_accessed=10**6, transcendentals=0),
    )(after, packed, own)


def pipelined(stages, groups):
    for step in range(len(groups) + len(stages) - 1):
        for k in range(len(stages)):
            if 0 <= step - k < len(groups):
                stages[k](groups[step - k])


def normalize(x, gain):
    mean = jnp.mean(x, axis=-1, keepdims=True)
    x = x - mean
    var = jnp.mean(x * x, axis=-1, keepdims=True)
    return x * lax.rsqrt(var + 1e-05) * gain


def attend(q, k, v, bias):
    left = iota((128, 128), 1) < HEAD_DIM
    ones_left, ones_right = one_hot(left), one_hot(~left)
    zero = jnp.zeros((128, 128), BF)
    out = []
    for pair in range(4):
        at = slice(pair * 128, pair * 128 + 128)
        kp, vp = k[:, at], v[:, at]
        keys = jnp.concatenate([jnp.where(left, kp, zero), jnp.where(left, zero, kp)], axis=0)
        s = mm_t(q[:, at], keys)
        if bias is not None:
            s = s + bias
        s0, s1 = s[:, :128], s[:, 128:]
        p0 = jnp.exp2(s0 - jnp.max(s0, axis=-1, keepdims=True))
        p1 = jnp.exp2(s1 - jnp.max(s1, axis=-1, keepdims=True))
        p = jnp.concatenate([p0, p1], axis=1).astype(BF)
        vals = jnp.concatenate(
            [
                jnp.concatenate([jnp.where(left, vp, zero), ones_left], axis=1),
                jnp.concatenate([jnp.where(left, zero, vp), ones_right], axis=1),
            ],
            axis=0,
        )
        o = mm(p, vals)
        out.append((o[:, :128] / o[:, 128:]).astype(BF))
    return jnp.concatenate(out, axis=1)


MIDDLE, EDGES = (1, 2, 3), (0, 4)


def first_kernel(parts, which, after_ref, *refs):
    del after_ref
    par_ref, refs = refs[0], refs[1:]
    leading = parts == (0,) and which == MIDDLE
    if leading:
        own_packed, edge_ref, near_ref, refs = refs[0], refs[1], refs[2], refs[3:]
    else:
        own_ref, refs = refs[0], refs[1:]
    if 1 in parts:
        far_ref, refs = refs[0], refs[1:]
    if which == EDGES:
        low_ref, high_ref, refs = refs[0], refs[1], refs[2:]
    wemb_ref, lev_ref, gain_ref, wq_ref, wkv_ref, wo_ref, *refs = refs
    x1_refs, refs = refs[: len(parts)], refs[len(parts) :]
    if 0 in parts:
        send_ref, refs = refs[0], refs[1:]
    if leading:
        own_ref, refs = refs[0], refs[1:]
    wide, gathered, x0, normed, query, keyval, heads, *refs = refs
    par = par_ref[0]
    if leading:
        packed, wq, wkv, wo, sems = refs
        loads = [
            pltpu.make_async_copy(src.at[0], dst, sems.at[n])
            for n, (src, dst) in enumerate([(wkv_ref, wkv), (wq_ref, wq), (wo_ref, wo)])
        ]
        for load in loads:
            load.start()
        packed[1:9] = own_packed[...]
        packed[pl.ds(9 * par, 1)] = near_ref[...]
        packed[pl.ds(9 * (1 - par), 1)] = edge_ref[...]
        unpack_rows(packed, own_ref)
    else:
        wq, wkv, wo = wq_ref.at[0], wkv_ref.at[0], wo_ref.at[0]

    def spread(part, to, count, center, low, high):
        rows = (slice(None), pl.ds(to, count))
        if which == EDGES:
            wide[part, *rows, 0:16, :] = low.astype(F32)
            wide[part, *rows, 16:32, :] = center[:, :, 0:16, :].astype(F32)
            wide[part, *rows, 64:80, :] = center[:, :, 48:64, :].astype(F32)
            wide[part, *rows, 80:96, :] = high.astype(F32)
        else:
            wide[part, *rows, 16:80, :] = center.astype(F32)

    sides = [r for r in ((low_ref, high_ref) if which == EDGES else ())]
    if 0 in parts:
        spread(0, 0, 10, own_ref[...], *([r[:, 0:10] for r in sides] or (None, None)))
    if 1 in parts:
        spread(1, 2 * par, 8, far_ref[...], *([r[:, 10:18] for r in sides] or (None, None)))
        beside = pl.ds(8 * par, 2)
        spread(1, 8 * (1 - par), 2, own_ref[:, beside], *([r[:, beside] for r in sides] or (None, None)))
    gain = gain_ref[0:1, :]
    half = 1 - par

    cols_of = len(which)

    def slots(part):
        at = parts.index(part) * cols_of
        return at, slice(at, at + cols_of)

    def embed(part):
        first, here = slots(part)
        for n, g in enumerate(which):
            for dj in range(3):
                cols = slice(g * 16 + 7 + dj, g * 16 + 23 + dj)
                got = wide[part, :, :, cols, :].astype(BF)
                gathered[first + n, :, :, :, dj * 128 : dj * 128 + 128] = got
        for n in range(cols_of):
            lhs = jnp.concatenate(
                [gathered[first + n, :, di : di + 8].reshape(256, 384) for di in range(3)], axis=1
            )
            x = mm(lhs, wemb_ref[...]).reshape(2, 8, 16, D)
            for level in range(2):
                x0[first + n, level] = x[level] + lev_ref[level : level + 1, :]

    def norm(part):
        first, here = slots(part)
        for slot in range(first, first + cols_of):
            for u in range(2):
                x = x0[slot, :, :, u * 8 : u * 8 + 8, :].reshape(128, D)
                normed[slot, u] = normalize(x, gain).astype(BF).reshape(2, 4, 16, D)

    def project(part):
        first, here = slots(part)
        n = normed[here].reshape(256 * cols_of, D)
        if leading:
            loads[0].wait()
            loads[1].wait()
        keyval[here] = mm(n, wkv[...]).astype(BF).reshape(cols_of, 2, 128, 1024)
        if part:
            n = normed[here, :, :, pl.ds(half * 2, 2)].reshape(128 * cols_of, D)
        q = (mm(n, wq[...]) * SCALE).astype(BF)
        query[here, :, : 64 if part else 128] = q.reshape(cols_of, 2, -1, D)

    def attention(part):
        first, here = slots(part)
        count = 64 if part else 128
        for slot in range(first, first + cols_of):
            for u in range(2):
                kv = keyval[slot, u]
                heads[slot, u, :count] = attend(query[slot, u, :count], kv[:, :D], kv[:, D:], None)

    def project_out(part):
        first, here = slots(part)
        count = 64 if part else 128
        if leading:
            loads[2].wait()
        out = mm(heads[here, :, :count].reshape(2 * cols_of * count, D), wo[...])
        for n in range(2 * cols_of):
            slot, u = first + n // 2, n % 2
            cols, mine = slice(n * 8, n * 8 + 8), slice(u * 8, u * 8 + 8)
            add = out[n * count : n * count + count].reshape(2, count // 16, 8, D)
            if part:
                x1_refs[-1][:, :, cols, :] = x0[slot, :, pl.ds(4 * half, 4), mine, :] + add
            else:
                for h in range(2):
                    to = pl.ds(4 * (par if h == 0 else half), 4)
                    rows = slice(4 * h, 4 * h + 4)
                    x1_refs[0][:, to, cols, :] = x0[slot, :, rows, mine, :] + add[:, rows]

    pipelined([embed, norm, project, attention, project_out], list(parts))
    if 0 in parts:
        send_ref[...] = x1_refs[0][:, 4:8].astype(BF)


def first_block(parts, which, after, par, patch_arrays, wemb, level_embed, norm_gain, w_query, w_keyval, w_out):
    vmem = pl.BlockSpec(memory_space=pltpu.VMEM)
    width, count = 16 * len(which), len(parts) * len(which)
    leading = parts == (0,) and which == MIDDLE
    outs = [jax.ShapeDtypeStruct((2, 4 if part else 8, width, D), F32) for part in parts]
    if 0 in parts:
        outs.append(jax.ShapeDtypeStruct((2, 4, width, D), BF))
    scratch = [
        pltpu.VMEM((2, 2, 10, 96, 128), F32),
        pltpu.VMEM((count, 2, 10, 16, 384), BF),
        pltpu.VMEM((count, 2, 8, 16, D), F32),
        pltpu.VMEM((count, 2, 2, 4, 16, D), BF),
        pltpu.VMEM((count, 2, 128, D), BF),
        pltpu.VMEM((count, 2, 128, 1024), BF),
        pltpu.VMEM((count, 2, 128, D), BF),
    ]
    projections = [w_query, w_keyval, w_out]
    if leading:
        outs.append(jax.ShapeDtypeStruct((2, 10, 64, 128), BF))
        scratch += [
            pltpu.VMEM((10, 96, 128), BF),
            pltpu.VMEM((D, D), BF),
            pltpu.VMEM((D, 1024), BF),
            pltpu.VMEM((D, D), BF),
            pltpu.SemaphoreType.DMA((3,)),
        ]
        projections = [pltpu.with_memory_space_constraint(w, pltpu.HBM) for w in projections]
    else:
        projections = [pltpu.with_memory_space_constraint(w, pltpu.VMEM) for w in projections]
    place_of = pl.BlockSpec(memory_space=pltpu.HBM if leading else pltpu.VMEM)
    return pl.pallas_call(
        functools.partial(first_kernel, parts, which),
        out_shape=tuple(outs),
        in_specs=[pl.BlockSpec(memory_space=pl.ANY), pl.BlockSpec(memory_space=pltpu.SMEM)]
        + [vmem] * (3 + len(patch_arrays)) + [place_of] * 3,
        out_specs=(vmem,) * len(outs),
        scratch_shapes=scratch,
        compiler_params=params(),
        cost_estimate=pl.CostEstimate(flops=10**10, bytes_accessed=10**7, transcendentals=0),
    )(after, par, *patch_arrays, wemb, level_embed, norm_gain, *projections)


SHIFTED = WINS - 1


def second_kernel(
    par_ref, own_mid, outer_mid, own_edge, outer_edge, near_mid_ref, near_edge_ref, gain_ref, mgain_ref,
    wq_ref, wkv_ref, wo_ref, wm_ref,
    out_ref,
    near, x2, normed, query, keyval, heads,
):
    par, pole = par_ref[0], par_ref[1]
    near[:, :, 0:16, :] = near_edge_ref[:, :, 0:16, :].astype(F32)
    near[:, :, 16:64, :] = near_mid_ref[...].astype(F32)
    near[:, :, 64:80, :] = near_edge_ref[:, :, 16:32, :].astype(F32)
    gain = gain_ref[1:2, :]
    upper = iota((8, D), 0) >= 4
    key_row = (iota((1, 256), 1) // 8) % 8
    bias = jnp.where(key_row < 4, F32(-1e30), F32(0)) * pole.astype(F32)

    def block(n, first, last):
        if first < 4 < last:
            return jnp.concatenate([block(n, first, 4), block(n, 4, last)], axis=1)
        if first >= 12:
            return near[:, first - 12 : last - 12, n * 8 : n * 8 + 8, :]
        middle = 2 <= n < 8
        at = n * 8 - (16 if middle else 48 if n >= 8 else 0)
        if first < 4:
            return (outer_mid if middle else outer_edge)[:, first:last, at : at + 8, :]
        return (own_mid if middle else own_edge)[:, first - 4 : last - 4, at : at + 8, :]

    def window(w, first, last):
        return jnp.where(upper, block(w, first, last), block(w + 1, first, last))

    def norm(s):
        for w in range(SHIFTED):
            if s == 0:
                x = window(w, 0, 8)
            else:
                x = jnp.concatenate(
                    [window(w, 8, 12), window(w, 12, 16)], axis=1
                )
            n = normalize(x.reshape(128, D), gain).astype(BF)
            normed[s * SHIFTED + w] = n.reshape(2, 4, 16, D)

    def project(s):
        at = slice(s * SHIFTED, s * SHIFTED + SHIFTED)
        n = normed[at].reshape(SHIFTED * 128, D)
        keyval[at] = mm(n, wkv_ref[1]).astype(BF).reshape(SHIFTED, 128, 1024)
        n = normed[at, :, 2 - 2 * s : 4 - 2 * s].reshape(SHIFTED * 64, D)
        query[at] = (mm(n, wq_ref[1]) * SCALE).astype(BF).reshape(SHIFTED, 64, D)

    def attention(s):
        for t in range(s * SHIFTED, s * SHIFTED + SHIFTED):
            kv = keyval[t]
            heads[t] = attend(query[t], kv[:, :D], kv[:, D:], None if s else bias)

    def project_out(s):
        at = slice(s * SHIFTED, s * SHIFTED + SHIFTED)
        out = mm(heads[at].reshape(SHIFTED * 64, D), wo_ref[1])
        rows = slice(s * 4, s * 4 + 4)
        for w in range(SHIFTED):
            new = window(w, 4 + s * 4, 8 + s * 4)
            new = new + out[w * 64 : w * 64 + 64].reshape(2, 4, 8, D)
            for c in range(4):
                piece = new[..., c * 128 : c * 128 + 128]
                x2[c, :, rows, w * 8 + 4 : w * 8 + 8, :] = piece[:, :, 4:8, :]
                x2[c, :, rows, w * 8 + 8 : w * 8 + 12, :] = piece[:, :, 0:4, :]

    def merge(s):
        parts = []
        for p in range(4):
            got = [
                jnp.concatenate(
                    [
                        x2[c, level, s * 4 + 2 * a + p % 2, pl.ds(8 + p // 2, 32, stride=2), :]
                        for c in range(4)
                    ],
                    axis=1,
                )
                for level in range(2)
                for a in range(2)
            ]
            parts.append(jnp.concatenate(got, axis=0))
        n = normalize(jnp.concatenate(parts, axis=1), mgain_ref[...]).astype(BF)
        out = mm(n, wm_ref[...]).astype(BF)
        out_ref[:, pl.ds(2 * ((par + s) % 2), 2)] = out.reshape(2, 2, 32, 1024)

    pipelined([norm, project, attention, project_out, merge], [0, 1])


def second_block(par, x1_parts, near_mid, near_edge, norm_gain, merge_gain, w_query, w_keyval, w_out, merge_weight):
    vmem = pl.BlockSpec(memory_space=pltpu.VMEM)
    weights = [
        pltpu.with_memory_space_constraint(w, pltpu.VMEM) for w in (w_query, w_keyval, w_out, merge_weight)
    ]
    return pl.pallas_call(
        second_kernel,
        out_shape=jax.ShapeDtypeStruct((2, 4, 32, 1024), BF),
        in_specs=[pl.BlockSpec(memory_space=pltpu.SMEM)] + [vmem] * 12,
        out_specs=vmem,
        scratch_shapes=[
            pltpu.VMEM((2, 4, 80, D), F32),
            pltpu.VMEM((4, 2, 8, 80, 128), F32),
            pltpu.VMEM((2 * SHIFTED, 2, 4, 16, D), BF),
            pltpu.VMEM((2 * SHIFTED, 64, D), BF),
            pltpu.VMEM((2 * SHIFTED, 128, 1024), BF),
            pltpu.VMEM((2 * SHIFTED, 64, D), BF),
        ],
        compiler_params=params(),
        cost_estimate=pl.CostEstimate(flops=10**10, bytes_accessed=10**7, transcendentals=0),
    )(
        par, *x1_parts, near_mid, near_edge, norm_gain, merge_gain, *weights
    )


def embedding_matrix(embed_weight, land_embed):
    w = jnp.pad(embed_weight, ((0, 0), (0, 0), (0, 2), (0, 0))).reshape(3, 4, 3, 4, 8, D)
    w = w.transpose(0, 2, 1, 3, 4, 5)
    share = land_embed / 16
    high = lax.reduce_precision(share, 8, 7)
    at = [lax.broadcasted_iota(jnp.int32, w.shape, d) for d in (0, 1, 4)]
    middle = (at[0] == 1) & (at[1] == 1)
    w = jnp.where(middle & (at[2] == 6), high.astype(BF), w)
    w = jnp.where(middle & (at[2] == 7), (share - high).astype(BF), w)
    return w.reshape(9 * 128, D)


def swap(block, first):
    count = lax.axis_size("lat")
    pairs = []
    for i in range(first, count - 1, 2):
        pairs += [(i, i + 1), (i + 1, i)]
    return lax.ppermute(block, "lat", pairs)


def around(block, distance):
    count = lax.axis_size("lon")
    return lax.ppermute(block, "lon", [(i, (i + distance) % count) for i in range(count)])


def shards(
    atmos, orography, land_sea, embed_weight, level_embed, land_embed, norm_gain,
    w_query, w_keyval, w_out, merge_gain, merge_weight,
):
    lat = lax.axis_index("lat")
    par = lat % 2
    pole = (lat == 0) | (lat == lax.axis_size("lat") - 1)
    place = jnp.stack([par, pole]).astype(jnp.int32)
    own, send, edge, near = patches(place, atmos, orography, land_sea)
    edge = swap(edge, 0)
    near = swap(near, 1)
    send = lax.dynamic_update_slice(send, edge, (7 * (1 - par), 0, 0))
    far = swap(send, 1)
    wemb = embedding_matrix(embed_weight, land_embed)
    weights = wemb, level_embed, norm_gain, w_query, w_keyval, w_out
    own_mid, send_mid, own = first_block((0,), MIDDLE, edge, place, (own, edge, near), *weights)
    near_mid = swap(send_mid, 0)
    far, low, high = unpack_far(own_mid, far, own)
    from_low, from_high = around(high, 1), around(low, -1)
    (outer_mid,) = first_block((1,), MIDDLE, own_mid, place, (own, far), *weights)
    own_edge, send_edge = first_block(
        (0,), EDGES, outer_mid, place, (own, from_low, from_high), *weights
    )
    near_edge = swap(send_edge, 0)
    (outer_edge,) = first_block(
        (1,), EDGES, own_edge, place, (own, far, from_low, from_high), *weights
    )
    return second_block(
        place, (own_mid, outer_mid, own_edge, outer_edge), near_mid, near_edge, norm_gain,
        merge_gain.reshape(1, -1), w_query, w_keyval, w_out, merge_weight,
    )


def solution(mesh):
    in_specs = (P(None, None, "lat", "lon"), P("lat", "lon"), P("lat", "lon")) + (P(),) * 9
    out_specs = P(None, "lat", "lon", None)
    return jax.shard_map(shards, mesh=mesh, in_specs=in_specs, out_specs=out_specs, check_vma=False)
```

```python
import functools
import math

import jax
import jax.numpy as jnp
from jax import lax
from jax.experimental import pallas as pl
from jax.experimental.pallas import tpu as pltpu
from jax.sharding import PartitionSpec as P

BF = jnp.bfloat16
F32 = jnp.float32
D = 512
HEAD_DIM = 64
WINS = 10
SCALE = HEAD_DIM ** (-0.5) * math.log2(math.e)
VMEM_LIMIT = 32 * 1024 * 1024


def iota(shape, dim):
    return lax.broadcasted_iota(jnp.int32, shape, dim)


def one_hot(cond):
    return jnp.where(cond, 1.0, 0.0).astype(BF)


def mm(a, b):
    return jnp.dot(a, b, preferred_element_type=F32)


def mm_t(a, b):
    return lax.dot_general(a, b, (((1,), (1,)), ((), ())), preferred_element_type=F32)


def params():
    return pltpu.CompilerParams(vmem_limit_bytes=VMEM_LIMIT)


def patch_kernel(
    par_ref, atmos_any, oro_any, land_any, own_ref, send_ref, edge_ref, near_ref,
    atmos_ref, oro_ref, land_ref, sems,
):
    par = par_ref[0]
    loads = [
        pltpu.make_async_copy(src, dst, sems.at[n])
        for n, (src, dst) in enumerate(
            [(atmos_any, atmos_ref), (oro_any, oro_ref), (land_any, land_ref)]
        )
    ]
    for load in loads:
        load.start()
    row, src = iota((1024, 384), 0), iota((1024, 384), 1)
    i, r, ch = row // 128, (row % 128) // 32, row % 8
    channel = jnp.where(ch < 5, ch, jnp.where(ch == 5, 10, jnp.where(ch == 6, 11, 9)))
    pick_main = one_hot(src == channel * 32 + i * 4 + r)
    pick_aux = one_hot(src == (5 + row % 4) * 32 + i * 4 + r)
    for load in loads:
        load.wait()
    cells = jnp.concatenate(
        [
            atmos_ref[...].reshape(320, 256),
            oro_ref[...],
            land_ref[...].astype(F32).astype(BF),
        ],
        axis=0,
    )
    main, aux = mm(pick_main, cells), mm(pick_aux, cells)
    row, col = iota((1024, 256), 0), iota((1024, 256), 1)
    c, half = (row % 32) // 8, (row % 8) // 4
    main = jnp.where(col % 4 == c, main, 0.0).astype(BF)
    aux = jnp.where((col % 4 == c) & (col // 128 == half), aux, 0.0).astype(BF)
    j, col = iota((64, 256), 0), iota((64, 256), 1)
    main = mm_t(one_hot(col // 4 == j), main).astype(BF)
    j, col = iota((32, 256), 0), iota((32, 256), 1)
    aux = mm_t(one_hot((col % 128) // 4 == j), aux).astype(BF)
    for i in range(8):
        own_ref[i, 0:64, :] = main[:, i * 128 : i * 128 + 128]
        own_ref[i, 64:96, :] = aux[:, i * 128 : i * 128 + 128]
    send_ref[pl.ds(par, 7)] = own_ref[pl.ds(1 - par, 7)]
    edge_ref[...] = own_ref[pl.ds(7 * (1 - par), 1)]
    near_ref[...] = own_ref[pl.ds(7 * par, 1)]


def patches(par, atmos, orography, land_sea):
    cells = [pltpu.with_memory_space_constraint(a, pltpu.HBM) for a in (atmos, orography, land_sea)]
    return pl.pallas_call(
        patch_kernel,
        out_shape=tuple(jax.ShapeDtypeStruct((n, 96, 128), BF) for n in (8, 8, 1, 1)),
        in_specs=[pl.BlockSpec(memory_space=pltpu.SMEM)] + [pl.BlockSpec(memory_space=pltpu.HBM)] * 3,
        out_specs=(pl.BlockSpec(memory_space=pltpu.VMEM),) * 4,
        scratch_shapes=[
            pltpu.VMEM(atmos.shape, BF),
            pltpu.VMEM(orography.shape, BF),
            pltpu.VMEM(land_sea.shape, jnp.int32),
            pltpu.SemaphoreType.DMA((3,)),
        ],
        compiler_params=params(),
        cost_estimate=pl.CostEstimate(flops=10**9, bytes_accessed=10**6, transcendentals=0),
    )(par, *cells)


def unpack_rows(packed, out_ref):
    rows = packed.shape[0]
    k, n = iota((256, 256), 0), iota((256, 256), 1)
    ch, lane = n % 8, n % 128
    from_main0 = jnp.where(ch == 7, lane - 1, lane)
    from_main1 = jnp.where(ch == 7, lane - 1, jnp.where(ch == 4, lane + 3, lane))
    aux = packed[:, 64:96, :]
    for half in range(2):
        from_one = jnp.where(ch < 4, 128 + lane + 4 * half, from_main1)
        pick = one_hot(k == jnp.where(n < 128, from_main0, from_one))
        both = jnp.concatenate([packed[:, half * 32 : half * 32 + 32, :], aux], axis=2)
        got = mm(both.reshape(rows * 32, 256), pick).astype(BF).reshape(rows, 32, 256)
        for level in range(2):
            tile = got[:, :, level * 128 : level * 128 + 128]
            out_ref[level, :, half * 32 : half * 32 + 32, :] = tile


def unpack_far_kernel(after_ref, packed_ref, own_ref, far_ref, high_ref):
    del after_ref
    unpack_rows(packed_ref, far_ref)
    high_ref[:, 0:10] = own_ref[:, :, 48:64, :]
    high_ref[:, 10:18] = far_ref[:, :, 48:64, :]


def unpack_far(after, packed, own):
    vmem = pl.BlockSpec(memory_space=pltpu.VMEM)
    return pl.pallas_call(
        unpack_far_kernel,
        out_shape=(
            jax.ShapeDtypeStruct((2, 8, 64, 128), BF),
            jax.ShapeDtypeStruct((2, 18, 16, 128), BF),
        ),
        in_specs=[pl.BlockSpec(memory_space=pl.ANY)] + [vmem] * 2,
        out_specs=(vmem,) * 2,
        compiler_params=params(),
        cost_estimate=pl.CostEstimate(flops=10**9, bytes_accessed=10**6, transcendentals=0),
    )(after, packed, own)


def pipelined(stages, groups):
    for step in range(len(groups) + len(stages) - 1):
        for k in range(len(stages)):
            if 0 <= step - k < len(groups):
                stages[k](groups[step - k])


def normalize(x, gain):
    mean = jnp.mean(x, axis=-1, keepdims=True)
    x = x - mean
    var = jnp.mean(x * x, axis=-1, keepdims=True)
    return x * lax.rsqrt(var + 1e-05) * gain


def attend(q, k, v, bias):
    left = iota((128, 128), 1) < HEAD_DIM
    ones_left, ones_right = one_hot(left), one_hot(~left)
    zero = jnp.zeros((128, 128), BF)
    out = []
    for pair in range(4):
        at = slice(pair * 128, pair * 128 + 128)
        kp, vp = k[:, at], v[:, at]
        keys = jnp.concatenate([jnp.where(left, kp, zero), jnp.where(left, zero, kp)], axis=0)
        s = mm_t(q[:, at], keys)
        if bias is not None:
            s = s + bias
        s0, s1 = s[:, :128], s[:, 128:]
        p0 = jnp.exp2(s0 - jnp.max(s0, axis=-1, keepdims=True))
        p1 = jnp.exp2(s1 - jnp.max(s1, axis=-1, keepdims=True))
        p = jnp.concatenate([p0, p1], axis=1).astype(BF)
        vals = jnp.concatenate(
            [
                jnp.concatenate([jnp.where(left, vp, zero), ones_left], axis=1),
                jnp.concatenate([jnp.where(left, zero, vp), ones_right], axis=1),
            ],
            axis=0,
        )
        o = mm(p, vals)
        out.append((o[:, :128] / o[:, 128:]).astype(BF))
    return jnp.concatenate(out, axis=1)


LOW, MIDDLE, HIGH = (0,), (1, 2, 3), (4,)


def first_kernel(parts, which, after_ref, *refs):
    del after_ref
    par_ref, refs = refs[0], refs[1:]
    leading, following = parts == (0,) and which == MIDDLE, parts == (1,) and which == MIDDLE
    if leading:
        own_packed, edge_ref, near_ref, refs = refs[0], refs[1], refs[2], refs[3:]
    else:
        own_ref, refs = refs[0], refs[1:]
    if 1 in parts:
        far_ref, refs = refs[0], refs[1:]
    if which != MIDDLE:
        side_ref, refs = refs[0], refs[1:]
    wemb_ref, lev_ref, gain_ref, wq_ref, wkv_ref, wo_ref, *refs = refs
    x1_refs, refs = refs[: len(parts)], refs[len(parts) :]
    if 0 in parts:
        send_ref, refs = refs[0], refs[1:]
    if leading:
        own_ref, refs = refs[0], refs[1:]
    if following:
        low_ref, refs = refs[0], refs[1:]
    wide, gathered, x0, normed, query, keyval, heads, *refs = refs
    par = par_ref[0]
    if leading:
        packed, wq, wkv, wo, sems = refs
        loads = [
            pltpu.make_async_copy(src.at[0], dst, sems.at[n])
            for n, (src, dst) in enumerate([(wkv_ref, wkv), (wq_ref, wq), (wo_ref, wo)])
        ]
        for load in loads:
            load.start()
        packed[1:9] = own_packed[...]
        packed[pl.ds(9 * par, 1)] = near_ref[...]
        packed[pl.ds(9 * (1 - par), 1)] = edge_ref[...]
        unpack_rows(packed, own_ref)
    else:
        wq, wkv, wo = wq_ref.at[0], wkv_ref.at[0], wo_ref.at[0]

    def spread(part, to, count, center, side):
        rows = (slice(None), pl.ds(to, count))
        if which == LOW:
            wide[part, *rows, 0:16, :] = side().astype(F32)
            wide[part, *rows, 16:32, :] = center[:, :, 0:16, :].astype(F32)
        elif which == HIGH:
            wide[part, *rows, 64:80, :] = center[:, :, 48:64, :].astype(F32)
            wide[part, *rows, 80:96, :] = side().astype(F32)
        else:
            wide[part, *rows, 16:80, :] = center.astype(F32)

    if 0 in parts:
        spread(0, 0, 10, own_ref[...], lambda: side_ref[:, 0:10])
    if 1 in parts:
        spread(1, 2 * par, 8, far_ref[...], lambda: side_ref[:, 10:18])
        beside = pl.ds(8 * par, 2)
        spread(1, 8 * (1 - par), 2, own_ref[:, beside], lambda: side_ref[:, beside])
    if following:
        low_ref[:, 0:10] = own_ref[:, :, 0:16, :]
        low_ref[:, 10:18] = far_ref[:, :, 0:16, :]
    gain = gain_ref[0:1, :]
    half = 1 - par

    cols_of = len(which)

    def slots(part):
        at = parts.index(part) * cols_of
        return at, slice(at, at + cols_of)

    def embed(part):
        first, here = slots(part)
        for n, g in enumerate(which):
            for dj in range(3):
                cols = slice(g * 16 + 7 + dj, g * 16 + 23 + dj)
                got = wide[part, :, :, cols, :].astype(BF)
                gathered[first + n, :, :, :, dj * 128 : dj * 128 + 128] = got
        for n in range(cols_of):
            lhs = jnp.concatenate(
                [gathered[first + n, :, di : di + 8].reshape(256, 384) for di in range(3)], axis=1
            )
            x = mm(lhs, wemb_ref[...]).reshape(2, 8, 16, D)
            for level in range(2):
                x0[first + n, level] = x[level] + lev_ref[level : level + 1, :]

    def norm(part):
        first, here = slots(part)
        for slot in range(first, first + cols_of):
            for u in range(2):
                x = x0[slot, :, :, u * 8 : u * 8 + 8, :].reshape(128, D)
                normed[slot, u] = normalize(x, gain).astype(BF).reshape(2, 4, 16, D)

    def project(part):
        first, here = slots(part)
        n = normed[here].reshape(256 * cols_of, D)
        if leading:
            loads[0].wait()
            loads[1].wait()
        keyval[here] = mm(n, wkv[...]).astype(BF).reshape(cols_of, 2, 128, 1024)
        if part:
            n = normed[here, :, :, pl.ds(half * 2, 2)].reshape(128 * cols_of, D)
        q = (mm(n, wq[...]) * SCALE).astype(BF)
        query[here, :, : 64 if part else 128] = q.reshape(cols_of, 2, -1, D)

    def attention(part):
        first, here = slots(part)
        count = 64 if part else 128
        for slot in range(first, first + cols_of):
            for u in range(2):
                kv = keyval[slot, u]
                heads[slot, u, :count] = attend(query[slot, u, :count], kv[:, :D], kv[:, D:], None)

    def project_out(part):
        first, here = slots(part)
        count = 64 if part else 128
        if leading:
            loads[2].wait()
        out = mm(heads[here, :, :count].reshape(2 * cols_of * count, D), wo[...])
        for n in range(2 * cols_of):
            slot, u = first + n // 2, n % 2
            cols, mine = slice(n * 8, n * 8 + 8), slice(u * 8, u * 8 + 8)
            add = out[n * count : n * count + count].reshape(2, count // 16, 8, D)
            if part:
                x1_refs[-1][:, :, cols, :] = x0[slot, :, pl.ds(4 * half, 4), mine, :] + add
            else:
                for h in range(2):
                    to = pl.ds(4 * (par if h == 0 else half), 4)
                    rows = slice(4 * h, 4 * h + 4)
                    x1_refs[0][:, to, cols, :] = x0[slot, :, rows, mine, :] + add[:, rows]

    pipelined([embed, norm, project, attention, project_out], list(parts))
    if 0 in parts:
        send_ref[...] = x1_refs[0][:, 4:8].astype(BF)


def first_block(parts, which, after, par, patch_arrays, wemb, level_embed, norm_gain, w_query, w_keyval, w_out):
    vmem = pl.BlockSpec(memory_space=pltpu.VMEM)
    width, count = 16 * len(which), len(parts) * len(which)
    leading = parts == (0,) and which == MIDDLE
    outs = [jax.ShapeDtypeStruct((2, 4 if part else 8, width, D), F32) for part in parts]
    if 0 in parts:
        outs.append(jax.ShapeDtypeStruct((2, 4, width, D), BF))
    scratch = [
        pltpu.VMEM((2, 2, 10, 96, 128), F32),
        pltpu.VMEM((count, 2, 10, 16, 384), BF),
        pltpu.VMEM((count, 2, 8, 16, D), F32),
        pltpu.VMEM((count, 2, 2, 4, 16, D), BF),
        pltpu.VMEM((count, 2, 128, D), BF),
        pltpu.VMEM((count, 2, 128, 1024), BF),
        pltpu.VMEM((count, 2, 128, D), BF),
    ]
    if parts == (1,) and which == MIDDLE:
        outs.append(jax.ShapeDtypeStruct((2, 18, 16, 128), BF))
    projections = [w_query, w_keyval, w_out]
    if leading:
        outs.append(jax.ShapeDtypeStruct((2, 10, 64, 128), BF))
        scratch += [
            pltpu.VMEM((10, 96, 128), BF),
            pltpu.VMEM((D, D), BF),
            pltpu.VMEM((D, 1024), BF),
            pltpu.VMEM((D, D), BF),
            pltpu.SemaphoreType.DMA((3,)),
        ]
        projections = [pltpu.with_memory_space_constraint(w, pltpu.HBM) for w in projections]
    else:
        projections = [pltpu.with_memory_space_constraint(w, pltpu.VMEM) for w in projections]
    place_of = pl.BlockSpec(memory_space=pltpu.HBM if leading else pltpu.VMEM)
    return pl.pallas_call(
        functools.partial(first_kernel, parts, which),
        out_shape=tuple(outs),
        in_specs=[pl.BlockSpec(memory_space=pl.ANY), pl.BlockSpec(memory_space=pltpu.SMEM)]
        + [vmem] * (3 + len(patch_arrays)) + [place_of] * 3,
        out_specs=(vmem,) * len(outs),
        scratch_shapes=scratch,
        compiler_params=params(),
        cost_estimate=pl.CostEstimate(flops=10**10, bytes_accessed=10**7, transcendentals=0),
    )(after, par, *patch_arrays, wemb, level_embed, norm_gain, *projections)


SHIFTED = WINS - 1


def second_kernel(
    par_ref, own_low, outer_low, own_mid, outer_mid, own_high, outer_high,
    near_low_ref, near_mid_ref, near_high_ref, gain_ref, mgain_ref,
    wq_ref, wkv_ref, wo_ref, wm_ref,
    out_ref,
    near, x2, normed, query, keyval, heads,
):
    par, pole = par_ref[0], par_ref[1]
    near[:, :, 0:16, :] = near_low_ref[...].astype(F32)
    near[:, :, 16:64, :] = near_mid_ref[...].astype(F32)
    near[:, :, 64:80, :] = near_high_ref[...].astype(F32)
    gain = gain_ref[1:2, :]
    upper = iota((8, D), 0) >= 4
    key_row = (iota((1, 256), 1) // 8) % 8
    bias = jnp.where(key_row < 4, F32(-1e30), F32(0)) * pole.astype(F32)

    def block(n, first, last):
        if first < 4 < last:
            return jnp.concatenate([block(n, first, 4), block(n, 4, last)], axis=1)
        if first >= 12:
            return near[:, first - 12 : last - 12, n * 8 : n * 8 + 8, :]
        part = 0 if n < 2 else 1 if n < 8 else 2
        at = n * 8 - (0, 16, 64)[part]
        if first < 4:
            return (outer_low, outer_mid, outer_high)[part][:, first:last, at : at + 8, :]
        return (own_low, own_mid, own_high)[part][:, first - 4 : last - 4, at : at + 8, :]

    def window(w, first, last):
        return jnp.where(upper, block(w, first, last), block(w + 1, first, last))

    def norm(s):
        for w in range(SHIFTED):
            if s == 0:
                x = window(w, 0, 8)
            else:
                x = jnp.concatenate(
                    [window(w, 8, 12), window(w, 12, 16)], axis=1
                )
            n = normalize(x.reshape(128, D), gain).astype(BF)
            normed[s * SHIFTED + w] = n.reshape(2, 4, 16, D)

    def project(s):
        at = slice(s * SHIFTED, s * SHIFTED + SHIFTED)
        n = normed[at].reshape(SHIFTED * 128, D)
        keyval[at] = mm(n, wkv_ref[1]).astype(BF).reshape(SHIFTED, 128, 1024)
        n = normed[at, :, 2 - 2 * s : 4 - 2 * s].reshape(SHIFTED * 64, D)
        query[at] = (mm(n, wq_ref[1]) * SCALE).astype(BF).reshape(SHIFTED, 64, D)

    def attention(s):
        for t in range(s * SHIFTED, s * SHIFTED + SHIFTED):
            kv = keyval[t]
            heads[t] = attend(query[t], kv[:, :D], kv[:, D:], None if s else bias)

    def project_out(s):
        at = slice(s * SHIFTED, s * SHIFTED + SHIFTED)
        out = mm(heads[at].reshape(SHIFTED * 64, D), wo_ref[1])
        rows = slice(s * 4, s * 4 + 4)
        for w in range(SHIFTED):
            new = window(w, 4 + s * 4, 8 + s * 4)
            new = new + out[w * 64 : w * 64 + 64].reshape(2, 4, 8, D)
            for c in range(4):
                piece = new[..., c * 128 : c * 128 + 128]
                x2[c, :, rows, w * 8 + 4 : w * 8 + 8, :] = piece[:, :, 4:8, :]
                x2[c, :, rows, w * 8 + 8 : w * 8 + 12, :] = piece[:, :, 0:4, :]

    def merge(s):
        parts = []
        for p in range(4):
            got = [
                jnp.concatenate(
                    [
                        x2[c, level, s * 4 + 2 * a + p % 2, pl.ds(8 + p // 2, 32, stride=2), :]
                        for c in range(4)
                    ],
                    axis=1,
                )
                for level in range(2)
                for a in range(2)
            ]
            parts.append(jnp.concatenate(got, axis=0))
        n = normalize(jnp.concatenate(parts, axis=1), mgain_ref[...]).astype(BF)
        out = mm(n, wm_ref[...]).astype(BF)
        out_ref[:, pl.ds(2 * ((par + s) % 2), 2)] = out.reshape(2, 2, 32, 1024)

    pipelined([norm, project, attention, project_out, merge], [0, 1])


def second_block(par, x1_parts, near_parts, norm_gain, merge_gain, w_query, w_keyval, w_out, merge_weight):
    vmem = pl.BlockSpec(memory_space=pltpu.VMEM)
    weights = [
        pltpu.with_memory_space_constraint(w, pltpu.VMEM) for w in (w_query, w_keyval, w_out, merge_weight)
    ]
    return pl.pallas_call(
        second_kernel,
        out_shape=jax.ShapeDtypeStruct((2, 4, 32, 1024), BF),
        in_specs=[pl.BlockSpec(memory_space=pltpu.SMEM)] + [vmem] * 15,
        out_specs=vmem,
        scratch_shapes=[
            pltpu.VMEM((2, 4, 80, D), F32),
            pltpu.VMEM((4, 2, 8, 80, 128), F32),
            pltpu.VMEM((2 * SHIFTED, 2, 4, 16, D), BF),
            pltpu.VMEM((2 * SHIFTED, 64, D), BF),
            pltpu.VMEM((2 * SHIFTED, 128, 1024), BF),
            pltpu.VMEM((2 * SHIFTED, 64, D), BF),
        ],
        compiler_params=params(),
        cost_estimate=pl.CostEstimate(flops=10**10, bytes_accessed=10**7, transcendentals=0),
    )(
        par, *x1_parts, *near_parts, norm_gain, merge_gain, *weights
    )


def embedding_matrix(embed_weight, land_embed):
    w = jnp.pad(embed_weight, ((0, 0), (0, 0), (0, 2), (0, 0))).reshape(3, 4, 3, 4, 8, D)
    w = w.transpose(0, 2, 1, 3, 4, 5)
    share = land_embed / 16
    high = lax.reduce_precision(share, 8, 7)
    at = [lax.broadcasted_iota(jnp.int32, w.shape, d) for d in (0, 1, 4)]
    middle = (at[0] == 1) & (at[1] == 1)
    w = jnp.where(middle & (at[2] == 6), high.astype(BF), w)
    w = jnp.where(middle & (at[2] == 7), (share - high).astype(BF), w)
    return w.reshape(9 * 128, D)


def swap(block, first):
    count = lax.axis_size("lat")
    pairs = []
    for i in range(first, count - 1, 2):
        pairs += [(i, i + 1), (i + 1, i)]
    return lax.ppermute(block, "lat", pairs)


def around(block, distance):
    count = lax.axis_size("lon")
    return lax.ppermute(block, "lon", [(i, (i + distance) % count) for i in range(count)])


def shards(
    atmos, orography, land_sea, embed_weight, level_embed, land_embed, norm_gain,
    w_query, w_keyval, w_out, merge_gain, merge_weight,
):
    lat = lax.axis_index("lat")
    par = lat % 2
    pole = (lat == 0) | (lat == lax.axis_size("lat") - 1)
    place = jnp.stack([par, pole]).astype(jnp.int32)
    own, send, edge, near = patches(place, atmos, orography, land_sea)
    edge = swap(edge, 0)
    near = swap(near, 1)
    send = lax.dynamic_update_slice(send, edge, (7 * (1 - par), 0, 0))
    far = swap(send, 1)
    wemb = embedding_matrix(embed_weight, land_embed)
    weights = wemb, level_embed, norm_gain, w_query, w_keyval, w_out
    own_mid, send_mid, own = first_block((0,), MIDDLE, edge, place, (own, edge, near), *weights)
    near_mid = swap(send_mid, 0)
    far, high = unpack_far(own_mid, far, own)
    from_low = around(high, 1)
    outer_mid, low = first_block((1,), MIDDLE, own_mid, place, (own, far), *weights)
    from_high = around(low, -1)
    own_low, outer_low, send_low = first_block(
        (0, 1), LOW, outer_mid, place, (own, far, from_low), *weights
    )
    near_low = swap(send_low, 0)
    own_high, send_high = first_block((0,), HIGH, own_low, place, (own, from_high), *weights)
    near_high = swap(send_high, 0)
    (outer_high,) = first_block((1,), HIGH, own_high, place, (own, far, from_high), *weights)
    return second_block(
        place, (own_low, outer_low, own_mid, outer_mid, own_high, outer_high),
        (near_low, near_mid, near_high), norm_gain,
        merge_gain.reshape(1, -1), w_query, w_keyval, w_out, merge_weight,
    )


def solution(mesh):
    in_specs = (P(None, None, "lat", "lon"), P("lat", "lon"), P("lat", "lon")) + (P(),) * 9
    out_specs = P(None, "lat", "lon", None)
    return jax.shard_map(shards, mesh=mesh, in_specs=in_specs, out_specs=out_specs, check_vma=False)
```

```python
import functools
import math

import jax
import jax.numpy as jnp
from jax import lax
from jax.experimental import pallas as pl
from jax.experimental.pallas import tpu as pltpu
from jax.sharding import PartitionSpec as P

BF = jnp.bfloat16
F32 = jnp.float32
D = 512
HEAD_DIM = 64
WINS = 10
SCALE = HEAD_DIM ** (-0.5) * math.log2(math.e)
VMEM_LIMIT = 32 * 1024 * 1024


def iota(shape, dim):
    return lax.broadcasted_iota(jnp.int32, shape, dim)


def one_hot(cond):
    return jnp.where(cond, 1.0, 0.0).astype(BF)


def mm(a, b):
    return jnp.dot(a, b, preferred_element_type=F32)


def mm_t(a, b):
    return lax.dot_general(a, b, (((1,), (1,)), ((), ())), preferred_element_type=F32)


def params():
    return pltpu.CompilerParams(vmem_limit_bytes=VMEM_LIMIT)


def patch_kernel(
    par_ref, atmos_any, oro_any, land_any, own_ref, send_ref, edge_ref, near_ref,
    atmos_ref, oro_ref, land_ref, sems,
):
    par = par_ref[0]
    loads = [
        pltpu.make_async_copy(src, dst, sems.at[n])
        for n, (src, dst) in enumerate(
            [(atmos_any, atmos_ref), (oro_any, oro_ref), (land_any, land_ref)]
        )
    ]
    for load in loads:
        load.start()
    row, src = iota((1024, 1), 0), iota((1024, 384), 1)
    i, r, ch = row >> 7, (row >> 5) & 3, row & 7
    channel = jnp.where(ch < 5, ch, jnp.where(ch == 5, 10, jnp.where(ch == 6, 11, 9)))
    pick_main = one_hot(src == channel * 32 + i * 4 + r)
    pick_aux = one_hot(src == (5 + (row & 3)) * 32 + i * 4 + r)
    for load in loads:
        load.wait()
    cells = jnp.concatenate(
        [
            atmos_ref[...].reshape(320, 256),
            oro_ref[...],
            land_ref[...].astype(F32).astype(BF),
        ],
        axis=0,
    )
    main, aux = mm(pick_main, cells), mm(pick_aux, cells)
    col = iota((1, 256), 1)
    c, half = (row >> 3) & 3, (row >> 2) & 1
    main = jnp.where((col & 3) == c, main, 0.0).astype(BF)
    aux = jnp.where((col & 3) + 4 * (col >> 7) == c + 4 * half, aux, 0.0).astype(BF)
    j, col = iota((64, 256), 0), iota((64, 256), 1)
    main = mm_t(one_hot((col >> 2) == j), main).astype(BF)
    j, col = iota((32, 256), 0), iota((32, 256), 1)
    aux = mm_t(one_hot(((col & 127) >> 2) == j), aux).astype(BF)
    for i in range(8):
        own_ref[i, 0:64, :] = main[:, i * 128 : i * 128 + 128]
        own_ref[i, 64:96, :] = aux[:, i * 128 : i * 128 + 128]
    send_ref[pl.ds(par, 7)] = own_ref[pl.ds(1 - par, 7)]
    edge_ref[...] = own_ref[pl.ds(7 * (1 - par), 1)]
    near_ref[...] = own_ref[pl.ds(7 * par, 1)]


def patches(par, atmos, orography, land_sea):
    cells = [pltpu.with_memory_space_constraint(a, pltpu.HBM) for a in (atmos, orography, land_sea)]
    return pl.pallas_call(
        patch_kernel,
        out_shape=tuple(jax.ShapeDtypeStruct((n, 96, 128), BF) for n in (8, 8, 1, 1)),
        in_specs=[pl.BlockSpec(memory_space=pltpu.SMEM)] + [pl.BlockSpec(memory_space=pltpu.HBM)] * 3,
        out_specs=(pl.BlockSpec(memory_space=pltpu.VMEM),) * 4,
        scratch_shapes=[
            pltpu.VMEM(atmos.shape, BF),
            pltpu.VMEM(orography.shape, BF),
            pltpu.VMEM(land_sea.shape, jnp.int32),
            pltpu.SemaphoreType.DMA((3,)),
        ],
        compiler_params=params(),
        cost_estimate=pl.CostEstimate(flops=10**9, bytes_accessed=10**6, transcendentals=0),
    )(par, *cells)


def unpack_rows(packed, out_ref):
    rows = packed.shape[0]
    k, n = iota((256, 256), 0), iota((256, 256), 1)
    ch, lane = n % 8, n % 128
    from_main0 = jnp.where(ch == 7, lane - 1, lane)
    from_main1 = jnp.where(ch == 7, lane - 1, jnp.where(ch == 4, lane + 3, lane))
    aux = packed[:, 64:96, :]
    for half in range(2):
        from_one = jnp.where(ch < 4, 128 + lane + 4 * half, from_main1)
        pick = one_hot(k == jnp.where(n < 128, from_main0, from_one))
        both = jnp.concatenate([packed[:, half * 32 : half * 32 + 32, :], aux], axis=2)
        got = mm(both.reshape(rows * 32, 256), pick).astype(BF).reshape(rows, 32, 256)
        for level in range(2):
            tile = got[:, :, level * 128 : level * 128 + 128]
            out_ref[level, :, half * 32 : half * 32 + 32, :] = tile


def unpack_far_kernel(after_ref, packed_ref, own_ref, far_ref, low_ref, high_ref, ninth):
    del after_ref
    unpack_rows(packed_ref, far_ref)
    for n, (first, inner, out_ref) in enumerate([(0, 8, low_ref), (48, 7, high_ref)]):
        cols = slice(first, first + 16)
        edge = jnp.concatenate([own_ref[:, :, cols, :], far_ref[:, :, cols, :]], axis=1).astype(F32)
        near = edge[:, :, 8 * n : 8 * n + 8, :]
        out_ref[0:18] = near.reshape(18, 16, 128).astype(BF)
        for level in range(2):
            for row in range(18):
                at = level * 18 + row
                ninth[n, at : at + 1, :] = edge[level, row, inner : inner + 1, :]
        ninth[n, 36:48, :] = jnp.zeros((12, 128), F32)
        out_ref[18:21] = ninth[n].reshape(3, 16, 128).astype(BF)


def unpack_far(after, packed, own):
    vmem = pl.BlockSpec(memory_space=pltpu.VMEM)
    return pl.pallas_call(
        unpack_far_kernel,
        out_shape=(
            jax.ShapeDtypeStruct((2, 8, 64, 128), BF),
            jax.ShapeDtypeStruct((21, 16, 128), BF),
            jax.ShapeDtypeStruct((21, 16, 128), BF),
        ),
        in_specs=[pl.BlockSpec(memory_space=pl.ANY)] + [vmem] * 2,
        out_specs=(vmem,) * 3,
        scratch_shapes=[pltpu.VMEM((2, 48, 128), F32)],
        compiler_params=params(),
        cost_estimate=pl.CostEstimate(flops=10**9, bytes_accessed=10**6, transcendentals=0),
    )(after, packed, own)


def pipelined(stages, groups):
    for step in range(len(groups) + len(stages) - 1):
        for k in range(len(stages)):
            if 0 <= step - k < len(groups):
                stages[k](groups[step - k])


def normalize(x, gain):
    mean = jnp.mean(x, axis=-1, keepdims=True)
    x = x - mean
    var = jnp.mean(x * x, axis=-1, keepdims=True)
    return x * lax.rsqrt(var + 1e-05) * gain


def attend(q, k, v, bias):
    left = iota((128, 128), 1) < HEAD_DIM
    ones_left, ones_right = one_hot(left), one_hot(~left)
    zero = jnp.zeros((128, 128), BF)
    out = []
    for pair in range(4):
        at = slice(pair * 128, pair * 128 + 128)
        kp, vp = k[:, at], v[:, at]
        keys = jnp.concatenate([jnp.where(left, kp, zero), jnp.where(left, zero, kp)], axis=0)
        s = mm_t(q[:, at], keys)
        if bias is not None:
            s = s + bias
        s0, s1 = s[:, :128], s[:, 128:]
        p0 = jnp.exp2(s0 - jnp.max(s0, axis=-1, keepdims=True))
        p1 = jnp.exp2(s1 - jnp.max(s1, axis=-1, keepdims=True))
        p = jnp.concatenate([p0, p1], axis=1).astype(BF)
        vals = jnp.concatenate(
            [
                jnp.concatenate([jnp.where(left, vp, zero), ones_left], axis=1),
                jnp.concatenate([jnp.where(left, zero, vp), ones_right], axis=1),
            ],
            axis=0,
        )
        o = mm(p, vals)
        out.append((o[:, :128] / o[:, 128:]).astype(BF))
    return jnp.concatenate(out, axis=1)


MIDDLE, EDGES = (1, 2, 3), (0, 4)


def first_kernel(parts, which, after_ref, *refs):
    del after_ref
    par_ref, refs = refs[0], refs[1:]
    leading = parts == (0,) and which == MIDDLE
    if leading:
        own_packed, edge_ref, near_ref, refs = refs[0], refs[1], refs[2], refs[3:]
    else:
        own_ref, refs = refs[0], refs[1:]
    if 1 in parts:
        far_ref, refs = refs[0], refs[1:]
    if which == EDGES:
        low_ref, high_ref, refs = refs[0], refs[1], refs[2:]
    wemb_ref, lev_ref, gain_ref, wq_ref, wkv_ref, wo_ref, *refs = refs
    x1_refs, refs = refs[: len(parts)], refs[len(parts) :]
    if 0 in parts:
        send_ref, refs = refs[0], refs[1:]
    if leading:
        own_ref, refs = refs[0], refs[1:]
    wide, ninth, gathered, x0, normed, query, keyval, heads, *refs = refs
    par = par_ref[0]
    if leading:
        packed, wq, wkv, wo, sems = refs
        loads = [
            pltpu.make_async_copy(src.at[0], dst, sems.at[n])
            for n, (src, dst) in enumerate([(wkv_ref, wkv), (wq_ref, wq), (wo_ref, wo)])
        ]
        for load in loads:
            load.start()
        packed[1:9] = own_packed[...]
        packed[pl.ds(9 * par, 1)] = near_ref[...]
        packed[pl.ds(9 * (1 - par), 1)] = edge_ref[...]
        unpack_rows(packed, own_ref)
    else:
        wq, wkv, wo = wq_ref.at[0], wkv_ref.at[0], wo_ref.at[0]

    if which == EDGES:
        for n, side in enumerate((low_ref, high_ref)):
            ninth[n] = side[18:21].astype(F32).reshape(48, 128)

    def spread(part, to, count, center, first):
        rows = (slice(None), pl.ds(to, count))
        if which != EDGES:
            wide[part, *rows, 16:80, :] = center.astype(F32)
            return
        wide[part, *rows, 16:32, :] = center[:, :, 0:16, :].astype(F32)
        wide[part, *rows, 64:80, :] = center[:, :, 48:64, :].astype(F32)
        for n, (side, cols, nine) in enumerate([(low_ref, slice(8, 16), 7), (high_ref, slice(80, 88), 88)]):
            for level in range(2):
                pairs = side[pl.ds(level * 9 + first // 2, count // 2)].astype(F32)
                wide[part, level, pl.ds(to, count), cols, :] = pairs.reshape(count, 8, 128)
                for row in range(count):
                    got = ninth[n, pl.ds(level * 18 + first + row, 1), :]
                    wide[part, level, pl.ds(to + row, 1), nine : nine + 1, :] = got.reshape(1, 1, 128)

    if 0 in parts:
        spread(0, 0, 10, own_ref[...], 0)
    if 1 in parts:
        spread(1, 2 * par, 8, far_ref[...], 10)
        spread(1, 8 * (1 - par), 2, own_ref[:, pl.ds(8 * par, 2)], 8 * par)
    gain = gain_ref[0:1, :]
    half = 1 - par

    cols_of = len(which)

    def slots(part):
        at = parts.index(part) * cols_of
        return at, slice(at, at + cols_of)

    def embed(part):
        first, here = slots(part)
        for n, g in enumerate(which):
            for dj in range(3):
                cols = slice(g * 16 + 7 + dj, g * 16 + 23 + dj)
                got = wide[part, :, :, cols, :].astype(BF)
                gathered[first + n, :, :, :, dj * 128 : dj * 128 + 128] = got
        for n in range(cols_of):
            lhs = jnp.concatenate(
                [gathered[first + n, :, di : di + 8].reshape(256, 384) for di in range(3)], axis=1
            )
            x = mm(lhs, wemb_ref[...]).reshape(2, 8, 16, D)
            for level in range(2):
                x0[first + n, level] = x[level] + lev_ref[level : level + 1, :]

    def norm(part):
        first, here = slots(part)
        for slot in range(first, first + cols_of):
            for u in range(2):
                x = x0[slot, :, :, u * 8 : u * 8 + 8, :].reshape(128, D)
                normed[slot, u] = normalize(x, gain).astype(BF).reshape(2, 4, 16, D)

    def project(part):
        first, here = slots(part)
        n = normed[here].reshape(256 * cols_of, D)
        if leading:
            loads[0].wait()
            loads[1].wait()
        keyval[here] = mm(n, wkv[...]).astype(BF).reshape(cols_of, 2, 128, 1024)
        if part:
            n = normed[here, :, :, pl.ds(half * 2, 2)].reshape(128 * cols_of, D)
        q = (mm(n, wq[...]) * SCALE).astype(BF)
        query[here, :, : 64 if part else 128] = q.reshape(cols_of, 2, -1, D)

    def attention(part):
        first, here = slots(part)
        count = 64 if part else 128
        for slot in range(first, first + cols_of):
            for u in range(2):
                kv = keyval[slot, u]
                heads[slot, u, :count] = attend(query[slot, u, :count], kv[:, :D], kv[:, D:], None)

    def project_out(part):
        first, here = slots(part)
        count = 64 if part else 128
        if leading:
            loads[2].wait()
        out = mm(heads[here, :, :count].reshape(2 * cols_of * count, D), wo[...])
        for n in range(2 * cols_of):
            slot, u = first + n // 2, n % 2
            cols, mine = slice(n * 8, n * 8 + 8), slice(u * 8, u * 8 + 8)
            add = out[n * count : n * count + count].reshape(2, count // 16, 8, D)
            if part:
                x1_refs[-1][:, :, cols, :] = x0[slot, :, pl.ds(4 * half, 4), mine, :] + add
            else:
                for h in range(2):
                    to = pl.ds(4 * (par if h == 0 else half), 4)
                    rows = slice(4 * h, 4 * h + 4)
                    x1_refs[0][:, to, cols, :] = x0[slot, :, rows, mine, :] + add[:, rows]

    pipelined([embed, norm, project, attention, project_out], list(parts))
    if 0 in parts:
        send_ref[...] = x1_refs[0][:, 4:8].astype(BF)


def first_block(parts, which, after, par, patch_arrays, wemb, level_embed, norm_gain, w_query, w_keyval, w_out):
    vmem = pl.BlockSpec(memory_space=pltpu.VMEM)
    width, count = 16 * len(which), len(parts) * len(which)
    leading = parts == (0,) and which == MIDDLE
    outs = [jax.ShapeDtypeStruct((2, 4 if part else 8, width, D), F32) for part in parts]
    if 0 in parts:
        outs.append(jax.ShapeDtypeStruct((2, 4, width, D), BF))
    scratch = [
        pltpu.VMEM((2, 2, 10, 96, 128), F32),
        pltpu.VMEM((2, 48, 128), F32),
        pltpu.VMEM((count, 2, 10, 16, 384), BF),
        pltpu.VMEM((count, 2, 8, 16, D), F32),
        pltpu.VMEM((count, 2, 2, 4, 16, D), BF),
        pltpu.VMEM((count, 2, 128, D), BF),
        pltpu.VMEM((count, 2, 128, 1024), BF),
        pltpu.VMEM((count, 2, 128, D), BF),
    ]
    projections = [w_query, w_keyval, w_out]
    if leading:
        outs.append(jax.ShapeDtypeStruct((2, 10, 64, 128), BF))
        scratch += [
            pltpu.VMEM((10, 96, 128), BF),
            pltpu.VMEM((D, D), BF),
            pltpu.VMEM((D, 1024), BF),
            pltpu.VMEM((D, D), BF),
            pltpu.SemaphoreType.DMA((3,)),
        ]
        projections = [pltpu.with_memory_space_constraint(w, pltpu.HBM) for w in projections]
    else:
        projections = [pltpu.with_memory_space_constraint(w, pltpu.VMEM) for w in projections]
    place_of = pl.BlockSpec(memory_space=pltpu.HBM if leading else pltpu.VMEM)
    return pl.pallas_call(
        functools.partial(first_kernel, parts, which),
        out_shape=tuple(outs),
        in_specs=[pl.BlockSpec(memory_space=pl.ANY), pl.BlockSpec(memory_space=pltpu.SMEM)]
        + [vmem] * (3 + len(patch_arrays)) + [place_of] * 3,
        out_specs=(vmem,) * len(outs),
        scratch_shapes=scratch,
        compiler_params=params(),
        cost_estimate=pl.CostEstimate(flops=10**10, bytes_accessed=10**7, transcendentals=0),
    )(after, par, *patch_arrays, wemb, level_embed, norm_gain, *projections)


SHIFTED = WINS - 1


def second_kernel(
    par_ref, own_mid, outer_mid, own_edge, outer_edge, near_mid_ref, near_edge_ref, gain_ref, mgain_ref,
    wq_ref, wkv_ref, wo_ref, wm_ref,
    out_ref,
    near, x2, normed, query, keyval, heads,
):
    par, pole = par_ref[0], par_ref[1]
    near[:, :, 0:16, :] = near_edge_ref[:, :, 0:16, :].astype(F32)
    near[:, :, 16:64, :] = near_mid_ref[...].astype(F32)
    near[:, :, 64:80, :] = near_edge_ref[:, :, 16:32, :].astype(F32)
    gain = gain_ref[1:2, :]
    upper = iota((8, D), 0) >= 4
    key_row = (iota((1, 256), 1) // 8) % 8
    bias = jnp.where(key_row < 4, F32(-1e30), F32(0)) * pole.astype(F32)

    def block(n, first, last):
        if first < 4 < last:
            return jnp.concatenate([block(n, first, 4), block(n, 4, last)], axis=1)
        if first >= 12:
            return near[:, first - 12 : last - 12, n * 8 : n * 8 + 8, :]
        middle = 2 <= n < 8
        at = n * 8 - (16 if middle else 48 if n >= 8 else 0)
        if first < 4:
            return (outer_mid if middle else outer_edge)[:, first:last, at : at + 8, :]
        return (own_mid if middle else own_edge)[:, first - 4 : last - 4, at : at + 8, :]

    def window(w, first, last):
        return jnp.where(upper, block(w, first, last), block(w + 1, first, last))

    def norm(s):
        for w in range(SHIFTED):
            if s == 0:
                x = window(w, 0, 8)
            else:
                x = jnp.concatenate(
                    [window(w, 8, 12), window(w, 12, 16)], axis=1
                )
            n = normalize(x.reshape(128, D), gain).astype(BF)
            normed[s * SHIFTED + w] = n.reshape(2, 4, 16, D)

    def project(s):
        at = slice(s * SHIFTED, s * SHIFTED + SHIFTED)
        n = normed[at].reshape(SHIFTED * 128, D)
        keyval[at] = mm(n, wkv_ref[1]).astype(BF).reshape(SHIFTED, 128, 1024)
        n = normed[at, :, 2 - 2 * s : 4 - 2 * s].reshape(SHIFTED * 64, D)
        query[at] = (mm(n, wq_ref[1]) * SCALE).astype(BF).reshape(SHIFTED, 64, D)

    def attention(s):
        for t in range(s * SHIFTED, s * SHIFTED + SHIFTED):
            kv = keyval[t]
            heads[t] = attend(query[t], kv[:, :D], kv[:, D:], None if s else bias)

    def project_out(s):
        at = slice(s * SHIFTED, s * SHIFTED + SHIFTED)
        out = mm(heads[at].reshape(SHIFTED * 64, D), wo_ref[1])
        rows = slice(s * 4, s * 4 + 4)
        for w in range(SHIFTED):
            new = window(w, 4 + s * 4, 8 + s * 4)
            new = new + out[w * 64 : w * 64 + 64].reshape(2, 4, 8, D)
            for c in range(4):
                piece = new[..., c * 128 : c * 128 + 128]
                x2[c, :, rows, w * 8 + 4 : w * 8 + 8, :] = piece[:, :, 4:8, :]
                x2[c, :, rows, w * 8 + 8 : w * 8 + 12, :] = piece[:, :, 0:4, :]

    def merge(s):
        parts = []
        for p in range(4):
            got = [
                jnp.concatenate(
                    [
                        x2[c, level, s * 4 + 2 * a + p % 2, pl.ds(8 + p // 2, 32, stride=2), :]
                        for c in range(4)
                    ],
                    axis=1,
                )
                for level in range(2)
                for a in range(2)
            ]
            parts.append(jnp.concatenate(got, axis=0))
        n = normalize(jnp.concatenate(parts, axis=1), mgain_ref[...]).astype(BF)
        out = mm(n, wm_ref[...]).astype(BF)
        out_ref[:, pl.ds(2 * ((par + s) % 2), 2)] = out.reshape(2, 2, 32, 1024)

    pipelined([norm, project, attention, project_out, merge], [0, 1])


def second_block(par, x1_parts, near_mid, near_edge, norm_gain, merge_gain, w_query, w_keyval, w_out, merge_weight):
    vmem = pl.BlockSpec(memory_space=pltpu.VMEM)
    weights = [
        pltpu.with_memory_space_constraint(w, pltpu.VMEM) for w in (w_query, w_keyval, w_out, merge_weight)
    ]
    return pl.pallas_call(
        second_kernel,
        out_shape=jax.ShapeDtypeStruct((2, 4, 32, 1024), BF),
        in_specs=[pl.BlockSpec(memory_space=pltpu.SMEM)] + [vmem] * 12,
        out_specs=vmem,
        scratch_shapes=[
            pltpu.VMEM((2, 4, 80, D), F32),
            pltpu.VMEM((4, 2, 8, 80, 128), F32),
            pltpu.VMEM((2 * SHIFTED, 2, 4, 16, D), BF),
            pltpu.VMEM((2 * SHIFTED, 64, D), BF),
            pltpu.VMEM((2 * SHIFTED, 128, 1024), BF),
            pltpu.VMEM((2 * SHIFTED, 64, D), BF),
        ],
        compiler_params=params(),
        cost_estimate=pl.CostEstimate(flops=10**10, bytes_accessed=10**7, transcendentals=0),
    )(
        par, *x1_parts, near_mid, near_edge, norm_gain, merge_gain, *weights
    )


def embedding_matrix(embed_weight, land_embed):
    w = jnp.pad(embed_weight, ((0, 0), (0, 0), (0, 2), (0, 0))).reshape(3, 4, 3, 4, 8, D)
    w = w.transpose(0, 2, 1, 3, 4, 5)
    share = land_embed / 16
    high = lax.reduce_precision(share, 8, 7)
    at = [lax.broadcasted_iota(jnp.int32, w.shape, d) for d in (0, 1, 4)]
    middle = (at[0] == 1) & (at[1] == 1)
    w = jnp.where(middle & (at[2] == 6), high.astype(BF), w)
    w = jnp.where(middle & (at[2] == 7), (share - high).astype(BF), w)
    return w.reshape(9 * 128, D)


def swap(block, first):
    count = lax.axis_size("lat")
    pairs = []
    for i in range(first, count - 1, 2):
        pairs += [(i, i + 1), (i + 1, i)]
    return lax.ppermute(block, "lat", pairs)


def around(block, distance):
    count = lax.axis_size("lon")
    return lax.ppermute(block, "lon", [(i, (i + distance) % count) for i in range(count)])


def shards(
    atmos, orography, land_sea, embed_weight, level_embed, land_embed, norm_gain,
    w_query, w_keyval, w_out, merge_gain, merge_weight,
):
    lat = lax.axis_index("lat")
    par = lat % 2
    pole = (lat == 0) | (lat == lax.axis_size("lat") - 1)
    place = jnp.stack([par, pole]).astype(jnp.int32)
    own, send, edge, near = patches(place, atmos, orography, land_sea)
    edge = swap(edge, 0)
    near = swap(near, 1)
    send = lax.dynamic_update_slice(send, edge, (7 * (1 - par), 0, 0))
    far = swap(send, 1)
    wemb = embedding_matrix(embed_weight, land_embed)
    weights = wemb, level_embed, norm_gain, w_query, w_keyval, w_out
    own_mid, send_mid, own = first_block((0,), MIDDLE, edge, place, (own, edge, near), *weights)
    near_mid = swap(send_mid, 0)
    far, low, high = unpack_far(own_mid, far, own)
    from_low, from_high = around(high, 1), around(low, -1)
    (outer_mid,) = first_block((1,), MIDDLE, own_mid, place, (own, far), *weights)
    own_edge, send_edge = first_block(
        (0,), EDGES, outer_mid, place, (own, from_low, from_high), *weights
    )
    near_edge = swap(send_edge, 0)
    (outer_edge,) = first_block(
        (1,), EDGES, own_edge, place, (own, far, from_low, from_high), *weights
    )
    return second_block(
        place, (own_mid, outer_mid, own_edge, outer_edge), near_mid, near_edge, norm_gain,
        merge_gain.reshape(1, -1), w_query, w_keyval, w_out, merge_weight,
    )


def solution(mesh):
    in_specs = (P(None, None, "lat", "lon"), P("lat", "lon"), P("lat", "lon")) + (P(),) * 9
    out_specs = P(None, "lat", "lon", None)
    return jax.shard_map(shards, mesh=mesh, in_specs=in_specs, out_specs=out_specs, check_vma=False)
```

```python
import functools
import math

import jax
import jax.numpy as jnp
from jax import lax
from jax.experimental import pallas as pl
from jax.experimental.pallas import tpu as pltpu
from jax.sharding import PartitionSpec as P

BF = jnp.bfloat16
F32 = jnp.float32
D = 512
HEAD_DIM = 64
WINS = 10
SCALE = HEAD_DIM ** (-0.5) * math.log2(math.e)
VMEM_LIMIT = 32 * 1024 * 1024


def iota(shape, dim):
    return lax.broadcasted_iota(jnp.int32, shape, dim)


def one_hot(cond):
    return jnp.where(cond, 1.0, 0.0).astype(BF)


def mm(a, b):
    return jnp.dot(a, b, preferred_element_type=F32)


def mm_t(a, b):
    return lax.dot_general(a, b, (((1,), (1,)), ((), ())), preferred_element_type=F32)


def params():
    return pltpu.CompilerParams(vmem_limit_bytes=VMEM_LIMIT)


def patch_kernel(
    par_ref, atmos_any, oro_any, land_any, own_ref, send_ref, edge_ref, near_ref,
    atmos_ref, oro_ref, land_ref, sems,
):
    par = par_ref[0]
    loads = [
        pltpu.make_async_copy(src, dst, sems.at[n])
        for n, (src, dst) in enumerate(
            [(atmos_any, atmos_ref), (oro_any, oro_ref), (land_any, land_ref)]
        )
    ]
    for load in loads:
        load.start()
    row, src = iota((1024, 1), 0), iota((1024, 384), 1)
    i, r, ch = row >> 7, (row >> 5) & 3, row & 7
    channel = jnp.where(ch < 5, ch, jnp.where(ch == 5, 10, jnp.where(ch == 6, 11, 9)))
    pick_main = one_hot(src == channel * 32 + i * 4 + r)
    pick_aux = one_hot(src == (5 + (row & 3)) * 32 + i * 4 + r)
    for load in loads:
        load.wait()
    cells = jnp.concatenate(
        [
            atmos_ref[...].reshape(320, 256),
            oro_ref[...],
            land_ref[...].astype(F32).astype(BF),
        ],
        axis=0,
    )
    main, aux = mm(pick_main, cells), mm(pick_aux, cells)
    col = iota((1, 256), 1)
    c, half = (row >> 3) & 3, (row >> 2) & 1
    main = jnp.where((col & 3) == c, main, 0.0).astype(BF)
    aux = jnp.where((col & 3) + 4 * (col >> 7) == c + 4 * half, aux, 0.0).astype(BF)
    j, col = iota((64, 256), 0), iota((64, 256), 1)
    main = mm_t(one_hot((col >> 2) == j), main).astype(BF)
    j, col = iota((32, 256), 0), iota((32, 256), 1)
    aux = mm_t(one_hot(((col & 127) >> 2) == j), aux).astype(BF)
    for i in range(8):
        own_ref[i, 0:64, :] = main[:, i * 128 : i * 128 + 128]
        own_ref[i, 64:96, :] = aux[:, i * 128 : i * 128 + 128]
    send_ref[pl.ds(par, 7)] = own_ref[pl.ds(1 - par, 7)]
    edge_ref[...] = own_ref[pl.ds(7 * (1 - par), 1)]
    near_ref[...] = own_ref[pl.ds(7 * par, 1)]


def patches(par, atmos, orography, land_sea):
    cells = [pltpu.with_memory_space_constraint(a, pltpu.HBM) for a in (atmos, orography, land_sea)]
    return pl.pallas_call(
        patch_kernel,
        out_shape=tuple(jax.ShapeDtypeStruct((n, 96, 128), BF) for n in (8, 8, 1, 1)),
        in_specs=[pl.BlockSpec(memory_space=pltpu.SMEM)] + [pl.BlockSpec(memory_space=pltpu.HBM)] * 3,
        out_specs=(pl.BlockSpec(memory_space=pltpu.VMEM),) * 4,
        scratch_shapes=[
            pltpu.VMEM(atmos.shape, BF),
            pltpu.VMEM(orography.shape, BF),
            pltpu.VMEM(land_sea.shape, jnp.int32),
            pltpu.SemaphoreType.DMA((3,)),
        ],
        compiler_params=params(),
        cost_estimate=pl.CostEstimate(flops=10**9, bytes_accessed=10**6, transcendentals=0),
    )(par, *cells)


def unpack_rows(packed, out_ref):
    rows = packed.shape[0]
    k, n = iota((256, 256), 0), iota((256, 256), 1)
    ch, lane = n % 8, n % 128
    from_main0 = jnp.where(ch == 7, lane - 1, lane)
    from_main1 = jnp.where(ch == 7, lane - 1, jnp.where(ch == 4, lane + 3, lane))
    aux = packed[:, 64:96, :]
    for half in range(2):
        from_one = jnp.where(ch < 4, 128 + lane + 4 * half, from_main1)
        pick = one_hot(k == jnp.where(n < 128, from_main0, from_one))
        both = jnp.concatenate([packed[:, half * 32 : half * 32 + 32, :], aux], axis=2)
        got = mm(both.reshape(rows * 32, 256), pick).astype(BF).reshape(rows, 32, 256)
        for level in range(2):
            tile = got[:, :, level * 128 : level * 128 + 128]
            out_ref[level, :, half * 32 : half * 32 + 32, :] = tile


def unpack_far_kernel(after_ref, packed_ref, own_ref, far_ref, low_ref, high_ref, ninth):
    del after_ref
    unpack_rows(packed_ref, far_ref)
    for n, (first, inner, out_ref) in enumerate([(0, 8, low_ref), (48, 7, high_ref)]):
        cols = slice(first, first + 16)
        edge = jnp.concatenate([own_ref[:, :, cols, :], far_ref[:, :, cols, :]], axis=1).astype(F32)
        near = edge[:, :, 8 * n : 8 * n + 8, :]
        out_ref[0:18] = near.reshape(18, 16, 128).astype(BF)
        for level in range(2):
            for row in range(18):
                at = level * 18 + row
                ninth[n, at : at + 1, :] = edge[level, row, inner : inner + 1, :]
        ninth[n, 36:48, :] = jnp.zeros((12, 128), F32)
        out_ref[18:21] = ninth[n].reshape(3, 16, 128).astype(BF)


def unpack_far(after, packed, own):
    vmem = pl.BlockSpec(memory_space=pltpu.VMEM)
    return pl.pallas_call(
        unpack_far_kernel,
        out_shape=(
            jax.ShapeDtypeStruct((2, 8, 64, 128), BF),
            jax.ShapeDtypeStruct((21, 16, 128), BF),
            jax.ShapeDtypeStruct((21, 16, 128), BF),
        ),
        in_specs=[pl.BlockSpec(memory_space=pl.ANY)] + [vmem] * 2,
        out_specs=(vmem,) * 3,
        scratch_shapes=[pltpu.VMEM((2, 48, 128), F32)],
        compiler_params=params(),
        cost_estimate=pl.CostEstimate(flops=10**9, bytes_accessed=10**6, transcendentals=0),
    )(after, packed, own)


def pipelined(stages, groups):
    for step in range(len(groups) + len(stages) - 1):
        for k in range(len(stages)):
            if 0 <= step - k < len(groups):
                stages[k](groups[step - k])


def normalize(x, gain):
    mean = jnp.mean(x, axis=-1, keepdims=True)
    x = x - mean
    var = jnp.mean(x * x, axis=-1, keepdims=True)
    return x * lax.rsqrt(var + 1e-05) * gain


def attend(q, k, v, bias):
    left = iota((128, 128), 1) < HEAD_DIM
    ones_left, ones_right, ones = one_hot(left), one_hot(~left), jnp.ones((128, 128), BF)
    zero = jnp.zeros((128, 128), BF)
    n = q.shape[0]
    out = []
    for pair in range(4):
        at = slice(pair * 128, pair * 128 + 128)
        kp, vp = k[:, at], v[:, at]
        keys = jnp.concatenate([jnp.where(left, kp, zero), jnp.where(left, zero, kp)], axis=0)
        s = mm_t(q[:, at], keys)
        if bias is not None:
            s = s + bias
        s0, s1 = s[:, :128], s[:, 128:]
        p0 = jnp.exp2(s0 - jnp.max(s0, axis=-1, keepdims=True))
        p1 = jnp.exp2(s1 - jnp.max(s1, axis=-1, keepdims=True))
        if n == 64:
            p = jnp.concatenate([p0.astype(BF), p1.astype(BF)], axis=0)
            o = mm(p, jnp.concatenate([vp, ones], axis=1))
            values = jnp.where(left[:n], o[:n, :128], o[n:, :128])
            total = jnp.where(left[:n], o[:n, 128:], o[n:, 128:])
            out.append((values / total).astype(BF))
            continue
        p = jnp.concatenate([p0, p1], axis=1).astype(BF)
        vals = jnp.concatenate(
            [
                jnp.concatenate([jnp.where(left, vp, zero), ones_left], axis=1),
                jnp.concatenate([jnp.where(left, zero, vp), ones_right], axis=1),
            ],
            axis=0,
        )
        o = mm(p, vals)
        out.append((o[:, :128] / o[:, 128:]).astype(BF))
    return jnp.concatenate(out, axis=1)


MIDDLE, EDGES = (1, 2, 3), (0, 4)


def first_kernel(parts, which, after_ref, *refs):
    del after_ref
    par_ref, refs = refs[0], refs[1:]
    leading = parts == (0,) and which == MIDDLE
    if leading:
        own_packed, edge_ref, near_ref, refs = refs[0], refs[1], refs[2], refs[3:]
    else:
        own_ref, refs = refs[0], refs[1:]
    if 1 in parts:
        far_ref, refs = refs[0], refs[1:]
    if which == EDGES:
        low_ref, high_ref, refs = refs[0], refs[1], refs[2:]
    wemb_ref, lev_ref, gain_ref, wq_ref, wkv_ref, wo_ref, *refs = refs
    x1_refs, refs = refs[: len(parts)], refs[len(parts) :]
    if 0 in parts:
        send_ref, refs = refs[0], refs[1:]
    if leading:
        own_ref, refs = refs[0], refs[1:]
    wide, ninth, gathered, x0, normed, query, keyval, heads, *refs = refs
    par = par_ref[0]
    if leading:
        packed, wq, wkv, wo, sems = refs
        loads = [
            pltpu.make_async_copy(src.at[0], dst, sems.at[n])
            for n, (src, dst) in enumerate([(wkv_ref, wkv), (wq_ref, wq), (wo_ref, wo)])
        ]
        for load in loads:
            load.start()
        packed[1:9] = own_packed[...]
        packed[pl.ds(9 * par, 1)] = near_ref[...]
        packed[pl.ds(9 * (1 - par), 1)] = edge_ref[...]
        unpack_rows(packed, own_ref)
    else:
        wq, wkv, wo = wq_ref.at[0], wkv_ref.at[0], wo_ref.at[0]

    if which == EDGES:
        for n, side in enumerate((low_ref, high_ref)):
            ninth[n] = side[18:21].astype(F32).reshape(48, 128)

    def spread(part, to, count, center, first):
        rows = (slice(None), pl.ds(to, count))
        if which != EDGES:
            wide[part, *rows, 16:80, :] = center.astype(F32)
            return
        wide[part, *rows, 16:32, :] = center[:, :, 0:16, :].astype(F32)
        wide[part, *rows, 64:80, :] = center[:, :, 48:64, :].astype(F32)
        for n, (side, cols, nine) in enumerate([(low_ref, slice(8, 16), 7), (high_ref, slice(80, 88), 88)]):
            for level in range(2):
                pairs = side[pl.ds(level * 9 + first // 2, count // 2)].astype(F32)
                wide[part, level, pl.ds(to, count), cols, :] = pairs.reshape(count, 8, 128)
                for row in range(count):
                    got = ninth[n, pl.ds(level * 18 + first + row, 1), :]
                    wide[part, level, pl.ds(to + row, 1), nine : nine + 1, :] = got.reshape(1, 1, 128)

    if 0 in parts:
        spread(0, 0, 10, own_ref[...], 0)
    if 1 in parts:
        spread(1, 2 * par, 8, far_ref[...], 10)
        spread(1, 8 * (1 - par), 2, own_ref[:, pl.ds(8 * par, 2)], 8 * par)
    gain = gain_ref[0:1, :]
    half = 1 - par

    cols_of = len(which)

    def slots(part):
        at = parts.index(part) * cols_of
        return at, slice(at, at + cols_of)

    def embed(part):
        first, here = slots(part)
        for n, g in enumerate(which):
            for dj in range(3):
                cols = slice(g * 16 + 7 + dj, g * 16 + 23 + dj)
                got = wide[part, :, :, cols, :].astype(BF)
                gathered[first + n, :, :, :, dj * 128 : dj * 128 + 128] = got
        for n in range(cols_of):
            lhs = jnp.concatenate(
                [gathered[first + n, :, di : di + 8].reshape(256, 384) for di in range(3)], axis=1
            )
            x = mm(lhs, wemb_ref[...]).reshape(2, 8, 16, D)
            for level in range(2):
                x0[first + n, level] = x[level] + lev_ref[level : level + 1, :]

    def norm(part):
        first, here = slots(part)
        for slot in range(first, first + cols_of):
            for u in range(2):
                x = x0[slot, :, :, u * 8 : u * 8 + 8, :].reshape(128, D)
                normed[slot, u] = normalize(x, gain).astype(BF).reshape(2, 4, 16, D)

    def project(part):
        first, here = slots(part)
        n = normed[here].reshape(256 * cols_of, D)
        if leading:
            loads[0].wait()
            loads[1].wait()
        keyval[here] = mm(n, wkv[...]).astype(BF).reshape(cols_of, 2, 128, 1024)
        if part:
            n = normed[here, :, :, pl.ds(half * 2, 2)].reshape(128 * cols_of, D)
        q = (mm(n, wq[...]) * SCALE).astype(BF)
        query[here, :, : 64 if part else 128] = q.reshape(cols_of, 2, -1, D)

    def attention(part):
        first, here = slots(part)
        count = 64 if part else 128
        for slot in range(first, first + cols_of):
            for u in range(2):
                kv = keyval[slot, u]
                heads[slot, u, :count] = attend(query[slot, u, :count], kv[:, :D], kv[:, D:], None)

    def project_out(part):
        first, here = slots(part)
        count = 64 if part else 128
        if leading:
            loads[2].wait()
        out = mm(heads[here, :, :count].reshape(2 * cols_of * count, D), wo[...])
        for n in range(2 * cols_of):
            slot, u = first + n // 2, n % 2
            cols, mine = slice(n * 8, n * 8 + 8), slice(u * 8, u * 8 + 8)
            add = out[n * count : n * count + count].reshape(2, count // 16, 8, D)
            if part:
                x1_refs[-1][:, :, cols, :] = x0[slot, :, pl.ds(4 * half, 4), mine, :] + add
            else:
                for h in range(2):
                    to = pl.ds(4 * (par if h == 0 else half), 4)
                    rows = slice(4 * h, 4 * h + 4)
                    x1_refs[0][:, to, cols, :] = x0[slot, :, rows, mine, :] + add[:, rows]

    pipelined([embed, norm, project, attention, project_out], list(parts))
    if 0 in parts:
        send_ref[...] = x1_refs[0][:, 4:8].astype(BF)


def first_block(parts, which, after, par, patch_arrays, wemb, level_embed, norm_gain, w_query, w_keyval, w_out):
    vmem = pl.BlockSpec(memory_space=pltpu.VMEM)
    width, count = 16 * len(which), len(parts) * len(which)
    leading = parts == (0,) and which == MIDDLE
    outs = [jax.ShapeDtypeStruct((2, 4 if part else 8, width, D), F32) for part in parts]
    if 0 in parts:
        outs.append(jax.ShapeDtypeStruct((2, 4, width, D), BF))
    scratch = [
        pltpu.VMEM((2, 2, 10, 96, 128), F32),
        pltpu.VMEM((2, 48, 128), F32),
        pltpu.VMEM((count, 2, 10, 16, 384), BF),
        pltpu.VMEM((count, 2, 8, 16, D), F32),
        pltpu.VMEM((count, 2, 2, 4, 16, D), BF),
        pltpu.VMEM((count, 2, 128, D), BF),
        pltpu.VMEM((count, 2, 128, 1024), BF),
        pltpu.VMEM((count, 2, 128, D), BF),
    ]
    projections = [w_query, w_keyval, w_out]
    if leading:
        outs.append(jax.ShapeDtypeStruct((2, 10, 64, 128), BF))
        scratch += [
            pltpu.VMEM((10, 96, 128), BF),
            pltpu.VMEM((D, D), BF),
            pltpu.VMEM((D, 1024), BF),
            pltpu.VMEM((D, D), BF),
            pltpu.SemaphoreType.DMA((3,)),
        ]
        projections = [pltpu.with_memory_space_constraint(w, pltpu.HBM) for w in projections]
    else:
        projections = [pltpu.with_memory_space_constraint(w, pltpu.VMEM) for w in projections]
    place_of = pl.BlockSpec(memory_space=pltpu.HBM if leading else pltpu.VMEM)
    return pl.pallas_call(
        functools.partial(first_kernel, parts, which),
        out_shape=tuple(outs),
        in_specs=[pl.BlockSpec(memory_space=pl.ANY), pl.BlockSpec(memory_space=pltpu.SMEM)]
        + [vmem] * (3 + len(patch_arrays)) + [place_of] * 3,
        out_specs=(vmem,) * len(outs),
        scratch_shapes=scratch,
        compiler_params=params(),
        cost_estimate=pl.CostEstimate(flops=10**10, bytes_accessed=10**7, transcendentals=0),
    )(after, par, *patch_arrays, wemb, level_embed, norm_gain, *projections)


SHIFTED = WINS - 1


def second_kernel(
    par_ref, own_mid, outer_mid, own_edge, outer_edge, near_mid_ref, near_edge_ref, gain_ref, mgain_ref,
    wq_ref, wkv_ref, wo_ref, wm_ref,
    out_ref,
    near, x2, normed, query, keyval, heads,
):
    par, pole = par_ref[0], par_ref[1]
    near[:, :, 0:16, :] = near_edge_ref[:, :, 0:16, :].astype(F32)
    near[:, :, 16:64, :] = near_mid_ref[...].astype(F32)
    near[:, :, 64:80, :] = near_edge_ref[:, :, 16:32, :].astype(F32)
    gain = gain_ref[1:2, :]
    upper = iota((8, D), 0) >= 4
    key_row = (iota((1, 256), 1) // 8) % 8
    bias = jnp.where(key_row < 4, F32(-1e30), F32(0)) * pole.astype(F32)

    def block(n, first, last):
        if first < 4 < last:
            return jnp.concatenate([block(n, first, 4), block(n, 4, last)], axis=1)
        if first >= 12:
            return near[:, first - 12 : last - 12, n * 8 : n * 8 + 8, :]
        middle = 2 <= n < 8
        at = n * 8 - (16 if middle else 48 if n >= 8 else 0)
        if first < 4:
            return (outer_mid if middle else outer_edge)[:, first:last, at : at + 8, :]
        return (own_mid if middle else own_edge)[:, first - 4 : last - 4, at : at + 8, :]

    def window(w, first, last):
        return jnp.where(upper, block(w, first, last), block(w + 1, first, last))

    def norm(s):
        for w in range(SHIFTED):
            if s == 0:
                x = window(w, 0, 8)
            else:
                x = jnp.concatenate(
                    [window(w, 8, 12), window(w, 12, 16)], axis=1
                )
            n = normalize(x.reshape(128, D), gain).astype(BF)
            normed[s * SHIFTED + w] = n.reshape(2, 4, 16, D)

    def project(s):
        at = slice(s * SHIFTED, s * SHIFTED + SHIFTED)
        n = normed[at].reshape(SHIFTED * 128, D)
        keyval[at] = mm(n, wkv_ref[1]).astype(BF).reshape(SHIFTED, 128, 1024)
        n = normed[at, :, 2 - 2 * s : 4 - 2 * s].reshape(SHIFTED * 64, D)
        query[at] = (mm(n, wq_ref[1]) * SCALE).astype(BF).reshape(SHIFTED, 64, D)

    def attention(s):
        for t in range(s * SHIFTED, s * SHIFTED + SHIFTED):
            kv = keyval[t]
            heads[t] = attend(query[t], kv[:, :D], kv[:, D:], None if s else bias)

    def project_out(s):
        at = slice(s * SHIFTED, s * SHIFTED + SHIFTED)
        out = mm(heads[at].reshape(SHIFTED * 64, D), wo_ref[1])
        rows = slice(s * 4, s * 4 + 4)
        for w in range(SHIFTED):
            new = window(w, 4 + s * 4, 8 + s * 4)
            new = new + out[w * 64 : w * 64 + 64].reshape(2, 4, 8, D)
            for c in range(4):
                piece = new[..., c * 128 : c * 128 + 128]
                x2[c, :, rows, w * 8 + 4 : w * 8 + 8, :] = piece[:, :, 4:8, :]
                x2[c, :, rows, w * 8 + 8 : w * 8 + 12, :] = piece[:, :, 0:4, :]

    def merge(s):
        parts = []
        for p in range(4):
            got = [
                jnp.concatenate(
                    [
                        x2[c, level, s * 4 + 2 * a + p % 2, pl.ds(8 + p // 2, 32, stride=2), :]
                        for c in range(4)
                    ],
                    axis=1,
                )
                for level in range(2)
                for a in range(2)
            ]
            parts.append(jnp.concatenate(got, axis=0))
        n = normalize(jnp.concatenate(parts, axis=1), mgain_ref[...]).astype(BF)
        out = mm(n, wm_ref[...]).astype(BF)
        out_ref[:, pl.ds(2 * ((par + s) % 2), 2)] = out.reshape(2, 2, 32, 1024)

    pipelined([norm, project, attention, project_out, merge], [0, 1])


def second_block(par, x1_parts, near_mid, near_edge, norm_gain, merge_gain, w_query, w_keyval, w_out, merge_weight):
    vmem = pl.BlockSpec(memory_space=pltpu.VMEM)
    weights = [
        pltpu.with_memory_space_constraint(w, pltpu.VMEM) for w in (w_query, w_keyval, w_out, merge_weight)
    ]
    return pl.pallas_call(
        second_kernel,
        out_shape=jax.ShapeDtypeStruct((2, 4, 32, 1024), BF),
        in_specs=[pl.BlockSpec(memory_space=pltpu.SMEM)] + [vmem] * 12,
        out_specs=vmem,
        scratch_shapes=[
            pltpu.VMEM((2, 4, 80, D), F32),
            pltpu.VMEM((4, 2, 8, 80, 128), F32),
            pltpu.VMEM((2 * SHIFTED, 2, 4, 16, D), BF),
            pltpu.VMEM((2 * SHIFTED, 64, D), BF),
            pltpu.VMEM((2 * SHIFTED, 128, 1024), BF),
            pltpu.VMEM((2 * SHIFTED, 64, D), BF),
        ],
        compiler_params=params(),
        cost_estimate=pl.CostEstimate(flops=10**10, bytes_accessed=10**7, transcendentals=0),
    )(
        par, *x1_parts, near_mid, near_edge, norm_gain, merge_gain, *weights
    )


def embedding_matrix(embed_weight, land_embed):
    w = jnp.pad(embed_weight, ((0, 0), (0, 0), (0, 2), (0, 0))).reshape(3, 4, 3, 4, 8, D)
    w = w.transpose(0, 2, 1, 3, 4, 5)
    share = land_embed / 16
    high = lax.reduce_precision(share, 8, 7)
    at = [lax.broadcasted_iota(jnp.int32, w.shape, d) for d in (0, 1, 4)]
    middle = (at[0] == 1) & (at[1] == 1)
    w = jnp.where(middle & (at[2] == 6), high.astype(BF), w)
    w = jnp.where(middle & (at[2] == 7), (share - high).astype(BF), w)
    return w.reshape(9 * 128, D)


def swap(block, first):
    count = lax.axis_size("lat")
    pairs = []
    for i in range(first, count - 1, 2):
        pairs += [(i, i + 1), (i + 1, i)]
    return lax.ppermute(block, "lat", pairs)


def around(block, distance):
    count = lax.axis_size("lon")
    return lax.ppermute(block, "lon", [(i, (i + distance) % count) for i in range(count)])


def shards(
    atmos, orography, land_sea, embed_weight, level_embed, land_embed, norm_gain,
    w_query, w_keyval, w_out, merge_gain, merge_weight,
):
    lat = lax.axis_index("lat")
    par = lat % 2
    pole = (lat == 0) | (lat == lax.axis_size("lat") - 1)
    place = jnp.stack([par, pole]).astype(jnp.int32)
    own, send, edge, near = patches(place, atmos, orography, land_sea)
    edge = swap(edge, 0)
    near = swap(near, 1)
    send = lax.dynamic_update_slice(send, edge, (7 * (1 - par), 0, 0))
    far = swap(send, 1)
    wemb = embedding_matrix(embed_weight, land_embed)
    weights = wemb, level_embed, norm_gain, w_query, w_keyval, w_out
    own_mid, send_mid, own = first_block((0,), MIDDLE, edge, place, (own, edge, near), *weights)
    near_mid = swap(send_mid, 0)
    far, low, high = unpack_far(own_mid, far, own)
    from_low, from_high = around(high, 1), around(low, -1)
    (outer_mid,) = first_block((1,), MIDDLE, own_mid, place, (own, far), *weights)
    own_edge, send_edge = first_block(
        (0,), EDGES, outer_mid, place, (own, from_low, from_high), *weights
    )
    near_edge = swap(send_edge, 0)
    (outer_edge,) = first_block(
        (1,), EDGES, own_edge, place, (own, far, from_low, from_high), *weights
    )
    return second_block(
        place, (own_mid, outer_mid, own_edge, outer_edge), near_mid, near_edge, norm_gain,
        merge_gain.reshape(1, -1), w_query, w_keyval, w_out, merge_weight,
    )


def solution(mesh):
    in_specs = (P(None, None, "lat", "lon"), P("lat", "lon"), P("lat", "lon")) + (P(),) * 9
    out_specs = P(None, "lat", "lon", None)
    return jax.shard_map(shards, mesh=mesh, in_specs=in_specs, out_specs=out_specs, check_vma=False)
```

```python
import functools
import math

import jax
import jax.numpy as jnp
from jax import lax
from jax.experimental import pallas as pl
from jax.experimental.pallas import tpu as pltpu
from jax.sharding import PartitionSpec as P

BF = jnp.bfloat16
F32 = jnp.float32
D = 512
HEAD_DIM = 64
WINS = 10
SCALE = HEAD_DIM ** (-0.5) * math.log2(math.e)
VMEM_LIMIT = 32 * 1024 * 1024


def iota(shape, dim):
    return lax.broadcasted_iota(jnp.int32, shape, dim)


def one_hot(cond):
    return jnp.where(cond, 1.0, 0.0).astype(BF)


def mm(a, b):
    return jnp.dot(a, b, preferred_element_type=F32)


def mm_t(a, b):
    return lax.dot_general(a, b, (((1,), (1,)), ((), ())), preferred_element_type=F32)


def params():
    return pltpu.CompilerParams(vmem_limit_bytes=VMEM_LIMIT)


def patch_kernel(
    par_ref, atmos_any, oro_any, land_any, own_ref, send_ref, edge_ref, near_ref,
    atmos_ref, oro_ref, land_ref, sems,
):
    par = par_ref[0]
    loads = [
        pltpu.make_async_copy(src, dst, sems.at[n])
        for n, (src, dst) in enumerate(
            [(atmos_any, atmos_ref), (oro_any, oro_ref), (land_any, land_ref)]
        )
    ]
    for load in loads:
        load.start()
    row, src = iota((1024, 1), 0), iota((1024, 384), 1)
    i, r, ch = row >> 7, (row >> 5) & 3, row & 7
    channel = jnp.where(ch < 5, ch, jnp.where(ch == 5, 10, jnp.where(ch == 6, 11, 9)))
    pick_main = one_hot(src == channel * 32 + i * 4 + r)
    pick_aux = one_hot(src == (5 + (row & 3)) * 32 + i * 4 + r)
    for load in loads:
        load.wait()
    cells = jnp.concatenate(
        [
            atmos_ref[...].reshape(320, 256),
            oro_ref[...],
            land_ref[...].astype(F32).astype(BF),
        ],
        axis=0,
    )
    main, aux = mm(pick_main, cells), mm(pick_aux, cells)
    col = iota((1, 256), 1)
    c, half = (row >> 3) & 3, (row >> 2) & 1
    main = jnp.where((col & 3) == c, main, 0.0).astype(BF)
    aux = jnp.where((col & 3) + 4 * (col >> 7) == c + 4 * half, aux, 0.0).astype(BF)
    j, col = iota((64, 256), 0), iota((64, 256), 1)
    main = mm_t(one_hot((col >> 2) == j), main).astype(BF)
    j, col = iota((32, 256), 0), iota((32, 256), 1)
    aux = mm_t(one_hot(((col & 127) >> 2) == j), aux).astype(BF)
    for i in range(8):
        own_ref[i, 0:64, :] = main[:, i * 128 : i * 128 + 128]
        own_ref[i, 64:96, :] = aux[:, i * 128 : i * 128 + 128]
    send_ref[pl.ds(par, 7)] = own_ref[pl.ds(1 - par, 7)]
    edge_ref[...] = own_ref[pl.ds(7 * (1 - par), 1)]
    near_ref[...] = own_ref[pl.ds(7 * par, 1)]


def patches(par, atmos, orography, land_sea):
    cells = [pltpu.with_memory_space_constraint(a, pltpu.HBM) for a in (atmos, orography, land_sea)]
    return pl.pallas_call(
        patch_kernel,
        out_shape=tuple(jax.ShapeDtypeStruct((n, 96, 128), BF) for n in (8, 8, 1, 1)),
        in_specs=[pl.BlockSpec(memory_space=pltpu.SMEM)] + [pl.BlockSpec(memory_space=pltpu.HBM)] * 3,
        out_specs=(pl.BlockSpec(memory_space=pltpu.VMEM),) * 4,
        scratch_shapes=[
            pltpu.VMEM(atmos.shape, BF),
            pltpu.VMEM(orography.shape, BF),
            pltpu.VMEM(land_sea.shape, jnp.int32),
            pltpu.SemaphoreType.DMA((3,)),
        ],
        compiler_params=params(),
        cost_estimate=pl.CostEstimate(flops=10**9, bytes_accessed=10**6, transcendentals=0),
    )(par, *cells)


def unpack_rows(packed, out_ref):
    rows = packed.shape[0]
    k, n = iota((256, 256), 0), iota((256, 256), 1)
    ch, lane = n % 8, n % 128
    from_main0 = jnp.where(ch == 7, lane - 1, lane)
    from_main1 = jnp.where(ch == 7, lane - 1, jnp.where(ch == 4, lane + 3, lane))
    aux = packed[:, 64:96, :]
    for half in range(2):
        from_one = jnp.where(ch < 4, 128 + lane + 4 * half, from_main1)
        pick = one_hot(k == jnp.where(n < 128, from_main0, from_one))
        both = jnp.concatenate([packed[:, half * 32 : half * 32 + 32, :], aux], axis=2)
        got = mm(both.reshape(rows * 32, 256), pick).astype(BF).reshape(rows, 32, 256)
        for level in range(2):
            tile = got[:, :, level * 128 : level * 128 + 128]
            out_ref[level, :, half * 32 : half * 32 + 32, :] = tile


def unpack_far_kernel(after_ref, packed_ref, own_ref, far_ref, low_ref, high_ref, ninth):
    del after_ref
    unpack_rows(packed_ref, far_ref)
    for n, (first, inner, out_ref) in enumerate([(0, 8, low_ref), (48, 7, high_ref)]):
        cols = slice(first, first + 16)
        edge = jnp.concatenate([own_ref[:, :, cols, :], far_ref[:, :, cols, :]], axis=1).astype(F32)
        near = edge[:, :, 8 * n : 8 * n + 8, :]
        out_ref[0:18] = near.reshape(18, 16, 128).astype(BF)
        for level in range(2):
            for row in range(18):
                at = level * 18 + row
                ninth[n, at : at + 1, :] = edge[level, row, inner : inner + 1, :]
        ninth[n, 36:48, :] = jnp.zeros((12, 128), F32)
        out_ref[18:21] = ninth[n].reshape(3, 16, 128).astype(BF)


def unpack_far(after, packed, own):
    vmem = pl.BlockSpec(memory_space=pltpu.VMEM)
    return pl.pallas_call(
        unpack_far_kernel,
        out_shape=(
            jax.ShapeDtypeStruct((2, 8, 64, 128), BF),
            jax.ShapeDtypeStruct((21, 16, 128), BF),
            jax.ShapeDtypeStruct((21, 16, 128), BF),
        ),
        in_specs=[pl.BlockSpec(memory_space=pl.ANY)] + [vmem] * 2,
        out_specs=(vmem,) * 3,
        scratch_shapes=[pltpu.VMEM((2, 48, 128), F32)],
        compiler_params=params(),
        cost_estimate=pl.CostEstimate(flops=10**9, bytes_accessed=10**6, transcendentals=0),
    )(after, packed, own)


def pipelined(stages, groups):
    for step in range(len(groups) + len(stages) - 1):
        for k in range(len(stages)):
            if 0 <= step - k < len(groups):
                stages[k](groups[step - k])


def normalize(x, gain):
    mean = jnp.mean(x, axis=-1, keepdims=True)
    x = x - mean
    var = jnp.mean(x * x, axis=-1, keepdims=True)
    return x * lax.rsqrt(var + 1e-05) * gain


def attend(q, k, v, bias):
    left = iota((128, 128), 1) < HEAD_DIM
    ones_left, ones_right, ones = one_hot(left), one_hot(~left), jnp.ones((128, 128), BF)
    zero = jnp.zeros((128, 128), BF)
    n = q.shape[0]
    out = []
    for pair in range(4):
        at = slice(pair * 128, pair * 128 + 128)
        kp, vp = k[:, at], v[:, at]
        keys = jnp.concatenate([jnp.where(left, kp, zero), jnp.where(left, zero, kp)], axis=0)
        s = mm_t(q[:, at], keys)
        if bias is not None:
            s = s + bias
        s0, s1 = s[:, :128], s[:, 128:]
        p0 = jnp.exp2(s0 - jnp.max(s0, axis=-1, keepdims=True))
        p1 = jnp.exp2(s1 - jnp.max(s1, axis=-1, keepdims=True))
        if n == 64:
            p = jnp.concatenate([p0.astype(BF), p1.astype(BF)], axis=0)
            o = mm(p, jnp.concatenate([vp, ones], axis=1))
            values = jnp.where(left[:n], o[:n, :128], o[n:, :128])
            total = jnp.where(left[:n], o[:n, 128:], o[n:, 128:])
            out.append((values / total).astype(BF))
            continue
        p = jnp.concatenate([p0, p1], axis=1).astype(BF)
        vals = jnp.concatenate(
            [
                jnp.concatenate([jnp.where(left, vp, zero), ones_left], axis=1),
                jnp.concatenate([jnp.where(left, zero, vp), ones_right], axis=1),
            ],
            axis=0,
        )
        o = mm(p, vals)
        out.append((o[:, :128] / o[:, 128:]).astype(BF))
    return jnp.concatenate(out, axis=1)


MIDDLE, EDGES = (1, 2, 3), (0, 4)


def first_kernel(parts, which, after_ref, *refs):
    del after_ref
    par_ref, refs = refs[0], refs[1:]
    leading = parts == (0,) and which == MIDDLE
    if leading:
        own_packed, edge_ref, near_ref, refs = refs[0], refs[1], refs[2], refs[3:]
    else:
        own_ref, refs = refs[0], refs[1:]
    if 1 in parts:
        far_ref, refs = refs[0], refs[1:]
    if which == EDGES:
        low_ref, high_ref, refs = refs[0], refs[1], refs[2:]
        if 0 in parts:
            middle_ref, refs = refs[0], refs[1:]
    wemb_ref, lev_ref, gain_ref, wq_ref, wkv_ref, wo_ref, *refs = refs
    x1_refs, refs = refs[: len(parts)], refs[len(parts) :]
    if 0 in parts:
        send_ref, refs = refs[0], refs[1:]
    if leading:
        own_ref, refs = refs[0], refs[1:]
    wide, ninth, gathered, x0, normed, query, keyval, heads, *refs = refs
    par = par_ref[0]
    if leading:
        packed, wq, wkv, wo, sems = refs
        loads = [
            pltpu.make_async_copy(src.at[0], dst, sems.at[n])
            for n, (src, dst) in enumerate([(wkv_ref, wkv), (wq_ref, wq), (wo_ref, wo)])
        ]
        for load in loads:
            load.start()
        packed[1:9] = own_packed[...]
        packed[pl.ds(9 * par, 1)] = near_ref[...]
        packed[pl.ds(9 * (1 - par), 1)] = edge_ref[...]
        unpack_rows(packed, own_ref)
    else:
        wq, wkv, wo = wq_ref.at[0], wkv_ref.at[0], wo_ref.at[0]

    if which == EDGES:
        for n, side in enumerate((low_ref, high_ref)):
            ninth[n] = side[18:21].astype(F32).reshape(48, 128)

    def spread(part, to, count, center, first):
        rows = (slice(None), pl.ds(to, count))
        if which != EDGES:
            wide[part, *rows, 16:80, :] = center.astype(F32)
            return
        wide[part, *rows, 16:32, :] = center[:, :, 0:16, :].astype(F32)
        wide[part, *rows, 64:80, :] = center[:, :, 48:64, :].astype(F32)
        for n, (side, cols, nine) in enumerate([(low_ref, slice(8, 16), 7), (high_ref, slice(80, 88), 88)]):
            for level in range(2):
                pairs = side[pl.ds(level * 9 + first // 2, count // 2)].astype(F32)
                wide[part, level, pl.ds(to, count), cols, :] = pairs.reshape(count, 8, 128)
                for row in range(count):
                    got = ninth[n, pl.ds(level * 18 + first + row, 1), :]
                    wide[part, level, pl.ds(to + row, 1), nine : nine + 1, :] = got.reshape(1, 1, 128)

    if 0 in parts:
        spread(0, 0, 10, own_ref[...], 0)
    if 1 in parts:
        spread(1, 2 * par, 8, far_ref[...], 10)
        spread(1, 8 * (1 - par), 2, own_ref[:, pl.ds(8 * par, 2)], 8 * par)
    gain = gain_ref[0:1, :]
    half = 1 - par

    cols_of = len(which)

    def slots(part):
        at = parts.index(part) * cols_of
        return at, slice(at, at + cols_of)

    def embed(part):
        first, here = slots(part)
        for n, g in enumerate(which):
            for dj in range(3):
                cols = slice(g * 16 + 7 + dj, g * 16 + 23 + dj)
                got = wide[part, :, :, cols, :].astype(BF)
                gathered[first + n, :, :, :, dj * 128 : dj * 128 + 128] = got
        for n in range(cols_of):
            lhs = jnp.concatenate(
                [gathered[first + n, :, di : di + 8].reshape(256, 384) for di in range(3)], axis=1
            )
            x = mm(lhs, wemb_ref[...]).reshape(2, 8, 16, D)
            for level in range(2):
                x0[first + n, level] = x[level] + lev_ref[level : level + 1, :]

    def norm(part):
        first, here = slots(part)
        for slot in range(first, first + cols_of):
            for u in range(2):
                x = x0[slot, :, :, u * 8 : u * 8 + 8, :].reshape(128, D)
                normed[slot, u] = normalize(x, gain).astype(BF).reshape(2, 4, 16, D)

    def project(part):
        first, here = slots(part)
        n = normed[here].reshape(256 * cols_of, D)
        if leading:
            loads[0].wait()
            loads[1].wait()
        keyval[here] = mm(n, wkv[...]).astype(BF).reshape(cols_of, 2, 128, 1024)
        if part:
            n = normed[here, :, :, pl.ds(half * 2, 2)].reshape(128 * cols_of, D)
        q = (mm(n, wq[...]) * SCALE).astype(BF)
        query[here, :, : 64 if part else 128] = q.reshape(cols_of, 2, -1, D)

    def attention(part):
        first, here = slots(part)
        count = 64 if part else 128
        for slot in range(first, first + cols_of):
            for u in range(2):
                kv = keyval[slot, u]
                heads[slot, u, :count] = attend(query[slot, u, :count], kv[:, :D], kv[:, D:], None)

    def project_out(part):
        first, here = slots(part)
        count = 64 if part else 128
        if leading:
            loads[2].wait()
        out = mm(heads[here, :, :count].reshape(2 * cols_of * count, D), wo[...])
        for n in range(2 * cols_of):
            slot, u = first + n // 2, n % 2
            cols, mine = slice(n * 8, n * 8 + 8), slice(u * 8, u * 8 + 8)
            add = out[n * count : n * count + count].reshape(2, count // 16, 8, D)
            if part:
                x1_refs[-1][:, :, cols, :] = x0[slot, :, pl.ds(4 * half, 4), mine, :] + add
            else:
                for h in range(2):
                    to = pl.ds(4 * (par if h == 0 else half), 4)
                    rows = slice(4 * h, 4 * h + 4)
                    x1_refs[0][:, to, cols, :] = x0[slot, :, rows, mine, :] + add[:, rows]

    pipelined([embed, norm, project, attention, project_out], list(parts))
    if 0 in parts:
        if which == EDGES:
            send_ref[:, :, 0:16, :] = x1_refs[0][:, 4:8, 0:16, :].astype(BF)
            send_ref[:, :, 16:64, :] = middle_ref[...]
            send_ref[:, :, 64:80, :] = x1_refs[0][:, 4:8, 16:32, :].astype(BF)
        else:
            send_ref[...] = x1_refs[0][:, 4:8].astype(BF)


def first_block(parts, which, after, par, patch_arrays, wemb, level_embed, norm_gain, w_query, w_keyval, w_out):
    vmem = pl.BlockSpec(memory_space=pltpu.VMEM)
    width, count = 16 * len(which), len(parts) * len(which)
    leading = parts == (0,) and which == MIDDLE
    outs = [jax.ShapeDtypeStruct((2, 4 if part else 8, width, D), F32) for part in parts]
    if 0 in parts:
        outs.append(jax.ShapeDtypeStruct((2, 4, 80 if which == EDGES else width, D), BF))
    scratch = [
        pltpu.VMEM((2, 2, 10, 96, 128), F32),
        pltpu.VMEM((2, 48, 128), F32),
        pltpu.VMEM((count, 2, 10, 16, 384), BF),
        pltpu.VMEM((count, 2, 8, 16, D), F32),
        pltpu.VMEM((count, 2, 2, 4, 16, D), BF),
        pltpu.VMEM((count, 2, 128, D), BF),
        pltpu.VMEM((count, 2, 128, 1024), BF),
        pltpu.VMEM((count, 2, 128, D), BF),
    ]
    projections = [w_query, w_keyval, w_out]
    if leading:
        outs.append(jax.ShapeDtypeStruct((2, 10, 64, 128), BF))
        scratch += [
            pltpu.VMEM((10, 96, 128), BF),
            pltpu.VMEM((D, D), BF),
            pltpu.VMEM((D, 1024), BF),
            pltpu.VMEM((D, D), BF),
            pltpu.SemaphoreType.DMA((3,)),
        ]
        projections = [pltpu.with_memory_space_constraint(w, pltpu.HBM) for w in projections]
    else:
        projections = [pltpu.with_memory_space_constraint(w, pltpu.VMEM) for w in projections]
    place_of = pl.BlockSpec(memory_space=pltpu.HBM if leading else pltpu.VMEM)
    return pl.pallas_call(
        functools.partial(first_kernel, parts, which),
        out_shape=tuple(outs),
        in_specs=[pl.BlockSpec(memory_space=pl.ANY), pl.BlockSpec(memory_space=pltpu.SMEM)]
        + [vmem] * (3 + len(patch_arrays)) + [place_of] * 3,
        out_specs=(vmem,) * len(outs),
        scratch_shapes=scratch,
        compiler_params=params(),
        cost_estimate=pl.CostEstimate(flops=10**10, bytes_accessed=10**7, transcendentals=0),
    )(after, par, *patch_arrays, wemb, level_embed, norm_gain, *projections)


SHIFTED = WINS - 1


def second_kernel(
    par_ref, own_mid, outer_mid, own_edge, outer_edge, near_ref, gain_ref, mgain_ref,
    wq_ref, wkv_ref, wo_ref, wm_ref,
    out_ref,
    near, x2, normed, query, keyval, heads,
):
    par, pole = par_ref[0], par_ref[1]
    near[...] = near_ref[...].astype(F32)
    gain = gain_ref[1:2, :]
    upper = iota((8, D), 0) >= 4
    key_row = (iota((1, 256), 1) // 8) % 8
    bias = jnp.where(key_row < 4, F32(-1e30), F32(0)) * pole.astype(F32)

    def block(n, first, last):
        if first < 4 < last:
            return jnp.concatenate([block(n, first, 4), block(n, 4, last)], axis=1)
        if first >= 12:
            return near[:, first - 12 : last - 12, n * 8 : n * 8 + 8, :]
        middle = 2 <= n < 8
        at = n * 8 - (16 if middle else 48 if n >= 8 else 0)
        if first < 4:
            return (outer_mid if middle else outer_edge)[:, first:last, at : at + 8, :]
        return (own_mid if middle else own_edge)[:, first - 4 : last - 4, at : at + 8, :]

    def window(w, first, last):
        return jnp.where(upper, block(w, first, last), block(w + 1, first, last))

    def norm(s):
        for w in range(SHIFTED):
            if s == 0:
                x = window(w, 0, 8)
            else:
                x = jnp.concatenate(
                    [window(w, 8, 12), window(w, 12, 16)], axis=1
                )
            n = normalize(x.reshape(128, D), gain).astype(BF)
            normed[s * SHIFTED + w] = n.reshape(2, 4, 16, D)

    def project(s):
        at = slice(s * SHIFTED, s * SHIFTED + SHIFTED)
        n = normed[at].reshape(SHIFTED * 128, D)
        keyval[at] = mm(n, wkv_ref[1]).astype(BF).reshape(SHIFTED, 128, 1024)
        n = normed[at, :, 2 - 2 * s : 4 - 2 * s].reshape(SHIFTED * 64, D)
        query[at] = (mm(n, wq_ref[1]) * SCALE).astype(BF).reshape(SHIFTED, 64, D)

    def attention(s):
        for t in range(s * SHIFTED, s * SHIFTED + SHIFTED):
            kv = keyval[t]
            heads[t] = attend(query[t], kv[:, :D], kv[:, D:], None if s else bias)

    def project_out(s):
        at = slice(s * SHIFTED, s * SHIFTED + SHIFTED)
        out = mm(heads[at].reshape(SHIFTED * 64, D), wo_ref[1])
        rows = slice(s * 4, s * 4 + 4)
        for w in range(SHIFTED):
            new = window(w, 4 + s * 4, 8 + s * 4)
            new = new + out[w * 64 : w * 64 + 64].reshape(2, 4, 8, D)
            for c in range(4):
                piece = new[..., c * 128 : c * 128 + 128]
                x2[c, :, rows, w * 8 + 4 : w * 8 + 8, :] = piece[:, :, 4:8, :]
                x2[c, :, rows, w * 8 + 8 : w * 8 + 12, :] = piece[:, :, 0:4, :]

    def merge(s):
        parts = []
        for p in range(4):
            got = [
                jnp.concatenate(
                    [
                        x2[c, level, s * 4 + 2 * a + p % 2, pl.ds(8 + p // 2, 32, stride=2), :]
                        for c in range(4)
                    ],
                    axis=1,
                )
                for level in range(2)
                for a in range(2)
            ]
            parts.append(jnp.concatenate(got, axis=0))
        n = normalize(jnp.concatenate(parts, axis=1), mgain_ref[...]).astype(BF)
        out = mm(n, wm_ref[...]).astype(BF)
        out_ref[:, pl.ds(2 * ((par + s) % 2), 2)] = out.reshape(2, 2, 32, 1024)

    pipelined([norm, project, attention, project_out, merge], [0, 1])


def second_block(par, x1_parts, near, norm_gain, merge_gain, w_query, w_keyval, w_out, merge_weight):
    vmem = pl.BlockSpec(memory_space=pltpu.VMEM)
    weights = [
        pltpu.with_memory_space_constraint(w, pltpu.VMEM) for w in (w_query, w_keyval, w_out, merge_weight)
    ]
    return pl.pallas_call(
        second_kernel,
        out_shape=jax.ShapeDtypeStruct((2, 4, 32, 1024), BF),
        in_specs=[pl.BlockSpec(memory_space=pltpu.SMEM)] + [vmem] * 11,
        out_specs=vmem,
        scratch_shapes=[
            pltpu.VMEM((2, 4, 80, D), F32),
            pltpu.VMEM((4, 2, 8, 80, 128), F32),
            pltpu.VMEM((2 * SHIFTED, 2, 4, 16, D), BF),
            pltpu.VMEM((2 * SHIFTED, 64, D), BF),
            pltpu.VMEM((2 * SHIFTED, 128, 1024), BF),
            pltpu.VMEM((2 * SHIFTED, 64, D), BF),
        ],
        compiler_params=params(),
        cost_estimate=pl.CostEstimate(flops=10**10, bytes_accessed=10**7, transcendentals=0),
    )(
        par, *x1_parts, near, norm_gain, merge_gain, *weights
    )


def embedding_matrix(embed_weight, land_embed):
    w = jnp.pad(embed_weight, ((0, 0), (0, 0), (0, 2), (0, 0))).reshape(3, 4, 3, 4, 8, D)
    w = w.transpose(0, 2, 1, 3, 4, 5)
    share = land_embed / 16
    high = lax.reduce_precision(share, 8, 7)
    at = [lax.broadcasted_iota(jnp.int32, w.shape, d) for d in (0, 1, 4)]
    middle = (at[0] == 1) & (at[1] == 1)
    w = jnp.where(middle & (at[2] == 6), high.astype(BF), w)
    w = jnp.where(middle & (at[2] == 7), (share - high).astype(BF), w)
    return w.reshape(9 * 128, D)


def swap(block, first):
    count = lax.axis_size("lat")
    pairs = []
    for i in range(first, count - 1, 2):
        pairs += [(i, i + 1), (i + 1, i)]
    return lax.ppermute(block, "lat", pairs)


def around(block, distance):
    count = lax.axis_size("lon")
    return lax.ppermute(block, "lon", [(i, (i + distance) % count) for i in range(count)])


def shards(
    atmos, orography, land_sea, embed_weight, level_embed, land_embed, norm_gain,
    w_query, w_keyval, w_out, merge_gain, merge_weight,
):
    lat = lax.axis_index("lat")
    par = lat % 2
    pole = (lat == 0) | (lat == lax.axis_size("lat") - 1)
    place = jnp.stack([par, pole]).astype(jnp.int32)
    own, send, edge, near = patches(place, atmos, orography, land_sea)
    edge = swap(edge, 0)
    near = swap(near, 1)
    send = lax.dynamic_update_slice(send, edge, (7 * (1 - par), 0, 0))
    far = swap(send, 1)
    wemb = embedding_matrix(embed_weight, land_embed)
    weights = wemb, level_embed, norm_gain, w_query, w_keyval, w_out
    own_mid, send_mid, own = first_block((0,), MIDDLE, edge, place, (own, edge, near), *weights)
    far, low, high = unpack_far(own_mid, far, own)
    from_low, from_high = around(high, 1), around(low, -1)
    (outer_mid,) = first_block((1,), MIDDLE, own_mid, place, (own, far), *weights)
    own_edge, send = first_block(
        (0,), EDGES, outer_mid, place, (own, from_low, from_high, send_mid), *weights
    )
    near = swap(send, 0)
    (outer_edge,) = first_block(
        (1,), EDGES, own_edge, place, (own, far, from_low, from_high), *weights
    )
    return second_block(
        place, (own_mid, outer_mid, own_edge, outer_edge), near, norm_gain,
        merge_gain.reshape(1, -1), w_query, w_keyval, w_out, merge_weight,
    )


def solution(mesh):
    in_specs = (P(None, None, "lat", "lon"), P("lat", "lon"), P("lat", "lon")) + (P(),) * 9
    out_specs = P(None, "lat", "lon", None)
    return jax.shard_map(shards, mesh=mesh, in_specs=in_specs, out_specs=out_specs, check_vma=False)
```
